32 devices in a mesh: dp: 8 (over z, y), tensor: 4 (over x, core).
Axes of the slice: x: 2, y: 2, z: 4, core: 2. Of those that a mesh axis runs over, the one named last changes fastest.
Arguments:
- hidden_rows: bfloat16 [2048, 8, 768], P('tensor', 'dp'), may hold values from -6 to 6
- out_grad: bfloat16 [2048, 8, 768], P('tensor', 'dp'), may hold values from -6 to 6
- doc_lengths: int32 [8, 4], P('dp'), may hold values from 1 to 2045, as said below
- zx_weight: bfloat16 [2, 768, 1536], P(None, 'dp', 'tensor'), may hold values from -0.21875 to 0.21875
- step_weight: bfloat16 [768, 24], P('dp', 'tensor'), may hold values from -0.21875 to 0.21875
- bc_weight: bfloat16 [768, 256], P('dp'), may hold values from -0.21875 to 0.21875
- conv_inner: bfloat16 [24, 256], P('tensor', 'dp'), may hold values from -3 to 3
- conv_shared: bfloat16 [1024], P('dp'), may hold values from -3 to 3
- out_weight: bfloat16 [1536, 768], P('tensor', 'dp'), may hold values from -0.15625 to 0.15625
- decay_log: float32 [24], P('tensor'), may hold values from 0 to 2.77
- step_bias: float32 [24], P('tensor'), may hold values from -6.5 to -2.3
- skip_gain: float32 [24], P('tensor'), may hold values from 0.5 to 1.5
- norm_gain: bfloat16 [768], P('dp'), may hold values from 0.5 to 1.5
- gate_gain: float32 [1536], P('tensor'), may hold values from 0.5 to 1.5
Outputs:
- block_out: bfloat16 [2048, 8, 768], P('tensor', 'dp')
- hidden_grad: bfloat16 [2048, 8, 768], P('tensor', 'dp')
- zx_weight_grad: float32 [2, 768, 1536], P(None, 'dp', 'tensor')
- step_weight_grad: float32 [768, 24], P('dp', 'tensor')
- bc_weight_grad: float32 [768, 256], P('dp')
- conv_inner_grad: float32 [24, 256], P('tensor', 'dp')
- conv_shared_grad: float32 [1024], P('dp')
- out_weight_grad: float32 [1536, 768], P('tensor', 'dp')
- decay_log_grad: float32 [24], P('tensor')
- step_bias_grad: float32 [24], P('tensor')
- skip_gain_grad: float32 [24], P('tensor')
- norm_gain_grad: float32 [768], P('dp')
- gate_gain_grad: float32 [1536], P('tensor')
The draws below stay inside these ranges and needn't reach their ends.
Inputs may be any that keep to these rules, and one draw needn't show every extreme that they name: `doc_lengths`: each row's 4 lengths add up to 2048; one document of each row, at a place drawn from the seed, is longer than 1536; in some row it is 2045 long and the others are 1 long.
All inputs are finite; a program needn't handle non-finite values.
Results may differ from the reference program's by a relative error of at most 0.013.
Values may be sent and summed in bfloat16 or wider, within the bound.
No kernel may reach another device: no remote copies, remote signals or barrier semaphores. Data moves between devices by JAX's collectives and lax.ppermute only.
A program may use at most 128 MiB of HBM per device.

```python
import jax
import jax.numpy as jnp
from jax import lax

D = 768
INNER = 1536
HEADS = 24
HEAD_DIM = 64
STATE = 128
CONV = 4
SPAN = 256
SEQ_DEV = 512
SEQS = 4
SEQ = 2048
BATCH = 8


def draw_doc_lengths(key, part):
    key = jax.random.fold_in(key, 7)
    key_rest, key_share, key_place, key_row = jax.random.split(key, 4)
    remainder = jax.random.randint(key_rest, (BATCH,), SEQS - 1, SEQ_DEV)
    tight_row = jax.random.randint(key_row, (), 0, BATCH)
    remainder = jnp.where(jnp.arange(BATCH) == tight_row, SEQS - 1, remainder)
    shares = jax.random.randint(key_share, (BATCH, SEQS - 1), 1, 100)
    spare_total = remainder - (SEQS - 1)
    pieces = 1 + spare_total[:, None] * shares // jnp.sum(shares, axis=1, keepdims=True)
    pieces = pieces.at[:, -1].add(remainder - jnp.sum(pieces, axis=1))
    longest = SEQ - remainder
    where_long = jax.random.randint(key_place, (BATCH, 1), 0, SEQS)
    position = jnp.arange(SEQS)[None, :]
    source_index = jnp.clip(jnp.where(position < where_long, position, position - 1), 0, SEQS - 2)
    picked = jnp.take_along_axis(pieces, jnp.broadcast_to(source_index, (BATCH, SEQS)), axis=1)
    return jnp.where(position == where_long, longest[:, None], picked).astype(jnp.int32)


def raised(values, own_key, source, target, shards_of, factor):
    owner, partner = [(jnp.arange(values.shape[dim]) // (values.shape[dim] // shards_of)).reshape([-1 if axis == dim else 1 for axis in range(values.ndim)]) for dim in (source, target)]
    chosen = jax.random.permutation(own_key, shards_of)[partner]
    strong = (owner == chosen) | (owner == (partner + shards_of // 2) % shards_of)
    return jnp.where(strong, factor * values, values)


def block_levels(stream_key, shape, cuts, least, largest):
    def one(axis_at, parts):
        steps = jax.random.uniform(jax.random.fold_in(jax.random.fold_in(stream_key, 6), axis_at), (parts,), jnp.float32, least / len(cuts), largest / len(cuts))
        return jnp.repeat(jnp.exp(steps), shape[axis_at] // parts).reshape((-1,) + (1,) * (len(shape) - axis_at - 1))

    gain = one(*cuts[0])
    for cut in cuts[1:]:
        gain = gain * one(*cut)
    return gain


def normal_values(stream_key, extent, deviation, bound, shards=(), kind=jnp.bfloat16):
    array = jax.random.normal(stream_key, extent, jnp.float32) * deviation
    if len(shards) > 0:
        array = block_levels(stream_key, extent, shards, -0.22, 0.18) * array
    return jnp.clip(array, min=-bound, max=bound).astype(kind)


def bell_draw_with(stream_key, dims, spread, bound, cuts, heavy, kind=jnp.bfloat16):
    values = spread * jax.random.normal(stream_key, dims, jnp.float32)
    if cuts:
        values = values * block_levels(stream_key, dims, cuts, -0.22, 0.18)
    return jnp.clip(raised(values, jax.random.fold_in(stream_key, 3), *heavy), -bound, bound).astype(kind)


def setup_inputs(seed: int = 0) -> dict:
    splits = jax.random.split(jax.random.key(seed), 15)
    return {
        "hidden_rows": normal_values(splits[0], (SEQ, BATCH, D), 1.0, 6.0, ((0, 4), (1, 8))),
        "out_grad": bell_draw_with(splits[1], (SEQ, BATCH, D), 1.0, 6.0, ((0, 4), (1, 8)), (1, 2, 8, 2.0)),
        "doc_lengths": draw_doc_lengths(jax.random.fold_in(splits[14], 71), 0),
        "zx_weight": normal_values(splits[3], (2, D, INNER), D ** -0.5, 0.21875, ((1, 8), (2, 4))),
        "step_weight": normal_values(splits[4], (D, HEADS), D ** -0.5, 0.21875, ((0, 8), (1, 4))),
        "bc_weight": normal_values(splits[5], (D, 2 * STATE), D ** -0.5, 0.21875, ((0, 8),)),
        "conv_inner": normal_values(splits[6], (HEADS, HEAD_DIM * CONV), CONV ** -0.5, 3.0, ((0, 4), (1, 8))),
        "conv_shared": normal_values(splits[7], (2 * STATE * CONV,), CONV ** -0.5, 3.0, ((0, 8),)),
        "out_weight": normal_values(splits[8], (INNER, D), INNER ** -0.5, 0.15625, ((0, 4), (1, 8))),
        "decay_log": jnp.clip(2.77 * jax.random.uniform(splits[9], (HEADS,), jnp.float32) ** block_levels(splits[9], (HEADS,), ((0, 4),), -0.2, 0.2), 0.0, 2.77),
        "step_bias": jnp.clip(-6.5 + 4.2 * jax.random.uniform(splits[10], (HEADS,), jnp.float32) ** block_levels(splits[10], (HEADS,), ((0, 4),), -0.2, 0.2), -6.5, -2.3),
        "skip_gain": jnp.clip(0.5 + 1.0 * jax.random.uniform(splits[11], (HEADS,), jnp.float32) ** block_levels(splits[11], (HEADS,), ((0, 4),), -0.2, 0.2), 0.5, 1.5),
        "norm_gain": jnp.clip(1.0 + 0.1 * jax.random.normal(splits[12], (D,), jnp.float32), 0.5, 1.5).astype(jnp.bfloat16),
        "gate_gain": jnp.clip(1.0 + 0.1 * jax.random.normal(splits[13], (INNER,), jnp.float32), 0.5, 1.5),
    }


epsilon = 1e-05
highest = lax.Precision.HIGHEST

@jax.custom_vjp
def low(v):
    return lax.optimization_barrier(v.astype(jnp.bfloat16)).astype(jnp.float32)

@jax.custom_vjp
def low_back(v):
    return v

def low_keep(v):
    return (low(v), None)

def low_pass(kept, grad):
    return (grad,)

def back_keep(v):
    return (v, None)

def back_low(kept, grad):
    return (low(grad),)
low.defvjp(low_keep, low_pass)
low_back.defvjp(back_keep, back_low)

def doc_ids(lengths, total_len):
    doc_ends = jnp.cumsum(lengths.astype(jnp.int32)).astype(jnp.int32)[:-1]
    position = jnp.arange(total_len, dtype=jnp.int32)
    return lax.optimization_barrier(jnp.sum((position[:, None] >= doc_ends[None, :]).astype(jnp.int32), axis=1)).astype(jnp.int32)

def causal_conv(signal, tap_table, doc_row):
    tap_count = tap_table.shape[1]
    total = signal * tap_table[:, tap_count - 1]
    for offset in range(1, tap_count):
        shifted = jnp.pad(signal, ((offset, 0), (0, 0)))[:-offset]
        before = jnp.pad(doc_row, (offset, 0), constant_values=-1)[:-offset]
        total = total + jnp.where((before == doc_row)[:, None], shifted, 0.0) * tap_table[:, tap_count - 1 - offset]
    return total

def state_space(inner_seq, input_map, output_map, step_size, rates, skip_gain, doc_row):
    length, head_count, head_width = inner_seq.shape
    block_count = length // SPAN
    state_count = input_map.shape[1]
    blocks_x = inner_seq.reshape(block_count, SPAN, head_count, head_width)
    blocks_b = input_map.reshape(block_count, SPAN, state_count)
    blocks_c = output_map.reshape(block_count, SPAN, state_count)
    blocks_dt = step_size.reshape(block_count, SPAN, head_count)
    blocks_doc = doc_row.reshape(block_count, SPAN)
    cumulative = jnp.cumsum(-blocks_dt * rates, axis=1)
    scores = jnp.einsum('cin,cjn->cij', blocks_c, blocks_b, precision=highest)
    position = jnp.arange(SPAN)
    visible = (position[None, :, None] >= position[None, None, :]) & (blocks_doc[:, :, None] == blocks_doc[:, None, :])
    gaps = cumulative[:, :, None, :] - cumulative[:, None, :, :]
    decays = jnp.exp(jnp.where(visible[..., None], gaps, 0.0)) * visible[..., None]
    mixing = low(scores[..., None] * decays * blocks_dt[:, None, :, :])
    inside = jnp.einsum('cijh,cjhp->cihp', mixing, blocks_x, precision=highest)
    final_cum = cumulative[:, -1, :]
    tail_doc = blocks_doc == blocks_doc[:, -1:]
    weight_in = jnp.exp(final_cum[:, None, :] - cumulative) * tail_doc[..., None] * blocks_dt
    scaled = low(blocks_x * weight_in[..., None])
    states = jnp.einsum('cjhp,cjn->chpn', scaled, blocks_b, precision=highest)
    before = jnp.concatenate([jnp.full((1,), -1, jnp.int32), blocks_doc[:-1, -1].astype(jnp.int32)])
    carry_keep = blocks_doc[:, -1] == before

    def advance(running, packed):
        incoming, drop_log, survives = packed
        following = jnp.exp(drop_log)[:, None, None] * jnp.where(survives, running, 0.0) + incoming
        return (following, running)
    initial = jnp.zeros((head_count, head_width, state_count), states.dtype)
    _, entering = lax.scan(advance, initial, (states, final_cum, carry_keep))
    head_keep = blocks_doc == before[:, None]
    outside = jnp.einsum('chpn,cin->cihp', low(entering), blocks_c, precision=highest)
    outside = outside * (jnp.exp(cumulative) * head_keep[..., None])[..., None]
    result = inside + outside + skip_gain[None, None, :, None] * blocks_x
    return result.reshape(length, head_count, head_width)

def mixer_row(gate_in, inner_in, step_in, shared_in, doc_row, taps_inner, taps_shared, decay_log, step_bias, skip_gain):
    head_count = step_in.shape[1]
    inner_act = jax.nn.silu(causal_conv(inner_in, taps_inner, doc_row))
    shared_act = jax.nn.silu(causal_conv(shared_in, taps_shared, doc_row))
    inner_seq = low(inner_act).reshape(inner_act.shape[0], head_count, -1)
    state_count = shared_act.shape[1] // 2
    input_map = low(shared_act[:, :state_count])
    output_map = low(shared_act[:, state_count:])
    step_size = jax.nn.softplus(step_in + step_bias)
    result = state_space(inner_seq, input_map, output_map, step_size, jnp.exp(decay_log), skip_gain, doc_row)
    return result.reshape(inner_act.shape) * jax.nn.silu(gate_in)

def block_row(residual, doc_row, params):
    zx_full, step_full, bc_full, taps_inner, taps_shared, out_full, decay_log, step_bias, skip_gain, norm_gain, gate_gain = params
    row_scale = lax.rsqrt(lax.optimization_barrier(jnp.mean(residual * residual, axis=1, keepdims=True)) + epsilon)
    normed = low(residual * row_scale * norm_gain)
    gate_in = low_back(jnp.dot(normed, zx_full[0], precision=highest, preferred_element_type=jnp.float32))
    inner_in = low_back(jnp.dot(normed, zx_full[1], precision=highest, preferred_element_type=jnp.float32))
    step_in = low_back(jnp.dot(normed, step_full, precision=highest, preferred_element_type=jnp.float32))
    shared_in = low_back(jnp.dot(normed, bc_full, precision=highest, preferred_element_type=jnp.float32))
    mixed = mixer_row(gate_in, inner_in, step_in, shared_in, doc_row, taps_inner, taps_shared, decay_log, step_bias, skip_gain)
    gate_scale = lax.rsqrt(lax.optimization_barrier(jnp.mean(mixed * mixed, axis=1, keepdims=True)) + epsilon)
    gated = low(mixed * gate_scale * gate_gain)
    return residual + jnp.dot(gated, out_full, precision=highest, preferred_element_type=jnp.float32)

def reference(hidden_rows, out_grad, doc_lengths, zx_weight, step_weight, bc_weight, conv_inner, conv_shared, out_weight, decay_log, step_bias, skip_gain, norm_gain, gate_gain):
    params = (zx_weight.astype(jnp.float32), step_weight.astype(jnp.float32), bc_weight.astype(jnp.float32), conv_inner.astype(jnp.float32).reshape(INNER, CONV), conv_shared.astype(jnp.float32).reshape(2 * STATE, CONV), out_weight.astype(jnp.float32), decay_log, step_bias, skip_gain, norm_gain.astype(jnp.float32), gate_gain)
    doc_table = jax.vmap(lambda lengths: doc_ids(lengths, SEQ))(doc_lengths)

    def forward(inputs, weights):
        rows_first = jnp.moveaxis(inputs, 1, 0)

        def one_row(packed):
            return jax.checkpoint(block_row)(packed[0], packed[1], weights)
        return jnp.moveaxis(lax.map(one_row, (rows_first, doc_table)), 0, 1)
    result, pullback = jax.vjp(forward, hidden_rows.astype(jnp.float32), params)
    input_grad, weight_grads = pullback(out_grad.astype(jnp.float32))
    zx_grad, step_grad, bc_grad, inner_taps_grad, shared_taps_grad, out_grad_w, decay_grad, bias_grad, skip_grad, norm_grad, gate_grad = weight_grads
    return (result.astype(jnp.bfloat16), input_grad.astype(jnp.bfloat16), zx_grad, step_grad, bc_grad, inner_taps_grad.reshape(HEADS, HEAD_DIM * CONV), shared_taps_grad.reshape(2 * STATE * CONV), out_grad_w, decay_grad, bias_grad, skip_grad, norm_grad, gate_grad)
```

```python
import functools

import jax
import jax.numpy as jnp
from jax import lax
from jax.experimental import pallas as pl
from jax.experimental.pallas import tpu as pltpu
from jax.sharding import PartitionSpec as P

CONV = 4
SPAN = 256
LANES = 128
epsilon = 1e-05
bf16 = jnp.bfloat16
f32 = jnp.float32
NN = (((1,), (0,)), ((), ()))
NT = (((1,), (1,)), ((), ()))
TN = (((0,), (0,)), ((), ()))


def mm(left, right, dims=NN):
    return lax.dot_general(left, right, dims, preferred_element_type=f32)


def split(values, parts):
    pieces = []
    for _ in range(parts):
        piece = values.astype(bf16)
        pieces.append(piece)
        values = values - piece.astype(f32)
    return pieces


def mm_left_exact(left, right, parts):
    return sum(mm(left, piece) for piece in split(right, parts))


def mm_right_exact(left, right, parts):
    return sum(mm(piece, right) for piece in split(left, parts))


def sigmoid(values):
    return 1.0 / (1.0 + jnp.exp(-values))


def softplus(values):
    return jnp.maximum(values, 0.0) + jnp.log1p(jnp.exp(-jnp.abs(values)))


def doc_start(position, ends):
    start = jnp.zeros_like(position)
    for end in ends:
        start = jnp.where(position >= end, end, start)
    return start


def scalar_start(position, ends):
    start = jnp.int32(0)
    for end in ends:
        start = jnp.where(position >= end, end, start)
    return start


def iota(shape, dim):
    return lax.broadcasted_iota(jnp.int32, shape, dim)


def conv_block(ext_ref, taps_ref, position, start, width):
    masks = [None] + [(position - k >= start).astype(f32) for k in range(1, CONV)]
    groups = []
    for at in range(0, width, LANES):
        cols = slice(at, at + LANES)
        total = ext_ref[8 : 8 + SPAN, cols] * taps_ref[CONV - 1 : CONV, cols]
        for k in range(1, CONV):
            total = total + ext_ref[8 - k : 8 - k + SPAN, cols] * masks[k] * (
                taps_ref[CONV - 1 - k : CONV - k, cols]
            )
        groups.append(total)
    return jnp.concatenate(groups, axis=1)


def wide(mask, width):
    return jnp.concatenate([mask] * (width // LANES), axis=1)


def forward_kernel(
    inner,
    state_count,
    heads,
    info_ref,
    hidden_ref,
    weight_ref,
    taps_ref,
    chan_ref,
    head_ref,
    gain_ref,
    expand_ref,
    normed_ref,
    pre_ref,
    y_ref,
    mixed_ref,
    cum_ref,
    entering_ref,
    ext_ref,
    state_ref,
):
    block = pl.program_id(0)
    conv_width = inner + 2 * state_count
    step_at = inner + conv_width
    ends = [info_ref[k] for k in range(3)]
    base = block * SPAN

    @pl.when(block == 0)
    def _():
        ext_ref[...] = jnp.zeros_like(ext_ref)
        state_ref[...] = jnp.zeros_like(state_ref)

    residual = hidden_ref[0].astype(f32)
    row_scale = lax.rsqrt(jnp.mean(residual * residual, axis=1, keepdims=True) + epsilon)
    normed = (residual * row_scale * gain_ref[0:1, :]).astype(bf16)
    normed_ref[...] = normed
    pre = mm(normed, weight_ref[...])
    pre_ref[...] = pre

    ext_ref[0:8, :] = ext_ref[SPAN : SPAN + 8, :]
    ext_ref[8 : 8 + SPAN, :] = pre[:, inner:step_at]
    position = base + iota((SPAN, LANES), 0)
    start = doc_start(position, ends)
    conv = conv_block(ext_ref, taps_ref, position, start, conv_width)
    active = conv * sigmoid(conv)
    x_val = active[:, :inner].astype(bf16).astype(f32)
    in_map = active[:, inner : inner + state_count].astype(bf16)
    out_map = active[:, inner + state_count :].astype(bf16)

    step_size = softplus(pre[:, step_at:] + head_ref[1:2, :])
    log_decay = step_size * head_ref[0:1, :]
    row_at = iota((SPAN, SPAN), 0)
    col_at = iota((SPAN, SPAN), 1)
    lower = (col_at <= row_at).astype(f32).astype(bf16)
    cum = mm_left_exact(lower, log_decay, 3)
    cum_ref[...] = cum
    cum_rows = cum.T

    start_last = scalar_start(base + SPAN - 1, ends)
    keep = (start < base).astype(f32)
    tail = (position >= start_last).astype(f32)
    survives = (start_last < base).astype(f32)
    expand = expand_ref[...]
    step_wide = mm_right_exact(step_size, expand, 2)
    decay_wide = mm_right_exact(jnp.exp(cum), expand, 2)
    into_wide = mm_right_exact(jnp.exp(cum[SPAN - 1 :, :] - cum) * tail, expand, 2)

    x_step = x_val * step_wide
    x_step_low = x_step.astype(bf16)
    state = state_ref[...]
    entering_ref[...] = state
    outside = mm(out_map, state.astype(bf16)) * (decay_wide * wide(keep, inner))
    visible = (col_at <= row_at) & (base + col_at >= wide(start, SPAN))
    scores = jnp.where(visible, mm(out_map, in_map, NT), 0.0)
    upper_half = iota((SPAN, LANES), 1) >= LANES // 2
    inside = []
    for pair in range(heads // 2):
        x_pair = x_step_low[:, pair * LANES : (pair + 1) * LANES]
        total = None
        for which in range(2):
            head = 2 * pair + which
            gap = cum[:, head : head + 1] - cum_rows[head : head + 1, :]
            mixing = (scores * jnp.exp(jnp.minimum(gap, 0.0))).astype(bf16)
            chosen = upper_half if which else jnp.logical_not(upper_half)
            part = mm(mixing, jnp.where(chosen, x_pair, jnp.zeros_like(x_pair)))
            total = part if total is None else total + part
        inside.append(total)
    y_val = jnp.concatenate(inside, axis=1) + outside + chan_ref[0:1, :] * x_val
    y_ref[...] = y_val
    gate = pre[:, :inner]
    mixed_ref[...] = y_val * (gate * sigmoid(gate))

    scaled = (x_step * into_wide).astype(bf16)
    state_ref[...] = (decay_wide[SPAN - 1 :, :] * survives) * state + mm(in_map, scaled, TN)


def branch_kernel(mixed_ref, grad_ref, out_ref, chan_ref, branch_ref, stats_ref):
    mixed = mixed_ref[...]
    out_w = out_ref[...]
    gain = chan_ref[1:2, :]
    branch_ref[0] = mm((mixed * gain).astype(bf16), out_w, NT).astype(bf16)
    weighted = mm(grad_ref[0], out_w) * gain
    squares = jnp.sum(mixed * mixed, axis=1, keepdims=True)
    crossed = jnp.sum(weighted * mixed, axis=1, keepdims=True)
    lane = iota((SPAN, LANES), 1)
    both = jnp.where(lane == 0, squares, jnp.where(lane == 1, crossed, 0.0))
    stats_ref[...] = both.T[0:8, :]


def backward_kernel(
    inner,
    state_count,
    heads,
    inner_total,
    info_ref,
    stats_ref,
    grad_ref,
    normed_ref,
    weight_ref,
    out_ref,
    pre_ref,
    halo_ref,
    y_ref,
    cum_ref,
    entering_ref,
    taps_ref,
    chan_ref,
    head_ref,
    gain_ref,
    expand_ref,
    gather_ref,
    total_ref,
    wide_grad_ref,
    small_ref,
    ext_ref,
    next_ref,
    state_grad_ref,
    weight_acc,
    out_acc,
    pre_grad_ref,
):
    step = pl.program_id(0)
    blocks = pl.num_programs(0)
    block = blocks - 1 - step
    base = block * SPAN
    conv_width = inner + 2 * state_count
    step_at = inner + conv_width
    ends = [info_ref[k] for k in range(3)]

    @pl.when(step == 0)
    def _():
        next_ref[...] = jnp.zeros_like(next_ref)
        state_grad_ref[...] = jnp.zeros_like(state_grad_ref)
        weight_acc[...] = jnp.zeros_like(weight_acc)
        out_acc[...] = jnp.zeros_like(out_acc)
        small_ref[...] = jnp.zeros_like(small_ref)

    stats = stats_ref[...].T
    gate_scale = lax.rsqrt(stats[:, 0:1] / inner_total + epsilon)
    crossed = stats[:, 1:2] / inner_total
    gate = pre_ref[:, :inner]
    gate_sig = sigmoid(gate)
    gate_act = gate * gate_sig
    y_val = y_ref[...]
    mixed = y_val * gate_act
    grad = grad_ref[0]
    gain = chan_ref[1:2, :]
    skip = chan_ref[0:1, :]
    gated_grad = mm(grad, out_ref[...])
    scaled_mixed = mixed * gate_scale
    out_acc[...] += mm(grad, (scaled_mixed * gain).astype(bf16), TN)
    gain_grad = jnp.sum(gated_grad * scaled_mixed, axis=0, keepdims=True)
    mixed_grad = gate_scale * (gated_grad * gain) - scaled_mixed * (
        gate_scale * gate_scale * crossed
    )
    gate_grad = mixed_grad * y_val * (gate_sig * (1.0 + gate * (1.0 - gate_sig)))
    pre_grad_ref[:, :inner] = gate_grad.astype(bf16)
    y_grad = mixed_grad * gate_act

    ext_ref[0:8, :] = halo_ref[:, inner:step_at]
    ext_ref[8 : 8 + SPAN, :] = pre_ref[:, inner:step_at]
    position = base + iota((SPAN, LANES), 0)
    start = doc_start(position, ends)
    conv = conv_block(ext_ref, taps_ref, position, start, conv_width)
    conv_sig = sigmoid(conv)
    active = conv * conv_sig
    act_slope = conv_sig * (1.0 + conv * (1.0 - conv_sig))
    x_val = active[:, :inner].astype(bf16).astype(f32)
    in_map = active[:, inner : inner + state_count].astype(bf16)
    out_map = active[:, inner + state_count :].astype(bf16)

    step_pre = pre_ref[:, step_at:] + head_ref[1:2, :]
    step_size = softplus(step_pre)
    rates = head_ref[0:1, :]
    cum = cum_ref[...]
    cum_rows = cum.T
    start_last = scalar_start(base + SPAN - 1, ends)
    keep = (start < base).astype(f32)
    tail = (position >= start_last).astype(f32)
    survives = (start_last < base).astype(f32)
    expand = expand_ref[...]
    step_wide = mm_right_exact(step_size, expand, 2)
    decay_wide = mm_right_exact(jnp.exp(cum), expand, 2)
    into_wide = mm_right_exact(jnp.exp(cum[SPAN - 1 :, :] - cum) * tail, expand, 2)
    keep_decay = decay_wide * wide(keep, inner)
    last_decay = decay_wide[SPAN - 1 :, :] * survives

    x_step = x_val * step_wide
    x_step_low = x_step.astype(bf16)
    scaled = (x_step * into_wide).astype(bf16)
    entering = entering_ref[...]
    entering_low = entering.astype(bf16)
    y_grad_low = y_grad.astype(bf16)
    state_grad = state_grad_ref[...]
    state_grad_low = state_grad.astype(bf16)

    outside = mm(out_map, entering_low)
    outside_grad = (y_grad * keep_decay).astype(bf16)
    scaled_grad = mm(in_map, state_grad_low)
    out_map_grad = mm(outside_grad, entering_low, NT)
    in_map_grad = mm(scaled, state_grad_low, NT)
    state_grad_ref[...] = last_decay * state_grad + mm(out_map, outside_grad, TN)

    row_at = iota((SPAN, SPAN), 0)
    col_at = iota((SPAN, SPAN), 1)
    col_start = doc_start(base + col_at, ends)
    visible = (row_at <= col_at) & (base + row_at >= col_start)
    scores = jnp.where(visible, mm(in_map, out_map, NT), 0.0)
    upper_half = iota((SPAN, LANES), 1) >= LANES // 2
    score_grad = jnp.zeros((SPAN, SPAN), f32)
    x_step_grads = []
    for pair in range(heads // 2):
        x_pair = x_step_low[:, pair * LANES : (pair + 1) * LANES]
        grad_pair = y_grad_low[:, pair * LANES : (pair + 1) * LANES]
        total = None
        for which in range(2):
            head = 2 * pair + which
            chosen = upper_half if which else jnp.logical_not(upper_half)
            grad_head = jnp.where(chosen, grad_pair, jnp.zeros_like(grad_pair))
            gap = cum_rows[head : head + 1, :] - cum[:, head : head + 1]
            decays = jnp.exp(jnp.minimum(gap, 0.0))
            score_grad = score_grad + mm(x_pair, grad_head, NT) * decays
            part = mm((scores * decays).astype(bf16), grad_head)
            total = part if total is None else total + part
        x_step_grads.append(total)
    x_step_grad = jnp.concatenate(x_step_grads, axis=1)
    score_grad = jnp.where(visible, score_grad, 0.0).astype(bf16)
    in_map_grad = in_map_grad + mm(score_grad, out_map)
    out_map_grad = out_map_grad + mm(score_grad, in_map, TN)

    inside = y_val - skip * x_val - keep_decay * outside
    into_terms = scaled.astype(f32) * scaled_grad
    cum_terms = (
        y_grad_low.astype(f32) * inside
        + outside_grad.astype(f32) * outside
        - x_step_low.astype(f32) * x_step_grad
        - into_terms
    )
    last_terms = jnp.sum(into_terms, axis=0, keepdims=True) + last_decay * jnp.sum(
        state_grad * entering, axis=0, keepdims=True
    )
    last_row = iota((SPAN, inner), 0) == SPAN - 1
    cum_terms = cum_terms + jnp.where(last_row, last_terms, 0.0)
    x_step_grad = x_step_grad + into_wide * scaled_grad
    gather = gather_ref[...]
    cum_grad = mm_right_exact(cum_terms, gather, 2)
    step_grad = mm_right_exact(x_val * x_step_grad, gather, 2)
    upper = (row_at <= col_at).astype(f32).astype(bf16)
    log_grad = mm_left_exact(upper, cum_grad, 3)
    step_grad = (step_grad + log_grad * rates) * sigmoid(step_pre)
    pre_grad_ref[:, step_at:] = step_grad.astype(bf16)
    x_grad = skip * y_grad + step_wide * x_step_grad

    small_ref[4:5, :inner] += jnp.sum(y_grad * x_val, axis=0, keepdims=True)
    small_ref[5:6, :inner] += gain_grad
    small_ref[6:7, :LANES] += jnp.sum(step_size * rates * log_grad, axis=0, keepdims=True)
    small_ref[7:8, :LANES] += jnp.sum(step_grad, axis=0, keepdims=True)

    conv_grad = jnp.concatenate([x_grad, in_map_grad, out_map_grad], axis=1) * act_slope
    next_ref[SPAN : SPAN + 8, :] = next_ref[0:8, :]
    next_ref[0:SPAN, :] = conv_grad
    back = [None] + [(position - k >= start).astype(f32) for k in range(1, CONV)]
    ahead = [None] + [
        (position >= doc_start(position + k, ends)).astype(f32) for k in range(1, CONV)
    ]
    for at in range(0, conv_width, LANES):
        cols = slice(at, at + LANES)
        grad_here = next_ref[0:SPAN, cols]
        total = grad_here * taps_ref[CONV - 1 : CONV, cols]
        small_ref[CONV - 1 : CONV, cols] += jnp.sum(
            grad_here * ext_ref[8 : 8 + SPAN, cols], axis=0, keepdims=True
        )
        for k in range(1, CONV):
            total = total + next_ref[k : k + SPAN, cols] * ahead[k] * (
                taps_ref[CONV - 1 - k : CONV - k, cols]
            )
            small_ref[CONV - 1 - k : CONV - k, cols] += jnp.sum(
                grad_here * back[k] * ext_ref[8 - k : 8 - k + SPAN, cols], axis=0, keepdims=True
            )
        pre_grad_ref[:, inner + at : inner + at + LANES] = total.astype(bf16)

    pre_grads = pre_grad_ref[...]
    total_ref[0] = mm(pre_grads, weight_ref[...], NT).astype(bf16)
    weight_acc[...] += mm(normed_ref[...], pre_grads, TN)

    @pl.when(step == blocks - 1)
    def _():
        span = weight_acc.shape[1]
        wide_grad_ref[:, :span] = weight_acc[...].astype(bf16)
        wide_grad_ref[:, span:] = out_acc[...].astype(bf16)
        products = weight_acc[...] * weight_ref[...].astype(f32)
        ones = jnp.ones((8, span), bf16)
        sums = sum(mm(ones, piece, NT) for piece in split(products, 3))
        width = gain_ref.shape[1]
        small_ref[0:1, conv_width : conv_width + width] = sums[0:1, :] / gain_ref[0:1, :]


def swap(values, axis, bit):
    size = lax.axis_size(axis)
    return lax.ppermute(values, axis, [(i, i ^ bit) for i in range(size)])


def bits_of(size):
    return [1 << k for k in range(size.bit_length() - 1)]


def sum_over(values, axis):
    for bit in bits_of(lax.axis_size(axis)):
        values = values + swap(values, axis, bit)
    return values


def gather_relative(values, axis):
    pieces = {0: values}
    for bit in reversed(bits_of(lax.axis_size(axis))):
        pieces.update({k | bit: swap(piece, axis, bit) for k, piece in list(pieces.items())})
    return jnp.stack([pieces[k] for k in range(len(pieces))])


def scatter_relative(pieces, axis):
    kept = [pieces[k] for k in range(pieces.shape[0])]
    for bit in bits_of(lax.axis_size(axis)):
        half = range(0, len(kept), 2)
        kept = [
            kept[k].astype(f32) + swap(kept[k + 1], axis, bit).astype(f32) for k in reversed(half)
        ][::-1]
        if len(kept) > 1:
            kept = [piece.astype(bf16) for piece in kept]
    return kept[0]


def line_gather(values, axis):
    size = lax.axis_size(axis)
    length = size // 2
    place = lax.axis_index(axis)
    at, side = place // 2, place % 2
    ahead, behind = [values], [values]
    for s in range(1, length):
        ahead.append(
            lax.ppermute(ahead[-1], axis, [(i, i + 2) for i in range(size - 2) if i // 2 >= s - 1])
        )
        behind.append(
            lax.ppermute(
                behind[-1], axis, [(i + 2, i) for i in range(size - 2) if i // 2 < length - s]
            )
        )
    result = jnp.zeros((length, 2) + values.shape, values.dtype)
    for s in range(length):
        if s == 0:
            piece, other = values, swap(values, axis, 1)
        else:
            over = lambda v, ok: lax.ppermute(
                v, axis, [(i, i ^ 1) for i in range(size) if ok(i // 2)]
            )
            piece = jnp.where(at >= s, ahead[s], behind[length - s])
            other = jnp.where(
                at >= s,
                over(ahead[s], lambda h: h >= s),
                over(behind[length - s], lambda h: h < s),
            )
        slot = lax.rem(at - s + length, length)
        for block, row in ((piece, side), (other, 1 - side)):
            result = lax.dynamic_update_slice(
                result, block[None, None], (slot, row) + (0,) * values.ndim
            )
    return result.reshape((size,) + values.shape)


def line_scatter(pieces, axis):
    size = lax.axis_size(axis)
    length = size // 2
    place = lax.axis_index(axis)
    at, side = place // 2, place % 2
    pieces = pieces.reshape((length, 2) + pieces.shape[1:])
    mine = lax.dynamic_index_in_dim(pieces, side, 1, keepdims=False)
    theirs = lax.dynamic_index_in_dim(pieces, 1 - side, 1, keepdims=False)
    folded = (mine.astype(f32) + swap(theirs, axis, 1).astype(f32)).astype(bf16)
    own = lambda where: lax.dynamic_index_in_dim(
        folded, jnp.clip(where, 0, length - 1), 0, keepdims=False
    ).astype(f32)
    ahead = behind = None
    for s in range(1, length):
        right = own(at + length - s)
        left = own(at - length + s)
        if s > 1:
            right = right + ahead.astype(f32)
            left = left + behind.astype(f32)
        ahead = lax.ppermute(
            right.astype(bf16), axis, [(i, i + 2) for i in range(size - 2) if i // 2 < s]
        )
        behind = lax.ppermute(
            left.astype(bf16), axis, [(i + 2, i) for i in range(size - 2) if i // 2 + 1 >= length - s]
        )
    result = own(at)
    if length > 1:
        result = result + ahead.astype(f32) + behind.astype(f32)
    return result


def per_device(
    hidden_rows,
    out_grad,
    doc_lengths,
    zx_weight,
    step_weight,
    bc_weight,
    conv_inner,
    conv_shared,
    out_weight,
    decay_log,
    step_bias,
    skip_gain,
    norm_gain,
    gate_gain,
):
    piece_len, _, width = hidden_rows.shape
    tensor = lax.axis_size("tensor")
    data = lax.axis_size("dp")
    full_len = piece_len * tensor
    blocks = full_len // SPAN
    per_piece = piece_len // SPAN
    share = zx_weight.shape[1]
    inner = zx_weight.shape[2]
    heads = step_weight.shape[1]
    head_dim = inner // heads
    state_count = bc_weight.shape[1] // 2
    conv_width = inner + 2 * state_count
    step_at = inner + conv_width
    span = step_at + LANES
    inner_total = float(inner * tensor)
    mine = lax.axis_index("tensor")

    hidden = hidden_rows[:, 0, :]
    grad_local = out_grad[:, 0, :]
    hidden_all = gather_relative(hidden, "tensor")
    shard = jnp.concatenate(
        [
            zx_weight[0],
            zx_weight[1],
            bc_weight,
            jnp.pad(step_weight, ((0, 0), (0, LANES - heads))),
            out_weight.T,
        ],
        axis=1,
    )
    params = jnp.concatenate([norm_gain, conv_inner.reshape(-1), conv_shared])[None, :]
    params_all = line_gather(params, "dp").reshape(data, -1).astype(f32)
    weights = line_gather(shard, "dp").reshape(width, -1)
    weight_in = weights[:, :span]
    weight_out = weights[:, span:]
    grad_all = gather_relative(grad_local, "tensor")

    gain_row = params_all[:, :share].reshape(1, width)
    inner_size = conv_inner.size
    taps_inner = (
        params_all[:, share : share + inner_size]
        .reshape(data, heads, -1)
        .transpose(1, 0, 2)
        .reshape(inner, CONV)
    )
    taps_shared = params_all[:, share + inner_size :].reshape(2 * state_count, CONV)
    taps = jnp.pad(jnp.concatenate([taps_inner, taps_shared]).T, ((0, 4), (0, 0)))
    chan = jnp.pad(
        jnp.stack([jnp.repeat(skip_gain, head_dim), gate_gain]), ((0, 6), (0, 0))
    )
    head_rows = jnp.pad(
        jnp.stack([-jnp.exp(decay_log), step_bias]), ((0, 6), (0, LANES - heads))
    )
    gain_rows = jnp.broadcast_to(gain_row, (8, width))
    expand = (
        jnp.arange(LANES)[:, None] == jnp.arange(inner)[None, :] // head_dim
    ).astype(bf16)
    gather = expand.T
    ends = jnp.cumsum(doc_lengths[0].astype(jnp.int32))[:3]
    info = jnp.concatenate([ends, mine[None].astype(jnp.int32)])

    fixed = lambda shape: pl.BlockSpec(shape, lambda i, info: (0,) * len(shape))
    limits = pltpu.CompilerParams(
        dimension_semantics=("arbitrary",), vmem_limit_bytes=56 * 1024 * 1024
    )
    piece_spec = pl.BlockSpec(
        (1, SPAN, width),
        lambda i, info: ((i // per_piece) ^ info[3], i % per_piece, 0),
    )
    rows = lambda cols: pl.BlockSpec((SPAN, cols), lambda i, info: (i, 0))
    shaped = jax.ShapeDtypeStruct
    normed, pre, y_val, mixed, cum, entering = pl.pallas_call(
        functools.partial(forward_kernel, inner, state_count, heads),
        grid_spec=pltpu.PrefetchScalarGridSpec(
            num_scalar_prefetch=1,
            grid=(blocks,),
            in_specs=[
                piece_spec,
                fixed((width, span)),
                fixed(taps.shape),
                fixed(chan.shape),
                fixed(head_rows.shape),
                fixed(gain_rows.shape),
                fixed(expand.shape),
            ],
            out_specs=[
                rows(width),
                rows(span),
                rows(inner),
                rows(inner),
                rows(LANES),
                pl.BlockSpec((state_count, inner), lambda i, info: (i, 0)),
            ],
            scratch_shapes=[
                pltpu.VMEM((SPAN + 8, conv_width), f32),
                pltpu.VMEM((state_count, inner), f32),
            ],
        ),
        out_shape=[
            shaped((full_len, width), bf16),
            shaped((full_len, span), f32),
            shaped((full_len, inner), f32),
            shaped((full_len, inner), f32),
            shaped((full_len, LANES), f32),
            shaped((blocks * state_count, inner), f32),
        ],
        compiler_params=limits,
        name="forward",
    )(info, hidden_all, weight_in, taps, chan, head_rows, gain_rows, expand)

    branch, stats = pl.pallas_call(
        lambda info_ref, *refs: branch_kernel(*refs),
        grid_spec=pltpu.PrefetchScalarGridSpec(
            num_scalar_prefetch=1,
            grid=(blocks,),
            in_specs=[rows(inner), piece_spec, fixed((width, inner)), fixed(chan.shape)],
            out_specs=[piece_spec, pl.BlockSpec((8, SPAN), lambda i, info: (0, i))],
        ),
        out_shape=[
            shaped((tensor, piece_len, width), bf16),
            shaped((8, full_len), f32),
        ],
        compiler_params=limits,
        name="branch",
    )(info, mixed, grad_all, weight_out, chan)

    stats = sum_over(stats, "tensor")
    branch_local = scatter_relative(branch, "tensor")
    gate_scale = lax.rsqrt(
        lax.dynamic_slice_in_dim(stats[0], mine * piece_len, piece_len) / inner_total + epsilon
    )
    residual = hidden.astype(f32)
    block_out = (residual + branch_local * gate_scale[:, None]).astype(bf16)

    back = lambda i: blocks - 1 - i
    back_piece = pl.BlockSpec(
        (1, SPAN, width),
        lambda i, info: ((back(i) // per_piece) ^ info[3], back(i) % per_piece, 0),
    )
    back_rows = lambda cols: pl.BlockSpec((SPAN, cols), lambda i, info: (back(i), 0))
    small_width = conv_width + width
    total, wide_grad, small = pl.pallas_call(
        functools.partial(backward_kernel, inner, state_count, heads, inner_total),
        grid_spec=pltpu.PrefetchScalarGridSpec(
            num_scalar_prefetch=1,
            grid=(blocks,),
            in_specs=[
                pl.BlockSpec((8, SPAN), lambda i, info: (0, back(i))),
                back_piece,
                back_rows(width),
                fixed((width, span)),
                fixed((width, inner)),
                back_rows(span),
                pl.BlockSpec(
                    (8, span), lambda i, info: (jnp.maximum(back(i) * (SPAN // 8) - 1, 0), 0)
                ),
                back_rows(inner),
                back_rows(LANES),
                pl.BlockSpec((state_count, inner), lambda i, info: (back(i), 0)),
                fixed(taps.shape),
                fixed(chan.shape),
                fixed(head_rows.shape),
                fixed(gain_rows.shape),
                fixed(expand.shape),
                fixed(gather.shape),
            ],
            out_specs=[
                back_piece,
                fixed((width, span + inner)),
                fixed((8, small_width)),
            ],
            scratch_shapes=[
                pltpu.VMEM((SPAN + 8, conv_width), f32),
                pltpu.VMEM((SPAN + 8, conv_width), f32),
                pltpu.VMEM((state_count, inner), f32),
                pltpu.VMEM((width, span), f32),
                pltpu.VMEM((width, inner), f32),
                pltpu.VMEM((SPAN, span), bf16),
            ],
        ),
        out_shape=[
            shaped((tensor, piece_len, width), bf16),
            shaped((width, span + inner), bf16),
            shaped((8, small_width), f32),
        ],
        compiler_params=limits,
        name="backward",
    )(
        info,
        stats,
        grad_all,
        normed,
        weight_in,
        weight_out,
        pre,
        pre,
        y_val,
        cum,
        entering,
        taps,
        chan,
        head_rows,
        gain_rows,
        expand,
        gather,
    )

    normed_grad = scatter_relative(total, "tensor")
    parts = line_scatter(wide_grad.reshape(data, share, span + inner), "dp")
    small = sum_over(small, "dp")
    shared_small = sum_over(small[:, inner:], "tensor")
    bc_part = sum_over(parts[:, 2 * inner : step_at], "tensor")

    row_scale = lax.rsqrt(jnp.mean(residual * residual, axis=1, keepdims=True) + epsilon)
    scaled_grad = normed_grad * gain_row
    hidden_grad = row_scale * scaled_grad - residual * row_scale**3 * jnp.mean(
        scaled_grad * residual, axis=1, keepdims=True
    )
    hidden_grad = (hidden_grad + grad_local.astype(f32)).astype(bf16)

    place = lax.axis_index("dp")
    local = lambda values: lax.dynamic_slice_in_dim(
        values, place * (values.shape[-1] // data), values.shape[-1] // data, values.ndim - 1
    )
    inner_grad = local(small[:CONV, :inner].T.reshape(heads, -1))
    shared_grad = local(shared_small[:CONV, : 2 * state_count].T.reshape(-1))
    norm_grad = local(shared_small[0, 2 * state_count :])
    return (
        block_out[:, None, :],
        hidden_grad[:, None, :],
        jnp.stack([parts[:, :inner], parts[:, inner : 2 * inner]]),
        parts[:, step_at : step_at + heads],
        bc_part,
        inner_grad,
        shared_grad,
        parts[:, span:].T,
        small[6, :heads],
        small[7, :heads],
        jnp.sum(small[4, :inner].reshape(heads, head_dim), axis=1),
        norm_grad,
        small[5, :inner],
    )


def solution(mesh):
    in_specs = (
        P("tensor", "dp", None),
        P("tensor", "dp", None),
        P("dp", None),
        P(None, "dp", "tensor"),
        P("dp", "tensor"),
        P("dp", None),
        P("tensor", "dp"),
        P("dp"),
        P("tensor", "dp"),
        P("tensor"),
        P("tensor"),
        P("tensor"),
        P("dp"),
        P("tensor"),
    )
    out_specs = (
        P("tensor", "dp", None),
        P("tensor", "dp", None),
        P(None, "dp", "tensor"),
        P("dp", "tensor"),
        P("dp", None),
        P("tensor", "dp"),
        P("dp"),
        P("tensor", "dp"),
        P("tensor"),
        P("tensor"),
        P("tensor"),
        P("dp"),
        P("tensor"),
    )
    return jax.shard_map(
        per_device, mesh=mesh, in_specs=in_specs, out_specs=out_specs, check_vma=False
    )
```

```python
import functools

import jax
import jax.numpy as jnp
import numpy as np
from jax import lax
from jax.experimental import pallas as pl
from jax.experimental.pallas import tpu as pltpu
from jax.sharding import PartitionSpec as P

CONV = 4
SPAN = 256
LANES = 128
TAPS_AT = 8
GAIN_AT = 12
GATE_AT = 16
HEAD_AT = 64
epsilon = 1e-05
bf16 = jnp.bfloat16
f32 = jnp.float32
NN = (((1,), (0,)), ((), ()))
NT = (((1,), (1,)), ((), ()))
TN = (((0,), (0,)), ((), ()))


def mm(left, right, dims=NN):
    return lax.dot_general(left, right, dims, preferred_element_type=f32)


def split(values, parts):
    pieces = []
    for _ in range(parts):
        piece = values.astype(bf16)
        pieces.append(piece)
        values = values - piece.astype(f32)
    return pieces


def mm_left_exact(left, right, parts):
    return sum(mm(left, piece) for piece in split(right, parts))


def mm_right_exact(left, right, parts):
    return sum(mm(piece, right) for piece in split(left, parts))


def sigmoid(values):
    return 1.0 / (1.0 + jnp.exp(-values))


def softplus(values):
    return jnp.maximum(values, 0.0) + jnp.log1p(jnp.exp(-jnp.abs(values)))


def doc_start(position, ends):
    start = jnp.zeros_like(position)
    for end in ends:
        start = jnp.where(position >= end, end, start)
    return start


def scalar_start(position, ends):
    start = jnp.int32(0)
    for end in ends:
        start = jnp.where(position >= end, end, start)
    return start


def iota(shape, dim):
    return lax.broadcasted_iota(jnp.int32, shape, dim)


def tap_row(rows_ref, back, cols):
    at = TAPS_AT + CONV - 1 - back
    return rows_ref[at : at + 1, cols]


def conv_block(ext_ref, rows_ref, position, start, width):
    masks = [None] + [(position - k >= start).astype(f32) for k in range(1, CONV)]
    groups = []
    for at in range(0, width, LANES):
        cols = slice(at, at + LANES)
        total = ext_ref[8 : 8 + SPAN, cols] * tap_row(rows_ref, 0, cols)
        for k in range(1, CONV):
            total = total + ext_ref[8 - k : 8 - k + SPAN, cols] * masks[k] * (
                tap_row(rows_ref, k, cols)
            )
        groups.append(total)
    return jnp.concatenate(groups, axis=1)


def wide(mask, width):
    return jnp.concatenate([mask] * (width // LANES), axis=1)


def pick_piece(block, per_piece, mine, refs, chosen_ref):
    relative = (block // per_piece) ^ mine
    for k, ref in enumerate(refs):

        @pl.when(relative == k)
        def _(ref=ref):
            chosen_ref[...] = ref[...]


def forward_kernel(
    inner,
    state_count,
    heads,
    per_piece,
    pieces,
    info_ref,
    *refs,
):
    hidden_refs, refs = refs[:pieces], refs[pieces:]
    (
        weight_ref,
        choose_ref,
        chan_ref,
        head_ref,
        expand_ref,
        normed_ref,
        pre_ref,
        y_ref,
        cum_ref,
        entering_ref,
        rows_ref,
        ext_ref,
        state_ref,
        hidden_ref,
    ) = refs
    block = pl.program_id(0)
    conv_width = inner + 2 * state_count
    ends = [info_ref[k] for k in range(3)]
    base = block * SPAN

    @pl.when(block == 0)
    def _():
        ext_ref[...] = jnp.zeros_like(ext_ref)
        state_ref[...] = jnp.zeros_like(state_ref)
        rows_ref[...] = mm(weight_ref[:, conv_width:], choose_ref[...], TN)[0:16, :]

    pick_piece(block, per_piece, info_ref[3], hidden_refs, hidden_ref)
    residual = hidden_ref[...].astype(f32)
    row_scale = lax.rsqrt(jnp.mean(residual * residual, axis=1, keepdims=True) + epsilon)
    normed = (residual * row_scale * rows_ref[GAIN_AT : GAIN_AT + 1, conv_width:]).astype(bf16)
    normed_ref[...] = normed
    pre = mm(normed, weight_ref[...])
    pre_ref[...] = pre

    ext_ref[0:8, :] = ext_ref[SPAN : SPAN + 8, :]
    ext_ref[8 : 8 + SPAN, :] = pre[:, :conv_width]
    position = base + iota((SPAN, LANES), 0)
    start = doc_start(position, ends)
    conv = conv_block(ext_ref, rows_ref, position, start, conv_width)
    active = conv * sigmoid(conv)
    x_val = active[:, :inner].astype(bf16).astype(f32)
    in_map = active[:, inner : inner + state_count].astype(bf16)
    out_map = active[:, inner + state_count :].astype(bf16)

    step_size = softplus(pre[:, conv_width:] + head_ref[1:2, :])
    log_decay = step_size * head_ref[0:1, :]
    row_at = iota((SPAN, SPAN), 0)
    col_at = iota((SPAN, SPAN), 1)
    lower = (col_at <= row_at).astype(f32).astype(bf16)
    cum = mm_left_exact(lower, log_decay, 3)
    cum_ref[...] = cum
    cum_rows = cum.T

    start_last = scalar_start(base + SPAN - 1, ends)
    keep = (start < base).astype(f32)
    tail = (position >= start_last).astype(f32)
    survives = (start_last < base).astype(f32)
    expand = expand_ref[...]
    step_wide = mm_right_exact(step_size, expand, 2)
    decay_wide = mm_right_exact(jnp.exp(cum), expand, 2)
    into_wide = mm_right_exact(jnp.exp(cum[SPAN - 1 :, :] - cum) * tail, expand, 2)

    x_step = x_val * step_wide
    x_step_low = x_step.astype(bf16)
    state = state_ref[...]
    entering_ref[...] = state
    outside = mm(out_map, state.astype(bf16)) * (decay_wide * wide(keep, inner))
    visible = (col_at <= row_at) & (base + col_at >= wide(start, SPAN))
    scores = jnp.where(visible, mm(out_map, in_map, NT), 0.0)
    upper_half = iota((SPAN, LANES), 1) >= LANES // 2
    inside = []
    for pair in range(heads // 2):
        x_pair = x_step_low[:, pair * LANES : (pair + 1) * LANES]
        total = None
        for which in range(2):
            head = 2 * pair + which
            gap = cum[:, head : head + 1] - cum_rows[head : head + 1, :]
            mixing = (scores * jnp.exp(jnp.minimum(gap, 0.0))).astype(bf16)
            chosen = upper_half if which else jnp.logical_not(upper_half)
            part = mm(mixing, jnp.where(chosen, x_pair, jnp.zeros_like(x_pair)))
            total = part if total is None else total + part
        inside.append(total)
    y_val = jnp.concatenate(inside, axis=1) + outside + chan_ref[0:1, :] * x_val
    y_ref[...] = y_val

    scaled = (x_step * into_wide).astype(bf16)
    state_ref[...] = (decay_wide[SPAN - 1 :, :] * survives) * state + mm(in_map, scaled, TN)


def branch_kernel(per_piece, pieces, info_ref, *refs):
    grad_refs, refs = refs[:pieces], refs[pieces:]
    normed_ref, y_ref, gate_w_ref, out_ref, chan_ref = refs[:5]
    gate_ref, branch_ref, stats_ref, grad_ref = refs[5:]
    block = pl.program_id(0)
    pick_piece(block, per_piece, info_ref[3], grad_refs, grad_ref)
    gate = mm(normed_ref[...], gate_w_ref[...])
    gate_ref[...] = gate
    mixed = y_ref[...] * (gate * sigmoid(gate))
    out_w = out_ref[...]
    gain = chan_ref[1:2, :]
    branch_ref[...] = mm((mixed * gain).astype(bf16), out_w, NT).astype(bf16)
    weighted = mm(grad_ref[...], out_w) * gain
    squares = jnp.sum(mixed * mixed, axis=1, keepdims=True)
    crossed = jnp.sum(weighted * mixed, axis=1, keepdims=True)
    lane = iota((mixed.shape[0], LANES), 1)
    both = jnp.where(lane == 0, squares, jnp.where(lane == 1, crossed, 0.0))
    stats_ref[...] = both.T[0:8, :]


def product_sums(left, right):
    ones = jnp.ones((8, left.shape[1]), bf16)
    return sum(mm(ones, piece, NT) for piece in split(left * right.astype(f32), 3))


def gate_kernel(inner, inner_total, per_piece, pieces, info_ref, *refs):
    grad_refs, refs = refs[:pieces], refs[pieces:]
    (
        stats_ref,
        normed_ref,
        gate_w_ref,
        out_ref,
        gate_ref,
        y_ref,
        chan_ref,
        gate_grad_ref,
        y_grad_ref,
        early_ref,
        gain_grad_ref,
        product_ref,
        gate_acc,
        out_acc,
        grad_ref,
    ) = refs
    block = pl.program_id(0)

    @pl.when(block == 0)
    def _():
        gate_acc[...] = jnp.zeros_like(gate_acc)
        out_acc[...] = jnp.zeros_like(out_acc)
        gain_grad_ref[...] = jnp.zeros_like(gain_grad_ref)

    pick_piece(block, per_piece, info_ref[3], grad_refs, grad_ref)
    stats = stats_ref[...].T
    gate_scale = lax.rsqrt(stats[:, 0:1] / inner_total + epsilon)
    crossed = stats[:, 1:2] / inner_total
    gate = gate_ref[...]
    gate_sig = sigmoid(gate)
    gate_act = gate * gate_sig
    y_val = y_ref[...]
    mixed = y_val * gate_act
    grad = grad_ref[...]
    gain = chan_ref[1:2, :]
    gated_grad = mm(grad, out_ref[...])
    scaled_mixed = mixed * gate_scale
    out_acc[...] += mm(grad, (scaled_mixed * gain).astype(bf16), TN)
    gain_grad_ref[0:1, :] += jnp.sum(gated_grad * scaled_mixed, axis=0, keepdims=True)
    mixed_grad = gate_scale * (gated_grad * gain) - scaled_mixed * (
        gate_scale * gate_scale * crossed
    )
    gate_grad = mixed_grad * y_val * (gate_sig * (1.0 + gate * (1.0 - gate_sig)))
    gate_grad = gate_grad.astype(bf16)
    gate_grad_ref[...] = gate_grad
    y_grad_ref[...] = mixed_grad * gate_act
    gate_acc[...] += mm(normed_ref[...], gate_grad, TN)

    @pl.when(block == pl.num_programs(0) - 1)
    def _():
        early_ref[:, :inner] = gate_acc[...].astype(bf16)
        early_ref[:, inner:] = out_acc[...].astype(bf16)
        product_ref[...] = product_sums(gate_acc[...], gate_w_ref[...])


def backward_kernel(inner, state_count, heads, blocks, at, final, info_ref, *refs):
    (
        normed_ref,
        weight_ref,
        gate_w_ref,
        pre_ref,
        halo_ref,
        y_ref,
        y_grad_ref,
        gate_grad_ref,
        cum_ref,
        entering_ref,
        rows_ref,
        chan_ref,
        head_ref,
        expand_ref,
        gather_ref,
    ) = refs[:15]
    refs = refs[15:]
    if at:
        next_in, state_in, late_in, small_in, head_in, product_ref, choose_ref, extra_ref, _ = refs[:9]
        refs = refs[9:]
    total_ref = refs[0]
    if final:
        late_ref = refs[1]
        ext_ref, next_ref, pre_grad_ref, state_grad_ref, late_acc, small_ref, heads_ref = refs[2:]
    else:
        next_out, state_grad_ref, late_acc, small_ref, heads_ref = refs[1:6]
        ext_ref, next_ref, pre_grad_ref = refs[6:]
    step = pl.program_id(0)
    block = blocks - 1 - at - step
    base = block * SPAN
    conv_width = inner + 2 * state_count
    ends = [info_ref[k] for k in range(3)]

    @pl.when(step == 0)
    def _():
        if at:
            next_ref[0:8, :] = next_in[...]
            state_grad_ref[...] = state_in[...]
            late_acc[...] = late_in[...]
            small_ref[...] = small_in[...]
            heads_ref[...] = head_in[...]
        else:
            next_ref[...] = jnp.zeros_like(next_ref)
            state_grad_ref[...] = jnp.zeros_like(state_grad_ref)
            late_acc[...] = jnp.zeros_like(late_acc)
            small_ref[...] = jnp.zeros_like(small_ref)
            heads_ref[...] = jnp.zeros_like(heads_ref)

    skip = chan_ref[0:1, :]
    y_val = y_ref[...]
    y_grad = y_grad_ref[...]

    ext_ref[0:8, :] = halo_ref[:, :conv_width]
    ext_ref[8 : 8 + SPAN, :] = pre_ref[:, :conv_width]
    position = base + iota((SPAN, LANES), 0)
    start = doc_start(position, ends)
    conv = conv_block(ext_ref, rows_ref, position, start, conv_width)
    conv_sig = sigmoid(conv)
    active = conv * conv_sig
    act_slope = conv_sig * (1.0 + conv * (1.0 - conv_sig))
    x_val = active[:, :inner].astype(bf16).astype(f32)
    in_map = active[:, inner : inner + state_count].astype(bf16)
    out_map = active[:, inner + state_count :].astype(bf16)

    step_pre = pre_ref[:, conv_width:] + head_ref[1:2, :]
    step_size = softplus(step_pre)
    rates = head_ref[0:1, :]
    cum = cum_ref[...]
    cum_rows = cum.T
    start_last = scalar_start(base + SPAN - 1, ends)
    keep = (start < base).astype(f32)
    tail = (position >= start_last).astype(f32)
    survives = (start_last < base).astype(f32)
    expand = expand_ref[...]
    step_wide = mm_right_exact(step_size, expand, 2)
    decay_wide = mm_right_exact(jnp.exp(cum), expand, 2)
    into_wide = mm_right_exact(jnp.exp(cum[SPAN - 1 :, :] - cum) * tail, expand, 2)
    keep_decay = decay_wide * wide(keep, inner)
    last_decay = decay_wide[SPAN - 1 :, :] * survives

    x_step = x_val * step_wide
    x_step_low = x_step.astype(bf16)
    scaled = (x_step * into_wide).astype(bf16)
    entering = entering_ref[...]
    entering_low = entering.astype(bf16)
    y_grad_low = y_grad.astype(bf16)
    state_grad = state_grad_ref[...]
    state_grad_low = state_grad.astype(bf16)

    outside = mm(out_map, entering_low)
    outside_grad = (y_grad * keep_decay).astype(bf16)
    scaled_grad = mm(in_map, state_grad_low)
    out_map_grad = mm(outside_grad, entering_low, NT)
    in_map_grad = mm(scaled, state_grad_low, NT)
    state_grad_ref[...] = last_decay * state_grad + mm(out_map, outside_grad, TN)

    row_at = iota((SPAN, SPAN), 0)
    col_at = iota((SPAN, SPAN), 1)
    col_start = doc_start(base + col_at, ends)
    visible = (row_at <= col_at) & (base + row_at >= col_start)
    scores = jnp.where(visible, mm(in_map, out_map, NT), 0.0)
    upper_half = iota((SPAN, LANES), 1) >= LANES // 2
    score_grad = jnp.zeros((SPAN, SPAN), f32)
    x_step_grads = []
    for pair in range(heads // 2):
        x_pair = x_step_low[:, pair * LANES : (pair + 1) * LANES]
        grad_pair = y_grad_low[:, pair * LANES : (pair + 1) * LANES]
        total = None
        for which in range(2):
            head = 2 * pair + which
            chosen = upper_half if which else jnp.logical_not(upper_half)
            grad_head = jnp.where(chosen, grad_pair, jnp.zeros_like(grad_pair))
            gap = cum_rows[head : head + 1, :] - cum[:, head : head + 1]
            decays = jnp.exp(jnp.minimum(gap, 0.0))
            score_grad = score_grad + mm(x_pair, grad_head, NT) * decays
            part = mm((scores * decays).astype(bf16), grad_head)
            total = part if total is None else total + part
        x_step_grads.append(total)
    x_step_grad = jnp.concatenate(x_step_grads, axis=1)
    score_grad = jnp.where(visible, score_grad, 0.0).astype(bf16)
    in_map_grad = in_map_grad + mm(score_grad, out_map)
    out_map_grad = out_map_grad + mm(score_grad, in_map, TN)

    inside = y_val - skip * x_val - keep_decay * outside
    into_terms = scaled.astype(f32) * scaled_grad
    cum_terms = (
        y_grad_low.astype(f32) * inside
        + outside_grad.astype(f32) * outside
        - x_step_low.astype(f32) * x_step_grad
        - into_terms
    )
    last_terms = jnp.sum(into_terms, axis=0, keepdims=True) + last_decay * jnp.sum(
        state_grad * entering, axis=0, keepdims=True
    )
    last_row = iota((SPAN, inner), 0) == SPAN - 1
    cum_terms = cum_terms + jnp.where(last_row, last_terms, 0.0)
    x_step_grad = x_step_grad + into_wide * scaled_grad
    gather = gather_ref[...]
    cum_grad = mm_right_exact(cum_terms, gather, 2)
    step_grad = mm_right_exact(x_val * x_step_grad, gather, 2)
    upper = (row_at <= col_at).astype(f32).astype(bf16)
    log_grad = mm_left_exact(upper, cum_grad, 3)
    step_grad = (step_grad + log_grad * rates) * sigmoid(step_pre)
    pre_grad_ref[:, conv_width:] = step_grad.astype(bf16)
    x_grad = skip * y_grad + step_wide * x_step_grad

    heads_ref[0:1, :] += jnp.sum(y_grad * x_val, axis=0, keepdims=True)
    heads_ref[1:2, :LANES] += jnp.sum(step_size * rates * log_grad, axis=0, keepdims=True)
    heads_ref[2:3, :LANES] += jnp.sum(step_grad, axis=0, keepdims=True)

    conv_grad = jnp.concatenate([x_grad, in_map_grad, out_map_grad], axis=1) * act_slope
    next_ref[SPAN : SPAN + 8, :] = next_ref[0:8, :]
    next_ref[0:SPAN, :] = conv_grad
    back = [None] + [(position - k >= start).astype(f32) for k in range(1, CONV)]
    ahead = [None] + [
        (position >= doc_start(position + k, ends)).astype(f32) for k in range(1, CONV)
    ]
    for col in range(0, conv_width, LANES):
        cols = slice(col, col + LANES)
        grad_here = next_ref[0:SPAN, cols]
        total = grad_here * tap_row(rows_ref, 0, cols)
        small_ref[TAPS_AT + CONV - 1 : TAPS_AT + CONV, cols] += jnp.sum(
            grad_here * ext_ref[8 : 8 + SPAN, cols], axis=0, keepdims=True
        )
        for k in range(1, CONV):
            total = total + next_ref[k : k + SPAN, cols] * ahead[k] * (
                tap_row(rows_ref, k, cols)
            )
            small_ref[TAPS_AT + CONV - 1 - k : TAPS_AT + CONV - k, cols] += jnp.sum(
                grad_here * back[k] * ext_ref[8 - k : 8 - k + SPAN, cols], axis=0, keepdims=True
            )
        pre_grad_ref[:, cols] = total.astype(bf16)

    pre_grads = pre_grad_ref[...]
    total = mm(pre_grads, weight_ref[...], NT) + mm(gate_grad_ref[...], gate_w_ref[...], NT)
    total_ref[...] = total.astype(bf16)
    late_acc[...] += mm(normed_ref[...], pre_grads, TN)

    @pl.when(step == pl.num_programs(0) - 1)
    def _():
        if final:
            late = late_acc[...]
            sums = product_sums(late, weight_ref[...]) + product_ref[...]
            gain = rows_ref[GAIN_AT : GAIN_AT + 1, conv_width:]
            small_ref[GAIN_AT : GAIN_AT + 1, conv_width:] = sums[0:1, :] / gain
            chosen = small_ref[...].astype(bf16)
            filler = jnp.zeros((LANES - chosen.shape[0], chosen.shape[1]), bf16)
            misc = mm(choose_ref[...], jnp.concatenate([chosen, filler], axis=0), NT)
            totals = heads_ref[...]
            skips = mm_right_exact(totals, gather_ref[...], 2)
            per_head = [totals[1:2, :LANES], totals[2:3, :LANES], skips[0:1, :]]
            for at_head, value in enumerate(per_head):
                value = jnp.broadcast_to(value, (8, LANES))
                misc = misc + pltpu.roll(value, HEAD_AT + at_head * heads, 1)[0:1, :]
            late_ref[:, :conv_width] = late[:, :conv_width].astype(bf16)
            late_ref[:, conv_width:] = (late[:, conv_width:] + misc + extra_ref[...]).astype(bf16)
        else:
            next_out[...] = next_ref[0:8, :]


def swap(values, axis, bits):
    size = lax.axis_size(axis)
    return lax.ppermute(values, axis, [(i, i ^ bits) for i in range(size)])


def bits_of(size):
    return [1 << k for k in range(size.bit_length() - 1)]


def after(values, *others):
    return lax.optimization_barrier((values,) + others)[0]


def sum_over(values, axis):
    size = lax.axis_size(axis)
    if size > 8:
        for bit in bits_of(size):
            values = values + swap(values, axis, bit)
        return values
    return tree_sum([values] + [swap(values, axis, k) for k in range(1, size)])


def tree_sum(pieces):
    while len(pieces) > 1:
        pieces = [pieces[k] + pieces[k + 1] for k in range(0, len(pieces), 2)]
    return pieces[0]


def gather_far(values, axis):
    pieces = {0: values}
    bits = bits_of(lax.axis_size(axis))
    for bit in reversed(bits[1:]):
        pieces.update({k | bit: swap(piece, axis, bit) for k, piece in list(pieces.items())})
    pieces[1] = swap(values, axis, 1)
    return pieces


def gather_near(pieces, axis, *others):
    pieces = dict(pieces)
    for k in list(pieces):
        if k > 1:
            pieces[k | 1] = swap(after(pieces[k], *others) if others else pieces[k], axis, 1)
    return [pieces[k] for k in range(len(pieces))]


def scatter_near(pieces, axis):
    far = {}
    for k in range(len(pieces) - 2, 0, -2):
        both = pieces[k].astype(f32) + swap(pieces[k + 1], axis, 1).astype(f32)
        far[k] = both.astype(bf16)
    return far


def scatter_far(pieces, far, axis, parts=1):
    near = swap(after(pieces[1], *far.values()), axis, 1)
    received = None
    for bit in bits_of(lax.axis_size(axis))[1:]:
        if received is not None:
            far = {
                k: (v.astype(f32) + received[k].astype(f32)).astype(bf16) for k, v in far.items()
            }
        if parts > 1 and len(far) == 1:
            (last,) = far.values()
            size = last.shape[0] // parts
            cuts = [last[at : at + size] for at in range(0, last.shape[0], size)]
            return near, [swap(cut, axis, bit) for cut in cuts]
        received = {
            k ^ bit: swap(v, axis, bit) for k, v in far.items() if k & bit
        }
        far = {k: v for k, v in far.items() if not k & bit}
    return near, received[0] if parts == 1 else received


def gather_direct(values, axis, other):
    size = lax.axis_size(axis)
    place = lax.axis_index(axis)
    near = swap(values, axis, 1)
    far = [swap(values, axis, k) for k in range(size - 2, 0, -2)]
    far, other = lax.optimization_barrier((jnp.stack(far), other))
    beside = swap(far, axis, 1)
    result = jnp.zeros((size,) + values.shape, values.dtype)
    pieces = {0: values, 1: near}
    for at, k in enumerate(range(size - 2, 0, -2)):
        pieces.update({k: far[at], k + 1: beside[at]})
    for k in range(size):
        result = lax.dynamic_update_slice(
            result, pieces[k][None], (place ^ k,) + (0,) * values.ndim
        )
    return result.reshape((-1,) + values.shape[1:])


def gather_pairs(values, axis):
    size = lax.axis_size(axis)
    place = lax.axis_index(axis)
    other = swap(values, axis, 1)
    first = place % 2 == 0
    pair = jnp.stack([jnp.where(first, values, other), jnp.where(first, other, values)])
    result = jnp.zeros((size // 2,) + pair.shape, values.dtype)
    for k in range(0, size, 2):
        piece = swap(pair, axis, k) if k else pair
        result = lax.dynamic_update_slice(
            result, piece[None], ((place ^ k) // 2,) + (0,) * pair.ndim
        )
    return result.reshape((-1,) + values.shape[1:])


def block_of(values, place, share):
    return lax.dynamic_slice_in_dim(values, place * share, share, 0)


def fold_pairs(values, axis, steps):
    size = lax.axis_size(axis)
    place = lax.axis_index(axis)
    share = values.shape[0] // size
    theirs = jnp.stack([block_of(values, place ^ k ^ 1, share) for k in steps])
    return swap(theirs, axis, 1)


def fold_sums(values, theirs, axis, steps):
    place = lax.axis_index(axis)
    share = values.shape[0] // lax.axis_size(axis)
    sums = [
        block_of(values, place ^ k, share).astype(f32) + theirs[at].astype(f32)
        for at, k in enumerate(steps)
    ]
    return [both.astype(bf16) if k else both for k, both in zip(steps, sums)]


def send_sums(folded, axis, steps):
    return [
        swap(both, axis, k) if k else both for k, both in zip(steps, folded)
    ]


def per_device(
    hidden_rows,
    out_grad,
    doc_lengths,
    zx_weight,
    step_weight,
    bc_weight,
    conv_inner,
    conv_shared,
    out_weight,
    decay_log,
    step_bias,
    skip_gain,
    norm_gain,
    gate_gain,
):
    piece_len, _, width = hidden_rows.shape
    tensor = lax.axis_size("tensor")
    data = lax.axis_size("dp")
    full_len = piece_len * tensor
    blocks = full_len // SPAN
    per_piece = piece_len // SPAN
    share = zx_weight.shape[1]
    inner = zx_weight.shape[2]
    heads = step_weight.shape[1]
    head_dim = inner // heads
    state_count = bc_weight.shape[1] // 2
    conv_width = inner + 2 * state_count
    span = conv_width + LANES
    inner_total = float(inner * tensor)
    mine = lax.axis_index("tensor")
    place = lax.axis_index("dp")

    hidden = hidden_rows[:, 0, :]
    hidden_all = gather_far(hidden, "tensor")
    hidden_far = hidden_all[tensor // 2]
    hidden_all = gather_near(hidden_all, "tensor")

    inner_share = conv_inner.size // CONV
    shared_share = conv_shared.size // CONV
    taps = jnp.concatenate([conv_inner.reshape(-1, CONV), conv_shared.reshape(-1, CONV)])
    taps = jnp.pad(taps, ((0, share - inner_share - shared_share), (0, 0)))
    misc = jnp.concatenate(
        [
            jnp.pad(step_weight, ((0, 0), (0, TAPS_AT - heads))),
            taps,
            norm_gain[:, None],
            jnp.zeros((share, LANES - GAIN_AT - 1), bf16),
        ],
        axis=1,
    )
    shard = jnp.concatenate([zx_weight[1], bc_weight, misc], axis=1)
    weights = gather_direct(shard, "dp", hidden_far)
    shard = jnp.concatenate([zx_weight[0], out_weight.T], axis=1)
    weights_late = gather_pairs(shard, "dp")
    grad_all = gather_far(after(out_grad, hidden_far)[:, 0, :], "tensor")

    channel = np.arange(inner)
    per_dev = head_dim // data
    sources = [
        (channel % head_dim) // per_dev * share
        + channel // head_dim * per_dev
        + channel % per_dev,
        np.arange(2 * state_count) // shared_share * share
        + inner_share
        + np.arange(2 * state_count) % shared_share,
        np.arange(width),
    ]
    sources = jnp.asarray(np.concatenate(sources), jnp.int32)
    choose = (jnp.arange(width, dtype=jnp.int32)[:, None] == sources[None, :]).astype(bf16)
    chan = jnp.pad(jnp.stack([jnp.repeat(skip_gain, head_dim), gate_gain]), ((0, 6), (0, 0)))
    head_rows = jnp.pad(
        jnp.stack([-jnp.exp(decay_log), step_bias]), ((0, 6), (0, LANES - heads))
    )
    expand = (jnp.arange(LANES)[:, None] == jnp.arange(inner)[None, :] // head_dim).astype(bf16)
    gather = expand.T
    lengths = doc_lengths[0].astype(jnp.int32)
    info = jnp.stack(
        [lengths[0], lengths[0] + lengths[1], lengths[0] + lengths[1] + lengths[2], mine]
    ).astype(jnp.int32)

    limits = pltpu.CompilerParams(
        dimension_semantics=("arbitrary",), vmem_limit_bytes=56 * 1024 * 1024
    )
    shaped = jax.ShapeDtypeStruct

    def fixed(shape, at=0):
        return pl.BlockSpec(shape, lambda i, info: (0,) * (len(shape) - 1) + (at,))

    def rows(cols, at=0, order=lambda i: i):
        return pl.BlockSpec((SPAN, cols), lambda i, info: (order(i), at))

    def piece_specs(order=lambda i: i):
        return [
            pl.BlockSpec(
                (SPAN, width),
                lambda i, info, k=k: (
                    jnp.clip(order(i) - (info[3] ^ k) * per_piece, 0, per_piece - 1),
                    0,
                ),
            )
            for k in range(tensor)
        ]

    def call(
        kernel, name, micros, steps, in_specs, out_specs, out_shape, scratch, args, aliases={}
    ):
        return pl.pallas_call(
            kernel,
            grid_spec=pltpu.PrefetchScalarGridSpec(
                num_scalar_prefetch=1,
                grid=(steps,),
                in_specs=in_specs,
                out_specs=out_specs,
                scratch_shapes=scratch,
            ),
            out_shape=out_shape,
            compiler_params=limits,
            input_output_aliases=aliases,
            cost_estimate=pl.CostEstimate(
                flops=int(micros * 1.0e9), bytes_accessed=int(micros * 3.0e6), transcendentals=0
            ),
            name=name,
        )(info, *args)

    def relative(order):
        return pl.BlockSpec(
            (SPAN, width),
            lambda i, info: (
                ((order(i) // per_piece) ^ info[3]) * per_piece + order(i) % per_piece,
                0,
            ),
        )

    natural = lambda i: i
    state_spec = lambda order: pl.BlockSpec(
        (state_count, inner), lambda i, info: (order(i), 0)
    )
    normed, pre, y_val, cum, entering, rows_all = call(
        functools.partial(forward_kernel, inner, state_count, heads, per_piece, tensor),
        "forward",
        22,
        blocks,
        piece_specs()
        + [
            fixed((width, span)),
            fixed(choose.shape),
            fixed(chan.shape),
            fixed(head_rows.shape),
            fixed(expand.shape),
        ],
        [
            rows(width),
            rows(span),
            rows(inner),
            rows(LANES),
            state_spec(natural),
            fixed((16, conv_width + width)),
        ],
        [
            shaped((full_len, width), bf16),
            shaped((full_len, span), f32),
            shaped((full_len, inner), f32),
            shaped((full_len, LANES), f32),
            shaped((blocks * state_count, inner), f32),
            shaped((16, conv_width + width), f32),
        ],
        [
            pltpu.VMEM((SPAN + 8, conv_width), f32),
            pltpu.VMEM((state_count, inner), f32),
            pltpu.VMEM((SPAN, width), bf16),
        ],
        (*hidden_all, weights, choose, chan, head_rows, expand),
    )

    tall = lambda cols: pl.BlockSpec((piece_len, cols), lambda i, info: (i, 0))
    whole_pieces = [fixed((piece_len, width))] * tensor
    grad_all = gather_near(grad_all, "tensor", rows_all)
    gate_spec, out_spec = fixed((width, inner)), fixed((width, inner), 1)
    gate, branch, stats = call(
        functools.partial(branch_kernel, 1, tensor),
        "branch",
        11,
        tensor,
        whole_pieces + [tall(width), tall(inner), gate_spec, out_spec, fixed(chan.shape)],
        [tall(inner), pl.BlockSpec((piece_len, width), lambda i, info: (i ^ info[3], 0)), pl.BlockSpec((8, piece_len), lambda i, info: (0, i))],
        [
            shaped((full_len, inner), f32),
            shaped((full_len, width), bf16),
            shaped((8, full_len), f32),
        ],
        [pltpu.VMEM((piece_len, width), bf16)],
        (*grad_all, normed, y_val, weights_late, weights_late, chan),
    )

    cut = lambda values: [
        values[k * piece_len : (k + 1) * piece_len] for k in range(tensor)
    ]
    branch = cut(branch)
    branch_sums = scatter_near(branch, "tensor")
    stats = sum_over(stats, "tensor")

    gate_grad, y_grad, early, gain_grad, product = call(
        functools.partial(gate_kernel, inner, inner_total, 1, tensor),
        "gate_back",
        13,
        tensor,
        whole_pieces
        + [
            pl.BlockSpec((8, piece_len), lambda i, info: (0, i)),
            tall(width),
            gate_spec,
            out_spec,
            tall(inner),
            tall(inner),
            fixed(chan.shape),
        ],
        [
            tall(inner),
            tall(inner),
            fixed((width, 2 * inner)),
            fixed((8, inner)),
            fixed((8, width)),
        ],
        [
            shaped((full_len, inner), bf16),
            shaped((full_len, inner), f32),
            shaped((width, 2 * inner), bf16),
            shaped((8, inner), f32),
            shaped((8, width), f32),
        ],
        [
            pltpu.VMEM((width, inner), f32),
            pltpu.VMEM((width, inner), f32),
            pltpu.VMEM((piece_len, width), bf16),
        ],
        (*grad_all, stats, normed, weights_late, weights_late, gate, y_val, chan),
    )
    far_first = list(range(data - 2, -1, -2))
    early_theirs = fold_pairs(early, "dp", far_first)
    gate_grad, *held = lax.optimization_barrier(
        (gate_grad, *branch_sums.values())
    )
    branch_sums = dict(zip(branch_sums, held))
    branch_near, branch_far = scatter_far(branch, branch_sums, "tensor")

    small_width = conv_width + width
    half = blocks // 2
    carried = [
        shaped((8, conv_width), f32),
        shaped((state_count, inner), f32),
        shaped((width, span), f32),
        shaped((16, small_width), f32),
        shaped((8, inner), f32),
    ]

    def backward(at, steps, final, extra):
        back = lambda i: blocks - 1 - at - i
        back_rows = lambda cols: rows(cols, 0, back)
        extra_specs = [fixed(value.shape) for value in extra[:-1]]
        extra_specs += [pl.BlockSpec(memory_space=pl.ANY)] * len(extra[-1:])
        outs = [shaped((width, span), bf16)] if final else carried
        scratch = [
            pltpu.VMEM((SPAN + 8, conv_width), f32),
            pltpu.VMEM((SPAN + 8, conv_width), f32),
            pltpu.VMEM((SPAN, span), bf16),
        ]
        if final:
            scratch += [pltpu.VMEM(value.shape, f32) for value in carried[1:]]
        return call(
            functools.partial(backward_kernel, inner, state_count, heads, blocks, at, final),
            "backward",
            23,
            steps,
            [
                back_rows(width),
                fixed((width, span)),
                gate_spec,
                back_rows(span),
                pl.BlockSpec(
                    (8, span), lambda i, info: (jnp.maximum(back(i) * (SPAN // 8) - 1, 0), 0)
                ),
                back_rows(inner),
                back_rows(inner),
                back_rows(inner),
                back_rows(LANES),
                state_spec(back),
                fixed((16, small_width)),
                fixed(chan.shape),
                fixed(head_rows.shape),
                fixed(expand.shape),
                fixed(gather.shape),
            ]
            + extra_specs,
            [relative(back)] + [fixed(out.shape) for out in outs],
            [shaped((full_len, width), bf16)] + outs,
            scratch,
            (
                normed,
                weights,
                weights_late,
                pre,
                pre,
                y_val,
                y_grad,
                gate_grad,
                cum,
                entering,
                rows_all,
                chan,
                head_rows,
                expand,
                gather,
                *extra,
            ),
            {24: 0} if extra else {},
        )

    total, next_rows, *rest = backward(0, half, False, ())
    next_rows, early_theirs, branch_near, branch_far = lax.optimization_barrier(
        (next_rows, early_theirs, branch_near, branch_far)
    )
    early_pieces = send_sums(
        fold_sums(early, early_theirs, "dp", far_first), "dp", far_first
    )
    gate_lanes = inner // share
    extra = jnp.tile(gain_grad[0].reshape(gate_lanes, share).T, (data, 1))
    extra = jnp.pad(extra, ((0, 0), (GATE_AT, LANES - GATE_AT - gate_lanes)))
    total, late = backward(
        half, blocks - half, True, (next_rows, *rest, product, choose, extra, total)
    )

    total, late, *early_pieces = lax.optimization_barrier((total, late, *early_pieces))
    total = cut(total)
    total_sums = scatter_near(total, "tensor")
    groups = far_first[: len(far_first) // 2], far_first[len(far_first) // 2 :]
    theirs = [fold_pairs(late, "dp", steps) for steps in groups]
    total_near, total_far = scatter_far(total, total_sums, "tensor")
    theirs[0] = after(theirs[0], *total_sums.values())
    folded = fold_sums(late, theirs[0], "dp", groups[0])
    theirs[1] = after(theirs[1], total_far, *folded)
    folded += fold_sums(late, theirs[1], "dp", groups[1])
    branch_far, *held = lax.optimization_barrier((branch_far, *early_pieces, folded[0]))
    early_pieces = held[: len(early_pieces)]
    late_part = tree_sum([piece.astype(f32) for piece in send_sums(folded, "dp", far_first)])
    late_part, total_far = lax.optimization_barrier((late_part, total_far))
    normed_grad = (
        total[0].astype(f32) + total_near.astype(f32) + total_far.astype(f32)
    )
    early_part = tree_sum([piece.astype(f32) for piece in early_pieces])
    misc_part = late_part[:, conv_width:]
    shared_part = sum_over(late_part[:, inner:], "tensor")
    bc_part, misc_shared = shared_part[:, : 2 * state_count], shared_part[:, 2 * state_count :]

    residual = hidden.astype(f32)
    gate_scale = lax.rsqrt(
        lax.dynamic_slice_in_dim(stats[0], mine * piece_len, piece_len) / inner_total + epsilon
    )
    branch_local = (
        branch[0].astype(f32) + branch_near.astype(f32) + branch_far.astype(f32)
    )
    block_out = (residual + branch_local * gate_scale[:, None]).astype(bf16)
    row_scale = lax.rsqrt(jnp.mean(residual * residual, axis=1, keepdims=True) + epsilon)
    scaled_grad = normed_grad * rows_all[GAIN_AT : GAIN_AT + 1, conv_width:]
    hidden_grad = row_scale * scaled_grad - residual * row_scale**3 * jnp.mean(
        scaled_grad * residual, axis=1, keepdims=True
    )
    hidden_grad = (hidden_grad + grad_all[0].astype(f32)).astype(bf16)

    taps_at = slice(TAPS_AT, TAPS_AT + CONV)
    head_values = misc_part[0, HEAD_AT : HEAD_AT + 3 * heads]
    return (
        block_out[:, None, :],
        hidden_grad[:, None, :],
        jnp.stack([early_part[:, :inner], late_part[:, :inner]]),
        misc_part[:, :heads],
        bc_part,
        misc_part[:inner_share, taps_at].reshape(conv_inner.shape),
        misc_shared[inner_share : inner_share + shared_share, taps_at].reshape(-1),
        early_part[:, inner:].T,
        head_values[:heads],
        head_values[heads : 2 * heads],
        head_values[2 * heads :],
        misc_shared[:, GAIN_AT],
        misc_part[:, GATE_AT : GATE_AT + gate_lanes].T.reshape(-1),
    )


def solution(mesh):
    in_specs = (
        P("tensor", "dp", None),
        P("tensor", "dp", None),
        P("dp", None),
        P(None, "dp", "tensor"),
        P("dp", "tensor"),
        P("dp", None),
        P("tensor", "dp"),
        P("dp"),
        P("tensor", "dp"),
        P("tensor"),
        P("tensor"),
        P("tensor"),
        P("dp"),
        P("tensor"),
    )
    out_specs = (
        P("tensor", "dp", None),
        P("tensor", "dp", None),
        P(None, "dp", "tensor"),
        P("dp", "tensor"),
        P("dp", None),
        P("tensor", "dp"),
        P("dp"),
        P("tensor", "dp"),
        P("tensor"),
        P("tensor"),
        P("tensor"),
        P("dp"),
        P("tensor"),
    )
    return jax.shard_map(
        per_device, mesh=mesh, in_specs=in_specs, out_specs=out_specs, check_vma=False
    )
```

```python
import functools

import jax
import jax.numpy as jnp
import numpy as np
from jax import lax
from jax.experimental import pallas as pl
from jax.experimental.pallas import tpu as pltpu
from jax.sharding import PartitionSpec as P

CONV = 4
SPAN = 256
LANES = 128
TAPS_AT = 8
GAIN_AT = 12
GATE_AT = 16
HEAD_AT = 64
LOG2E = 1.4426950408889634
epsilon = 1e-05
bf16 = jnp.bfloat16
f32 = jnp.float32
NN = (((1,), (0,)), ((), ()))
NT = (((1,), (1,)), ((), ()))
TN = (((0,), (0,)), ((), ()))


def mm(left, right, dims=NN):
    return lax.dot_general(left, right, dims, preferred_element_type=f32)


def split(values, parts):
    pieces = []
    for _ in range(parts):
        piece = values.astype(bf16)
        pieces.append(piece)
        values = values - piece.astype(f32)
    return pieces


def mm_left_exact(left, right):
    both = mm(left, jnp.concatenate(split(right, 2), axis=1))
    return both[:, : right.shape[1]] + both[:, right.shape[1] :]


def mm_right_exact(left, right):
    return sum(mm(piece, right) for piece in split(left, 2))


def widen(values, expand):
    half = LANES // 2
    first = jnp.where(iota(values.shape, 1) < half, values, 0.0)
    high = first.astype(bf16).astype(f32)
    packed = (high + pltpu.roll(first - high, half, 1)).astype(bf16)
    return mm(packed, expand)


def sigmoid(values):
    return 1.0 / (1.0 + jnp.exp(-values))


def softplus(values):
    return jnp.maximum(values, 0.0) + jnp.log1p(jnp.exp(-jnp.abs(values)))


def doc_start(position, ends):
    start = jnp.zeros_like(position)
    for end in ends:
        start = jnp.where(position >= end, end, start)
    return start


def scalar_start(position, ends):
    start = jnp.int32(0)
    for end in ends:
        start = jnp.where(position >= end, end, start)
    return start


def iota(shape, dim):
    return lax.broadcasted_iota(jnp.int32, shape, dim)


def tap_row(rows_ref, back, cols):
    at = TAPS_AT + CONV - 1 - back
    return rows_ref[at : at + 1, cols]


def conv_block(ext_ref, rows_ref, position, start, width):
    masks = [None] + [(position - k >= start).astype(f32) for k in range(1, CONV)]
    groups = []
    for at in range(0, width, LANES):
        cols = slice(at, at + LANES)
        total = ext_ref[8 : 8 + SPAN, cols] * tap_row(rows_ref, 0, cols)
        for k in range(1, CONV):
            total = total + ext_ref[8 - k : 8 - k + SPAN, cols] * masks[k] * (
                tap_row(rows_ref, k, cols)
            )
        groups.append(total)
    return jnp.concatenate(groups, axis=1)


def wide(mask, width):
    return jnp.concatenate([mask] * (width // LANES), axis=1)


def pick_piece(block, per_piece, mine, refs, chosen_ref):
    relative = (block // per_piece) ^ mine
    for k, ref in enumerate(refs):

        @pl.when(relative == k)
        def _(ref=ref):
            chosen_ref[...] = ref[...]


def place_rows(ref, slot, values):
    rows = values.shape[0]
    ref[pl.ds(pl.multiple_of(slot * rows, 16), rows), :] = values


def forward_kernel(
    inner,
    state_count,
    heads,
    per_piece,
    pieces,
    parts,
    info_ref,
    *refs,
):
    hidden_refs, refs = refs[:pieces], refs[pieces:]
    part_refs, refs = refs[:parts], refs[parts:]
    if parts:
        refs, weight_ref, scratch = refs[:-4], refs[-4], refs[-3:]
        refs = refs + scratch
    else:
        weight_ref, refs = refs[0], refs[1:]
    (
        choose_ref,
        chan_ref,
        head_ref,
        expand_ref,
        normed_ref,
        pre_ref,
        step_ref,
        y_ref,
        cum_ref,
        entering_ref,
        conv_ref,
        rows_ref,
        ext_ref,
        state_ref,
        hidden_ref,
    ) = refs
    block = pl.program_id(0)
    conv_width = inner + 2 * state_count
    ends = [info_ref[k] for k in range(3)]
    base = block * SPAN

    @pl.when(block == 0)
    def _():
        ext_ref[...] = jnp.zeros_like(ext_ref)
        state_ref[...] = jnp.zeros_like(state_ref)
        if parts:
            put = lambda k, value: place_rows(weight_ref, info_ref[4] ^ k, value)
            own_ref, near_ref, far_ref, beside_ref = part_refs
            put(0, own_ref[...])
            put(1, near_ref[...])
            for at in range(far_ref.shape[0]):
                k = 2 * (far_ref.shape[0] - at)
                put(k, far_ref[at])
                put(k + 1, beside_ref[at])
        rows_ref[...] = mm(weight_ref[:, conv_width:], choose_ref[...], TN)[0:16, :]

    pick_piece(block, per_piece, info_ref[3], hidden_refs, hidden_ref)
    residual = hidden_ref[...].astype(f32)
    row_scale = lax.rsqrt(jnp.mean(residual * residual, axis=1, keepdims=True) + epsilon)
    normed = (residual * row_scale * rows_ref[GAIN_AT : GAIN_AT + 1, conv_width:]).astype(bf16)
    normed_ref[...] = normed
    pre = mm(normed, weight_ref[...])
    pre_ref[...] = pre[:, :conv_width].astype(bf16)
    step_ref[...] = pre[:, conv_width:]

    ext_ref[0:8, :] = ext_ref[SPAN : SPAN + 8, :]
    ext_ref[8 : 8 + SPAN, :] = pre[:, :conv_width]
    position = base + iota((SPAN, LANES), 0)
    start = doc_start(position, ends)
    conv = conv_block(ext_ref, rows_ref, position, start, conv_width)
    conv_ref[...] = conv
    active = conv * sigmoid(conv)
    x_val = active[:, :inner].astype(bf16).astype(f32)
    in_map = active[:, inner : inner + state_count].astype(bf16)
    out_map = active[:, inner + state_count :].astype(bf16)

    step_size = softplus(pre[:, conv_width:] + head_ref[1:2, :])
    log_decay = step_size * head_ref[0:1, :]
    row_at = iota((SPAN, SPAN), 0)
    col_at = iota((SPAN, SPAN), 1)
    lower = (col_at <= row_at).astype(f32).astype(bf16)
    cum = mm_left_exact(lower, log_decay * LOG2E)
    cum_ref[...] = cum
    cum_rows = cum.T

    start_last = scalar_start(base + SPAN - 1, ends)
    keep = (start < base).astype(f32)
    tail = (position >= start_last).astype(f32)
    survives = (start_last < base).astype(f32)
    expand = expand_ref[...]
    step_wide = widen(step_size, expand)
    decay_wide = widen(jnp.exp2(cum), expand)
    into_wide = widen(jnp.exp2(cum[SPAN - 1 :, :] - cum) * tail, expand)

    x_step = x_val * step_wide
    x_step_low = x_step.astype(bf16)
    state = state_ref[...]
    entering_ref[...] = state
    outside = mm(out_map, state.astype(bf16)) * (decay_wide * wide(keep, inner))
    visible = (col_at <= row_at) & (base + col_at >= wide(start, SPAN))
    scores = jnp.where(visible, mm(out_map, in_map, NT), 0.0)
    upper_half = iota((SPAN, LANES), 1) >= LANES // 2
    half = SPAN // 2
    inside = []
    for pair in range(heads // 2):
        x_pair = x_step_low[:, pair * LANES : (pair + 1) * LANES]
        tops, bottoms = [], []
        for which in range(2):
            head = 2 * pair + which
            column, row = cum[:, head : head + 1], cum_rows[head : head + 1, :]
            chosen = upper_half if which else jnp.logical_not(upper_half)
            x_head = jnp.where(chosen, x_pair, jnp.zeros_like(x_pair))
            decays = jnp.exp2(jnp.minimum(column[:half] - row[:, :half], 0.0))
            mixing = (scores[:half, :half] * decays).astype(bf16)
            tops.append(mm(mixing, x_head[:half]))
            far = jnp.exp2(column[half:] - row[:, :half])
            near = jnp.exp2(jnp.minimum(column[half:] - row[:, half:], 0.0))
            mixing = (scores[half:] * jnp.concatenate([far, near], axis=1)).astype(bf16)
            bottoms.append(mm(mixing, x_head))
        inside.append(jnp.concatenate([tops[0] + tops[1], bottoms[0] + bottoms[1]], axis=0))
    y_val = jnp.concatenate(inside, axis=1) + outside + chan_ref[0:1, :] * x_val
    y_ref[...] = y_val

    scaled = (x_step * into_wide).astype(bf16)
    state_ref[...] = (decay_wide[SPAN - 1 :, :] * survives) * state + mm(in_map, scaled, TN)


def branch_kernel(per_piece, pieces, info_ref, *refs):
    grad_refs, refs = refs[:pieces], refs[pieces:]
    normed_ref, y_ref, gate_w_ref, out_ref, chan_ref = refs[:5]
    gate_ref, branch_ref, stats_ref, grad_ref = refs[5:]
    block = pl.program_id(0)
    pick_piece(block, per_piece, info_ref[3], grad_refs, grad_ref)
    gate = mm(normed_ref[...], gate_w_ref[...])
    gate_ref[...] = gate
    mixed = y_ref[...] * (gate * sigmoid(gate))
    out_w = out_ref[...]
    gain = chan_ref[1:2, :]
    branch_ref[...] = mm((mixed * gain).astype(bf16), out_w, NT).astype(bf16)
    weighted = mm(grad_ref[...], out_w) * gain
    squares = jnp.sum(mixed * mixed, axis=1, keepdims=True)
    crossed = jnp.sum(weighted * mixed, axis=1, keepdims=True)
    lane = iota((mixed.shape[0], LANES), 1)
    both = jnp.where(lane == 0, squares, jnp.where(lane == 1, crossed, 0.0))
    stats_ref[...] = both.T[0:8, :]


def product_sums(left, right):
    products = left * right.astype(f32)
    return sum(products[:, at : at + LANES] for at in range(0, left.shape[1], LANES))


def gate_kernel(inner, inner_total, per_piece, pieces, info_ref, *refs):
    grad_refs, refs = refs[:pieces], refs[pieces:]
    (
        stats_ref,
        normed_ref,
        gate_w_ref,
        out_ref,
        gate_ref,
        y_ref,
        chan_ref,
        gate_grad_ref,
        y_grad_ref,
        early_ref,
        gain_grad_ref,
        product_ref,
        gate_acc,
        out_acc,
        grad_ref,
    ) = refs
    block = pl.program_id(0)

    @pl.when(block == 0)
    def _():
        gate_acc[...] = jnp.zeros_like(gate_acc)
        out_acc[...] = jnp.zeros_like(out_acc)
        gain_grad_ref[...] = jnp.zeros_like(gain_grad_ref)

    pick_piece(block, per_piece, info_ref[3], grad_refs, grad_ref)
    stats = stats_ref[...].T
    gate_scale = lax.rsqrt(stats[:, 0:1] / inner_total + epsilon)
    crossed = stats[:, 1:2] / inner_total
    gate = gate_ref[...]
    gate_sig = sigmoid(gate)
    gate_act = gate * gate_sig
    y_val = y_ref[...]
    mixed = y_val * gate_act
    grad = grad_ref[...]
    gain = chan_ref[1:2, :]
    gated_grad = mm(grad, out_ref[...])
    scaled_mixed = mixed * gate_scale
    out_acc[...] += mm(grad, (scaled_mixed * gain).astype(bf16), TN)
    gain_grad_ref[0:1, :] += jnp.sum(gated_grad * scaled_mixed, axis=0, keepdims=True)
    mixed_grad = gate_scale * (gated_grad * gain) - scaled_mixed * (
        gate_scale * gate_scale * crossed
    )
    gate_grad = mixed_grad * y_val * (gate_sig * (1.0 + gate * (1.0 - gate_sig)))
    gate_grad = gate_grad.astype(bf16)
    gate_grad_ref[...] = gate_grad
    y_grad_ref[...] = (mixed_grad * gate_act).astype(bf16)
    gate_acc[...] += mm(normed_ref[...], gate_grad, TN)

    @pl.when(block == pl.num_programs(0) - 1)
    def _():
        early_ref[:, :inner] = gate_acc[...].astype(bf16)
        early_ref[:, inner:] = out_acc[...].astype(bf16)
        product_ref[...] = product_sums(gate_acc[...], gate_w_ref[...])


def backward_kernel(inner, state_count, heads, blocks, info_ref, *refs):
    (
        normed_ref,
        weight_ref,
        gate_w_ref,
        pre_ref,
        halo_ref,
        step_ref,
        conv_ref,
        y_ref,
        y_grad_ref,
        gate_grad_ref,
        cum_ref,
        entering_ref,
        rows_ref,
        chan_ref,
        head_ref,
        expand_ref,
        gather_ref,
    ) = refs[:17]
    refs = refs[17:]
    product_ref, choose_ref, extra_ref, total_ref, late_ref = refs[:5]
    ext_ref, next_ref, pre_grad_ref, state_grad_ref, late_acc, small_ref, heads_ref = refs[5:]
    step = pl.program_id(0)
    block = blocks - 1 - step
    base = block * SPAN
    conv_width = inner + 2 * state_count
    ends = [info_ref[k] for k in range(3)]

    @pl.when(step == 0)
    def _():
        next_ref[...] = jnp.zeros_like(next_ref)
        state_grad_ref[...] = jnp.zeros_like(state_grad_ref)
        late_acc[...] = jnp.zeros_like(late_acc)
        small_ref[...] = jnp.zeros_like(small_ref)
        heads_ref[...] = jnp.zeros_like(heads_ref)

    skip = chan_ref[0:1, :]
    y_val = y_ref[...]
    y_grad_low = y_grad_ref[...]
    y_grad = y_grad_low.astype(f32)

    ext_ref[0:8, :] = halo_ref[...].astype(f32)[8:16, :]
    ext_ref[8 : 8 + SPAN, :] = pre_ref[...].astype(f32)
    position = base + iota((SPAN, LANES), 0)
    start = doc_start(position, ends)
    conv = conv_ref[...]
    conv_sig = sigmoid(conv)
    active = conv * conv_sig
    act_slope = conv_sig * (1.0 + conv * (1.0 - conv_sig))
    x_val = active[:, :inner].astype(bf16).astype(f32)
    in_map = active[:, inner : inner + state_count].astype(bf16)
    out_map = active[:, inner + state_count :].astype(bf16)

    step_pre = step_ref[...] + head_ref[1:2, :]
    step_size = softplus(step_pre)
    rates = head_ref[0:1, :]
    cum = cum_ref[...]
    cum_rows = cum.T
    start_last = scalar_start(base + SPAN - 1, ends)
    keep = (start < base).astype(f32)
    tail = (position >= start_last).astype(f32)
    survives = (start_last < base).astype(f32)
    expand = expand_ref[...]
    step_wide = widen(step_size, expand)
    decay_wide = widen(jnp.exp2(cum), expand)
    into_wide = widen(jnp.exp2(cum[SPAN - 1 :, :] - cum) * tail, expand)
    keep_decay = decay_wide * wide(keep, inner)
    last_decay = decay_wide[SPAN - 1 :, :] * survives

    x_step = x_val * step_wide
    x_step_low = x_step.astype(bf16)
    scaled = (x_step * into_wide).astype(bf16)
    entering = entering_ref[...]
    entering_low = entering.astype(bf16)
    state_grad = state_grad_ref[...]
    state_grad_low = state_grad.astype(bf16)

    outside = mm(out_map, entering_low)
    outside_grad = (y_grad * keep_decay).astype(bf16)
    scaled_grad = mm(in_map, state_grad_low)
    out_map_grad = mm(outside_grad, entering_low, NT)
    in_map_grad = mm(scaled, state_grad_low, NT)
    state_grad_ref[...] = last_decay * state_grad + mm(out_map, outside_grad, TN)

    row_at = iota((SPAN, SPAN), 0)
    col_at = iota((SPAN, SPAN), 1)
    col_start = doc_start(base + col_at, ends)
    visible = (row_at <= col_at) & (base + row_at >= col_start)
    scores = jnp.where(visible, mm(in_map, out_map, NT), 0.0)
    upper_half = iota((SPAN, LANES), 1) >= LANES // 2
    half = SPAN // 2
    top_grad = jnp.zeros((half, SPAN), f32)
    bottom_grad = jnp.zeros((half, half), f32)
    x_step_grads = []
    for pair in range(heads // 2):
        x_pair = x_step_low[:, pair * LANES : (pair + 1) * LANES]
        grad_pair = y_grad_low[:, pair * LANES : (pair + 1) * LANES]
        tops, bottoms = [], []
        for which in range(2):
            head = 2 * pair + which
            column, row = cum[:, head : head + 1], cum_rows[head : head + 1, :]
            chosen = upper_half if which else jnp.logical_not(upper_half)
            grad_head = jnp.where(chosen, grad_pair, jnp.zeros_like(grad_pair))
            near = jnp.exp2(jnp.minimum(row[:, :half] - column[:half], 0.0))
            far = jnp.exp2(row[:, half:] - column[:half])
            decays = jnp.concatenate([near, far], axis=1)
            top_grad = top_grad + mm(x_pair[:half], grad_head, NT) * decays
            tops.append(mm((scores[:half] * decays).astype(bf16), grad_head))
            decays = jnp.exp2(jnp.minimum(row[:, half:] - column[half:], 0.0))
            bottom_grad = bottom_grad + mm(x_pair[half:], grad_head[half:], NT) * decays
            tail_mix = (scores[half:, half:] * decays).astype(bf16)
            bottoms.append(mm(tail_mix, grad_head[half:]))
        x_step_grads.append(
            jnp.concatenate([tops[0] + tops[1], bottoms[0] + bottoms[1]], axis=0)
        )
    x_step_grad = jnp.concatenate(x_step_grads, axis=1)
    bottom_grad = jnp.concatenate([jnp.zeros((half, half), f32), bottom_grad], axis=1)
    score_grad = jnp.concatenate([top_grad, bottom_grad], axis=0)
    score_grad = jnp.where(visible, score_grad, 0.0).astype(bf16)
    in_map_grad = in_map_grad + mm(score_grad, out_map)
    out_map_grad = out_map_grad + mm(score_grad, in_map, TN)

    inside = y_val - skip * x_val - keep_decay * outside
    into_terms = scaled.astype(f32) * scaled_grad
    cum_terms = (
        y_grad * inside
        + outside_grad.astype(f32) * outside
        - x_step_low.astype(f32) * x_step_grad
        - into_terms
    )
    last_terms = jnp.sum(into_terms, axis=0, keepdims=True) + last_decay * jnp.sum(
        state_grad * entering, axis=0, keepdims=True
    )
    last_row = iota((SPAN, inner), 0) == SPAN - 1
    cum_terms = cum_terms + jnp.where(last_row, last_terms, 0.0)
    x_step_grad = x_step_grad + into_wide * scaled_grad
    gather = gather_ref[...]
    cum_grad = mm_right_exact(cum_terms, gather)
    step_grad = mm_right_exact(x_val * x_step_grad, gather)
    upper = (row_at <= col_at).astype(f32).astype(bf16)
    log_grad = mm_left_exact(upper, cum_grad)
    step_grad = (step_grad + log_grad * rates) * sigmoid(step_pre)
    pre_grad_ref[:, conv_width:] = step_grad.astype(bf16)
    x_grad = skip * y_grad + step_wide * x_step_grad

    heads_ref[0:1, :] += jnp.sum(y_grad * x_val, axis=0, keepdims=True)
    heads_ref[1:2, :LANES] += jnp.sum(step_size * rates * log_grad, axis=0, keepdims=True)
    heads_ref[2:3, :LANES] += jnp.sum(step_grad, axis=0, keepdims=True)

    conv_grad = jnp.concatenate([x_grad, in_map_grad, out_map_grad], axis=1) * act_slope
    next_ref[SPAN : SPAN + 8, :] = next_ref[0:8, :]
    next_ref[0:SPAN, :] = conv_grad
    back = [None] + [(position - k >= start).astype(f32) for k in range(1, CONV)]
    ahead = [None] + [
        (position >= doc_start(position + k, ends)).astype(f32) for k in range(1, CONV)
    ]
    for col in range(0, conv_width, LANES):
        cols = slice(col, col + LANES)
        grad_here = next_ref[0:SPAN, cols]
        total = grad_here * tap_row(rows_ref, 0, cols)
        small_ref[TAPS_AT + CONV - 1 : TAPS_AT + CONV, cols] += jnp.sum(
            grad_here * ext_ref[8 : 8 + SPAN, cols], axis=0, keepdims=True
        )
        for k in range(1, CONV):
            total = total + next_ref[k : k + SPAN, cols] * ahead[k] * (
                tap_row(rows_ref, k, cols)
            )
            small_ref[TAPS_AT + CONV - 1 - k : TAPS_AT + CONV - k, cols] += jnp.sum(
                grad_here * back[k] * ext_ref[8 - k : 8 - k + SPAN, cols], axis=0, keepdims=True
            )
        pre_grad_ref[:, cols] = total.astype(bf16)

    pre_grads = pre_grad_ref[...]
    total = mm(pre_grads, weight_ref[...], NT) + mm(gate_grad_ref[...], gate_w_ref[...], NT)
    total_ref[...] = total.astype(bf16)
    late_acc[...] += mm(normed_ref[...], pre_grads, TN)

    @pl.when(step == pl.num_programs(0) - 1)
    def _():
        late = late_acc[...]
        sums = product_sums(late, weight_ref[...]) + product_ref[...]
        gain = weight_ref[:, conv_width + GAIN_AT : conv_width + GAIN_AT + 1].astype(f32)
        sums = jnp.sum(sums, axis=1, keepdims=True) / gain
        chosen = small_ref[...].astype(bf16)
        filler = jnp.zeros((LANES - chosen.shape[0], chosen.shape[1]), bf16)
        misc = mm(choose_ref[...], jnp.concatenate([chosen, filler], axis=0), NT)
        misc = misc + jnp.where(iota(misc.shape, 1) == GAIN_AT, sums, 0.0)
        totals = heads_ref[...]
        skips = mm_right_exact(totals, gather_ref[...])
        per_head = [totals[1:2, :LANES], totals[2:3, :LANES], skips[0:1, :]]
        for at_head, value in enumerate(per_head):
            value = jnp.broadcast_to(value, (8, LANES))
            misc = misc + pltpu.roll(value, HEAD_AT + at_head * heads, 1)[0:1, :]
        late_ref[:, :conv_width] = late[:, :conv_width].astype(bf16)
        late_ref[:, conv_width:] = (late[:, conv_width:] + misc + extra_ref[...]).astype(bf16)


def weights_kernel(early_count, inner, *refs):
    early_refs, late_refs = refs[:early_count], refs[early_count:-3]
    zx_ref, out_ref, rest_ref = refs[-3:]
    early = tree_sum([ref[...].astype(f32) for ref in early_refs])
    late = tree_sum([ref[...].astype(f32) for ref in late_refs])
    zx_ref[0] = early[:, :inner]
    zx_ref[1] = late[:, :inner]
    out_ref[...] = early[:, inner:]
    rest_ref[...] = late[:, inner:]


def hidden_kernel(
    gain_at, hidden_ref, grad_ref, own_ref, near_ref, far_ref, rest_ref, rows_ref, out_ref
):
    gain = rows_ref[GAIN_AT : GAIN_AT + 1, gain_at:]
    half = far_ref.shape[0]
    for at, part_ref in ((0, far_ref), (half, rest_ref)):
        rows = slice(at, at + half)
        total = own_ref[rows, :].astype(f32) + near_ref[rows, :].astype(f32)
        scaled = (total + part_ref[...].astype(f32)) * gain
        residual = hidden_ref[rows, :].astype(f32)
        row_scale = lax.rsqrt(jnp.mean(residual * residual, axis=1, keepdims=True) + epsilon)
        crossed = jnp.mean(scaled * residual, axis=1, keepdims=True)
        result = row_scale * scaled - residual * (row_scale * row_scale * row_scale * crossed)
        out_ref[rows, :] = (result + grad_ref[rows, :].astype(f32)).astype(bf16)


def swap(values, axis, bits):
    size = lax.axis_size(axis)
    return lax.ppermute(values, axis, [(i, i ^ bits) for i in range(size)])


def bits_of(size):
    return [1 << k for k in range(size.bit_length() - 1)]


def after(values, *others):
    return lax.optimization_barrier((values,) + others)[0]


def sum_over(values, axis):
    size = lax.axis_size(axis)
    if size > 8:
        for bit in bits_of(size):
            values = values + swap(values, axis, bit)
        return values
    return tree_sum([values] + [swap(values, axis, k) for k in range(1, size)])


def tree_sum(pieces):
    while len(pieces) > 1:
        pieces = [pieces[k] + pieces[k + 1] for k in range(0, len(pieces), 2)]
    return pieces[0]


def gather_far(values, axis):
    pieces = {0: values}
    bits = bits_of(lax.axis_size(axis))
    for bit in reversed(bits[1:]):
        pieces.update({k | bit: swap(piece, axis, bit) for k, piece in list(pieces.items())})
    pieces[1] = swap(values, axis, 1)
    return pieces


def gather_near(pieces, axis, *others):
    pieces = dict(pieces)
    for k in list(pieces):
        if k > 1:
            pieces[k | 1] = swap(after(pieces[k], *others) if others else pieces[k], axis, 1)
    return [pieces[k] for k in range(len(pieces))]


def gather_direct(values, axis, others):
    size = lax.axis_size(axis)
    near = swap(values, axis, 1)
    far = [swap(values, axis, k) for k in range(size - 2, 0, -2)]
    far = after(jnp.stack(far), *others)
    return values, near, far, swap(far, axis, 1)


def assemble(own, near, far, beside, axis):
    size = lax.axis_size(axis)
    place = lax.axis_index(axis)
    result = jnp.zeros((size,) + own.shape, own.dtype)
    pieces = {0: own, 1: near}
    for at, k in enumerate(range(size - 2, 0, -2)):
        pieces.update({k: far[at], k + 1: beside[at]})
    for k in range(size):
        result = lax.dynamic_update_slice(
            result, pieces[k][None], (place ^ k,) + (0,) * own.ndim
        )
    return result.reshape((-1,) + own.shape[1:])


def gather_pairs(values, other, axis):
    size = lax.axis_size(axis)
    place = lax.axis_index(axis)
    first = place % 2 == 0
    pair = jnp.stack([jnp.where(first, values, other), jnp.where(first, other, values)])
    result = jnp.zeros((size // 2,) + pair.shape, values.dtype)
    for k in range(0, size, 2):
        piece = swap(pair, axis, k) if k else pair
        result = lax.dynamic_update_slice(
            result, piece[None], ((place ^ k) // 2,) + (0,) * pair.ndim
        )
    return result.reshape((-1,) + values.shape[1:])


def block_of(values, place, share):
    return lax.dynamic_slice_in_dim(values, place * share, share, 0)


def fold_pairs(values, axis, steps):
    size = lax.axis_size(axis)
    place = lax.axis_index(axis)
    share = values.shape[0] // size
    theirs = jnp.stack([block_of(values, place ^ k ^ 1, share) for k in steps])
    return swap(theirs, axis, 1)


def fold_sums(values, theirs, axis, steps):
    place = lax.axis_index(axis)
    share = values.shape[0] // lax.axis_size(axis)
    sums = [
        block_of(values, place ^ k, share).astype(f32) + theirs[at].astype(f32)
        for at, k in enumerate(steps)
    ]
    return [both.astype(bf16) if k else both for k, both in zip(steps, sums)]


def send_sums(folded, axis, steps):
    return [
        swap(both, axis, k) if k else both for k, both in zip(steps, folded)
    ]


def per_device(
    hidden_rows,
    out_grad,
    doc_lengths,
    zx_weight,
    step_weight,
    bc_weight,
    conv_inner,
    conv_shared,
    out_weight,
    decay_log,
    step_bias,
    skip_gain,
    norm_gain,
    gate_gain,
):
    piece_len, _, width = hidden_rows.shape
    tensor = lax.axis_size("tensor")
    data = lax.axis_size("dp")
    full_len = piece_len * tensor
    blocks = full_len // SPAN
    per_piece = piece_len // SPAN
    share = zx_weight.shape[1]
    inner = zx_weight.shape[2]
    heads = step_weight.shape[1]
    head_dim = inner // heads
    state_count = bc_weight.shape[1] // 2
    conv_width = inner + 2 * state_count
    span = conv_width + LANES
    inner_total = float(inner * tensor)
    mine = lax.axis_index("tensor")
    place = lax.axis_index("dp")

    hidden = hidden_rows[:, 0, :]
    hidden_all = gather_far(hidden, "tensor")
    hidden_far = hidden_all[tensor // 2]
    hidden_all = gather_near(hidden_all, "tensor")

    inner_share = conv_inner.size // CONV
    shared_share = conv_shared.size // CONV
    taps = jnp.concatenate([conv_inner.reshape(-1, CONV), conv_shared.reshape(-1, CONV)])
    taps = jnp.pad(taps, ((0, share - inner_share - shared_share), (0, 0)))
    misc = jnp.concatenate(
        [
            jnp.pad(step_weight, ((0, 0), (0, TAPS_AT - heads))),
            taps,
            norm_gain[:, None],
            jnp.zeros((share, LANES - GAIN_AT - 1), bf16),
        ],
        axis=1,
    )
    channel = np.arange(inner)
    per_dev = head_dim // data
    sources = [
        (channel % head_dim) // per_dev * share
        + channel // head_dim * per_dev
        + channel % per_dev,
        np.arange(2 * state_count) // shared_share * share
        + inner_share
        + np.arange(2 * state_count) % shared_share,
        np.arange(width),
    ]
    sources = jnp.asarray(np.concatenate(sources), jnp.int32)
    choose = (jnp.arange(width, dtype=jnp.int32)[:, None] == sources[None, :]).astype(bf16)
    chan = jnp.pad(jnp.stack([jnp.repeat(skip_gain, head_dim), gate_gain]), ((0, 6), (0, 0)))
    head_rows = jnp.pad(
        jnp.stack([-jnp.exp(decay_log), step_bias]), ((0, 6), (0, LANES - heads))
    )
    channel_head = jnp.arange(inner)[None, :] // head_dim
    expand = (jnp.arange(LANES)[:, None] % (LANES // 2) == channel_head).astype(bf16)
    gather = (jnp.arange(LANES)[:, None] == channel_head).astype(bf16).T
    lengths = doc_lengths[0].astype(jnp.int32)
    info = jnp.stack(
        [lengths[0], lengths[0] + lengths[1], lengths[0] + lengths[1] + lengths[2], mine, place]
    ).astype(jnp.int32)

    late_shard = jnp.concatenate([zx_weight[0], out_weight.T], axis=1)
    late_other = swap(late_shard, "dp", 1)
    shard = jnp.concatenate([zx_weight[1], bc_weight, misc], axis=1)
    weight_parts = gather_direct(
        shard, "dp", (hidden_far, late_other, choose, chan, head_rows, expand, info)
    )
    in_kernel = share % 16 == 0
    if not in_kernel:
        weight_parts = (assemble(*weight_parts, "dp"),)
    weights_late = gather_pairs(late_shard, late_other, "dp")
    grad_all = gather_far(after(out_grad, hidden_far)[:, 0, :], "tensor")

    def limits(mebi):
        return pltpu.CompilerParams(
            dimension_semantics=("arbitrary",), vmem_limit_bytes=mebi * 1024 * 1024
        )

    shaped = jax.ShapeDtypeStruct

    def fixed(shape, at=0):
        return pl.BlockSpec(shape, lambda i, info: (0,) * (len(shape) - 1) + (at,))

    def rows(cols, at=0, order=lambda i: i):
        return pl.BlockSpec((SPAN, cols), lambda i, info: (order(i), at))

    def piece_specs(order=lambda i: i):
        return [
            pl.BlockSpec(
                (SPAN, width),
                lambda i, info, k=k: (
                    jnp.clip(order(i) - (info[3] ^ k) * per_piece, 0, per_piece - 1),
                    0,
                ),
            )
            for k in range(tensor)
        ]

    def call(
        kernel, name, micros, steps, in_specs, out_specs, out_shape, scratch, args, aliases={}
    ):
        return pl.pallas_call(
            kernel,
            grid_spec=pltpu.PrefetchScalarGridSpec(
                num_scalar_prefetch=1,
                grid=(steps,),
                in_specs=in_specs,
                out_specs=out_specs,
                scratch_shapes=scratch,
            ),
            out_shape=out_shape,
            compiler_params=limits(56 if name == "backward" else 36),
            input_output_aliases=aliases,
            cost_estimate=pl.CostEstimate(
                flops=int(micros * 1.0e9), bytes_accessed=int(micros * 3.0e6), transcendentals=0
            ),
            name=name,
        )(info, *args)

    def relative(order):
        return pl.BlockSpec(
            (SPAN, width),
            lambda i, info: (
                ((order(i) // per_piece) ^ info[3]) * per_piece + order(i) % per_piece,
                0,
            ),
        )

    natural = lambda i: i
    state_spec = lambda order: pl.BlockSpec(
        (state_count, inner), lambda i, info: (order(i), 0)
    )
    normed, pre, step_pre, y_val, cum, entering, conv, rows_all, *weights = call(
        functools.partial(
            forward_kernel,
            inner,
            state_count,
            heads,
            per_piece,
            tensor,
            len(weight_parts) if in_kernel else 0,
        ),
        "forward",
        22,
        blocks,
        piece_specs()
        + [fixed(part.shape) for part in weight_parts]
        + [
            fixed(choose.shape),
            fixed(chan.shape),
            fixed(head_rows.shape),
            fixed(expand.shape),
        ],
        [
            rows(width),
            rows(conv_width),
            rows(LANES),
            rows(inner),
            rows(LANES),
            state_spec(natural),
            rows(conv_width),
            fixed((16, conv_width + width)),
        ]
        + [fixed((width, span))] * in_kernel,
        [
            shaped((full_len, width), bf16),
            pltpu.HBM((full_len, conv_width), bf16),
            pltpu.HBM((full_len, LANES), f32),
            shaped((full_len, inner), f32),
            pltpu.HBM((full_len, LANES), f32),
            pltpu.HBM((blocks * state_count, inner), f32),
            pltpu.HBM((full_len, conv_width), f32),
            shaped((16, conv_width + width), f32),
        ]
        + [shaped((width, span), bf16)] * in_kernel,
        [
            pltpu.VMEM((SPAN + 8, conv_width), f32),
            pltpu.VMEM((state_count, inner), f32),
            pltpu.VMEM((SPAN, width), bf16),
        ],
        (*hidden_all, *weight_parts, choose, chan, head_rows, expand),
    )
    (weights,) = weights or weight_parts

    tall = lambda cols: pl.BlockSpec((piece_len, cols), lambda i, info: (i, 0))
    whole_pieces = [fixed((piece_len, width))] * tensor
    grad_all = gather_near(grad_all, "tensor", rows_all)
    gate_spec, out_spec = fixed((width, inner)), fixed((width, inner), 1)
    gate, branch, stats = call(
        functools.partial(branch_kernel, 1, tensor),
        "branch",
        11,
        tensor,
        whole_pieces + [tall(width), tall(inner), gate_spec, out_spec, fixed(chan.shape)],
        [tall(inner), pl.BlockSpec((piece_len, width), lambda i, info: (i ^ info[3], 0)), pl.BlockSpec((8, piece_len), lambda i, info: (0, i))],
        [
            shaped((full_len, inner), f32),
            shaped((full_len, width), bf16),
            shaped((8, full_len), f32),
        ],
        [pltpu.VMEM((piece_len, width), bf16)],
        (*grad_all, normed, y_val, weights_late, weights_late, chan),
    )

    cut = lambda values, k: values[k * piece_len : (k + 1) * piece_len]
    branch_sum = cut(branch, 2).astype(f32) + swap(cut(branch, 3), "tensor", 1).astype(f32)
    branch_sum = branch_sum.astype(bf16)
    branch_near = swap(cut(branch, 1), "tensor", 1)
    stats = sum_over(stats, "tensor")

    gate_grad, y_grad, early, gain_grad, product = call(
        functools.partial(gate_kernel, inner, inner_total, 1, tensor),
        "gate_back",
        13,
        tensor,
        whole_pieces
        + [
            pl.BlockSpec((8, piece_len), lambda i, info: (0, i)),
            tall(width),
            gate_spec,
            out_spec,
            tall(inner),
            tall(inner),
            fixed(chan.shape),
        ],
        [
            tall(inner),
            tall(inner),
            fixed((width, 2 * inner)),
            fixed((8, inner)),
            fixed((width, LANES)),
        ],
        [
            shaped((full_len, inner), bf16),
            shaped((full_len, inner), bf16),
            shaped((width, 2 * inner), bf16),
            shaped((8, inner), f32),
            shaped((width, LANES), f32),
        ],
        [
            pltpu.VMEM((width, inner), f32),
            pltpu.VMEM((width, inner), f32),
            pltpu.VMEM((piece_len, width), bf16),
        ],
        (*grad_all, stats, normed, weights_late, weights_late, gate, y_val, chan),
    )
    far_first = list(range(data - 2, -1, -2))
    early_theirs = fold_pairs(early, "dp", far_first)
    gate_grad, branch_sum = lax.optimization_barrier((gate_grad, branch_sum))
    branch_far = swap(branch_sum, "tensor", 2)

    small_width = conv_width + width
    back = lambda i: blocks - 1 - i
    back_rows = lambda cols: rows(cols, 0, back)
    gate_lanes = inner // share
    extra = jnp.tile(gain_grad[0].reshape(gate_lanes, share).T, (data, 1))
    extra = jnp.pad(extra, ((0, 0), (GATE_AT, LANES - GATE_AT - gate_lanes)))
    total, late = call(
        functools.partial(backward_kernel, inner, state_count, heads, blocks),
        "backward",
        36,
        blocks,
        [
            back_rows(width),
            fixed((width, span)),
            gate_spec,
            back_rows(conv_width),
            pl.BlockSpec(
                (16, conv_width),
                lambda i, info: (jnp.maximum(back(i) * (SPAN // 16) - 1, 0), 0),
            ),
            back_rows(LANES),
            back_rows(conv_width),
            back_rows(inner),
            back_rows(inner),
            back_rows(inner),
            back_rows(LANES),
            state_spec(back),
            fixed((16, small_width)),
            fixed(chan.shape),
            fixed(head_rows.shape),
            fixed(expand.shape),
            fixed(gather.shape),
            fixed((width, LANES)),
            fixed((width, conv_width)),
            fixed((width, LANES)),
        ],
        [relative(back), fixed((width, span))],
        [shaped((full_len, width), bf16), shaped((width, span), bf16)],
        [
            pltpu.VMEM((SPAN + 8, conv_width), f32),
            pltpu.VMEM((SPAN + 8, conv_width), f32),
            pltpu.VMEM((SPAN, span), bf16),
            pltpu.VMEM((state_count, inner), f32),
            pltpu.VMEM((width, span), f32),
            pltpu.VMEM((16, conv_width), f32),
            pltpu.VMEM((8, inner), f32),
        ],
        (
            normed,
            weights,
            weights_late,
            pre,
            pre,
            step_pre,
            conv,
            y_val,
            y_grad,
            gate_grad,
            cum,
            entering,
            rows_all,
            chan,
            head_rows,
            expand,
            gather,
            product,
            choose,
            extra,
        ),
    )

    total, late, branch_near, branch_far, early_theirs = lax.optimization_barrier(
        (total, late, branch_near, branch_far, early_theirs)
    )
    early_pieces = send_sums(
        fold_sums(early, early_theirs, "dp", far_first), "dp", far_first
    )
    total_sum = cut(total, 2).astype(f32) + swap(cut(total, 3), "tensor", 1).astype(f32)
    total_sum = total_sum.astype(bf16)
    groups = far_first[: len(far_first) // 2], far_first[len(far_first) // 2 :]
    theirs = [fold_pairs(late, "dp", steps) for steps in groups]
    total_far = swap(total_sum[: piece_len // 2], "tensor", 2)
    total_rest = swap(total_sum[piece_len // 2 :], "tensor", 2)
    theirs[0], total = lax.optimization_barrier((theirs[0], after(total, total_sum)))
    folded = fold_sums(late, theirs[0], "dp", groups[0])
    theirs[1] = after(theirs[1], total_far, *folded)
    folded += fold_sums(late, theirs[1], "dp", groups[1])
    branch_far, _ = lax.optimization_barrier((branch_far, folded[0]))
    late_pieces = send_sums(folded, "dp", far_first)
    total_own, total_near = cut(total, 0), swap(cut(total, 1), "tensor", 1)

    def whole(kernel, name, out_shape, args):
        return pl.pallas_call(
            kernel, out_shape=out_shape, compiler_params=plain, name=name
        )(*args)

    plain = pltpu.CompilerParams(vmem_limit_bytes=24 * 1024 * 1024)
    zx_part, out_part, rest_part = whole(
        functools.partial(weights_kernel, len(early_pieces), inner),
        "weight_sums",
        [
            shaped((2, share, inner), f32),
            shaped((share, inner), f32),
            shaped((share, span - inner), f32),
        ],
        (*early_pieces, *late_pieces),
    )
    rest_part, total_rest = lax.optimization_barrier((rest_part, total_rest))
    misc_part = rest_part[:, 2 * state_count :]
    shared = [rest_part] + [swap(rest_part, "tensor", k) for k in range(1, tensor)]
    hidden_grad = whole(
        functools.partial(hidden_kernel, conv_width),
        "hidden_back",
        shaped((piece_len, width), bf16),
        (hidden, grad_all[0], total_own, total_near, total_far, total_rest, rows_all),
    )
    hidden_grad, *shared = lax.optimization_barrier((hidden_grad, *shared))
    shared_part = tree_sum(shared)
    bc_part, misc_shared = shared_part[:, : 2 * state_count], shared_part[:, 2 * state_count :]

    residual = hidden.astype(f32)
    gate_scale = lax.rsqrt(
        lax.dynamic_slice_in_dim(stats[0], mine * piece_len, piece_len) / inner_total + epsilon
    )
    branch_local = (
        cut(branch, 0).astype(f32) + branch_near.astype(f32) + branch_far.astype(f32)
    )
    block_out = (residual + branch_local * gate_scale[:, None]).astype(bf16)
    taps_at = slice(TAPS_AT, TAPS_AT + CONV)
    head_values = misc_part[0, HEAD_AT : HEAD_AT + 3 * heads]
    return (
        block_out[:, None, :],
        hidden_grad[:, None, :],
        zx_part,
        misc_part[:, :heads],
        bc_part,
        misc_part[:inner_share, taps_at].reshape(conv_inner.shape),
        misc_shared[inner_share : inner_share + shared_share, taps_at].reshape(-1),
        out_part.T,
        head_values[:heads],
        head_values[heads : 2 * heads],
        head_values[2 * heads :],
        misc_shared[:, GAIN_AT],
        misc_part[:, GATE_AT : GATE_AT + gate_lanes].T.reshape(-1),
    )


def solution(mesh):
    in_specs = (
        P("tensor", "dp", None),
        P("tensor", "dp", None),
        P("dp", None),
        P(None, "dp", "tensor"),
        P("dp", "tensor"),
        P("dp", None),
        P("tensor", "dp"),
        P("dp"),
        P("tensor", "dp"),
        P("tensor"),
        P("tensor"),
        P("tensor"),
        P("dp"),
        P("tensor"),
    )
    out_specs = (
        P("tensor", "dp", None),
        P("tensor", "dp", None),
        P(None, "dp", "tensor"),
        P("dp", "tensor"),
        P("dp", None),
        P("tensor", "dp"),
        P("dp"),
        P("tensor", "dp"),
        P("tensor"),
        P("tensor"),
        P("tensor"),
        P("dp"),
        P("tensor"),
    )
    return jax.shard_map(
        per_device, mesh=mesh, in_specs=in_specs, out_specs=out_specs, check_vma=False
    )
```

```python
import functools

import jax
import jax.numpy as jnp
import numpy as np
from jax import lax
from jax.experimental import pallas as pl
from jax.experimental.pallas import tpu as pltpu
from jax.sharding import PartitionSpec as P

CONV = 4
SPAN = 256
LANES = 128
TAPS_AT = 8
GAIN_AT = 12
GATE_AT = 16
HEAD_AT = 64
LOG2E = 1.4426950408889634
epsilon = 1e-05
bf16 = jnp.bfloat16
f32 = jnp.float32
NN = (((1,), (0,)), ((), ()))
NT = (((1,), (1,)), ((), ()))
TN = (((0,), (0,)), ((), ()))


def mm(left, right, dims=NN):
    return lax.dot_general(left, right, dims, preferred_element_type=f32)


def split(values, parts):
    pieces = []
    for _ in range(parts):
        piece = values.astype(bf16)
        pieces.append(piece)
        values = values - piece.astype(f32)
    return pieces


def mm_left_exact(left, right):
    both = mm(left, jnp.concatenate(split(right, 2), axis=1))
    return both[:, : right.shape[1]] + both[:, right.shape[1] :]


def mm_right_exact(left, right):
    return sum(mm(piece, right) for piece in split(left, 2))


def widen(values, expand):
    half = LANES // 2
    first = jnp.where(iota(values.shape, 1) < half, values, 0.0)
    high = first.astype(bf16).astype(f32)
    packed = (high + pltpu.roll(first - high, half, 1)).astype(bf16)
    return mm(packed, expand)


def sigmoid(values):
    return 1.0 / (1.0 + jnp.exp(-values))


def softplus(values):
    return jnp.maximum(values, 0.0) + jnp.log1p(jnp.exp(-jnp.abs(values)))


def doc_start(position, ends):
    start = jnp.zeros_like(position)
    for end in ends:
        start = jnp.where(position >= end, end, start)
    return start


def scalar_start(position, ends):
    start = jnp.int32(0)
    for end in ends:
        start = jnp.where(position >= end, end, start)
    return start


def iota(shape, dim):
    return lax.broadcasted_iota(jnp.int32, shape, dim)


def tap_row(rows_ref, back, cols):
    at = TAPS_AT + CONV - 1 - back
    return rows_ref[at : at + 1, cols]


def conv_block(ext_ref, rows_ref, position, start, width):
    masks = [None] + [(position - k >= start).astype(f32) for k in range(1, CONV)]
    groups = []
    for at in range(0, width, LANES):
        cols = slice(at, at + LANES)
        total = ext_ref[8 : 8 + SPAN, cols] * tap_row(rows_ref, 0, cols)
        for k in range(1, CONV):
            total = total + ext_ref[8 - k : 8 - k + SPAN, cols] * masks[k] * (
                tap_row(rows_ref, k, cols)
            )
        groups.append(total)
    return jnp.concatenate(groups, axis=1)


def wide(mask, width):
    return jnp.concatenate([mask] * (width // LANES), axis=1)


def pick_piece(block, per_piece, mine, refs, chosen_ref):
    relative = (block // per_piece) ^ mine
    for k, ref in enumerate(refs):

        @pl.when(relative == k)
        def _(ref=ref):
            chosen_ref[...] = ref[...]


def place_rows(ref, slot, values):
    rows = values.shape[0]
    ref[pl.ds(pl.multiple_of(slot * rows, 16), rows), :] = values


def forward_kernel(
    inner,
    state_count,
    heads,
    per_piece,
    pieces,
    parts,
    info_ref,
    *refs,
):
    hidden_refs, refs = refs[:pieces], refs[pieces:]
    part_refs, refs = refs[:parts], refs[parts:]
    if parts:
        refs, weight_ref, scratch = refs[:-4], refs[-4], refs[-3:]
        refs = refs + scratch
    else:
        weight_ref, refs = refs[0], refs[1:]
    (
        choose_ref,
        chan_ref,
        head_ref,
        expand_ref,
        normed_ref,
        pre_ref,
        step_ref,
        y_ref,
        cum_ref,
        entering_ref,
        conv_ref,
        rows_ref,
        ext_ref,
        state_ref,
        hidden_ref,
    ) = refs
    block = pl.program_id(0)
    conv_width = inner + 2 * state_count
    ends = [info_ref[k] for k in range(3)]
    base = block * SPAN

    @pl.when(block == 0)
    def _():
        ext_ref[...] = jnp.zeros_like(ext_ref)
        state_ref[...] = jnp.zeros_like(state_ref)
        if parts:
            put = lambda k, value: place_rows(weight_ref, info_ref[4] ^ k, value)
            own_ref, near_ref, far_ref, beside_ref, close_ref, last_ref = part_refs
            put(2, close_ref[...])
            put(3, last_ref[...])
            put(0, own_ref[...])
            put(1, near_ref[...])
            for at in range(far_ref.shape[0]):
                k = 2 * (far_ref.shape[0] - at) + 2
                put(k, far_ref[at])
                put(k + 1, beside_ref[at])
        rows_ref[...] = mm(weight_ref[:, conv_width:], choose_ref[...], TN)[0:16, :]

    pick_piece(block, per_piece, info_ref[3], hidden_refs, hidden_ref)
    residual = hidden_ref[...].astype(f32)
    row_scale = lax.rsqrt(jnp.mean(residual * residual, axis=1, keepdims=True) + epsilon)
    normed = (residual * row_scale * rows_ref[GAIN_AT : GAIN_AT + 1, conv_width:]).astype(bf16)
    normed_ref[...] = normed
    pre = mm(normed, weight_ref[...])
    pre_ref[...] = pre[:, :conv_width].astype(bf16)
    step_ref[...] = pre[:, conv_width:]

    ext_ref[0:8, :] = ext_ref[SPAN : SPAN + 8, :]
    ext_ref[8 : 8 + SPAN, :] = pre[:, :conv_width]
    position = base + iota((SPAN, LANES), 0)
    start = doc_start(position, ends)
    conv = conv_block(ext_ref, rows_ref, position, start, conv_width)
    conv_ref[...] = conv
    active = conv * sigmoid(conv)
    x_val = active[:, :inner].astype(bf16).astype(f32)
    in_map = active[:, inner : inner + state_count].astype(bf16)
    out_map = active[:, inner + state_count :].astype(bf16)

    step_size = softplus(pre[:, conv_width:] + head_ref[1:2, :])
    log_decay = step_size * head_ref[0:1, :]
    row_at = iota((SPAN, SPAN), 0)
    col_at = iota((SPAN, SPAN), 1)
    lower = (col_at <= row_at).astype(f32).astype(bf16)
    cum = mm_left_exact(lower, log_decay * LOG2E)
    cum_ref[...] = cum
    cum_rows = cum.T

    start_last = scalar_start(base + SPAN - 1, ends)
    keep = (start < base).astype(f32)
    tail = (position >= start_last).astype(f32)
    survives = (start_last < base).astype(f32)
    expand = expand_ref[...]
    step_wide = widen(step_size, expand)
    decay_wide = widen(jnp.exp2(cum), expand)
    into_wide = widen(jnp.exp2(cum[SPAN - 1 :, :] - cum) * tail, expand)

    x_step = x_val * step_wide
    x_step_low = x_step.astype(bf16)
    state = state_ref[...]
    entering_ref[...] = state
    outside = mm(out_map, state.astype(bf16)) * (decay_wide * wide(keep, inner))
    visible = (col_at <= row_at) & (base + col_at >= wide(start, SPAN))
    scores = jnp.where(visible, mm(out_map, in_map, NT), 0.0)
    upper_half = iota((SPAN, LANES), 1) >= LANES // 2
    half = SPAN // 2
    inside = []
    for pair in range(heads // 2):
        x_pair = x_step_low[:, pair * LANES : (pair + 1) * LANES]
        tops, bottoms = [], []
        for which in range(2):
            head = 2 * pair + which
            column, row = cum[:, head : head + 1], cum_rows[head : head + 1, :]
            chosen = upper_half if which else jnp.logical_not(upper_half)
            x_head = jnp.where(chosen, x_pair, jnp.zeros_like(x_pair))
            decays = jnp.exp2(jnp.minimum(column[:half] - row[:, :half], 0.0))
            mixing = (scores[:half, :half] * decays).astype(bf16)
            tops.append(mm(mixing, x_head[:half]))
            far = jnp.exp2(column[half:] - row[:, :half])
            near = jnp.exp2(jnp.minimum(column[half:] - row[:, half:], 0.0))
            mixing = (scores[half:] * jnp.concatenate([far, near], axis=1)).astype(bf16)
            bottoms.append(mm(mixing, x_head))
        inside.append(jnp.concatenate([tops[0] + tops[1], bottoms[0] + bottoms[1]], axis=0))
    y_val = jnp.concatenate(inside, axis=1) + outside + chan_ref[0:1, :] * x_val
    y_ref[...] = y_val

    scaled = (x_step * into_wide).astype(bf16)
    state_ref[...] = (decay_wide[SPAN - 1 :, :] * survives) * state + mm(in_map, scaled, TN)


def branch_kernel(per_piece, pieces, info_ref, *refs):
    grad_refs, refs = refs[:pieces], refs[pieces:]
    normed_ref, y_ref, gate_w_ref, out_ref, chan_ref = refs[:5]
    gate_ref, branch_ref, stats_ref, grad_ref = refs[5:]
    block = pl.program_id(0)
    pick_piece(block, per_piece, info_ref[3], grad_refs, grad_ref)
    gate = mm(normed_ref[...], gate_w_ref[...])
    gate_ref[...] = gate
    mixed = y_ref[...] * (gate * sigmoid(gate))
    out_w = out_ref[...]
    gain = chan_ref[1:2, :]
    branch_ref[...] = mm((mixed * gain).astype(bf16), out_w, NT).astype(bf16)
    weighted = mm(grad_ref[...], out_w) * gain
    squares = jnp.sum(mixed * mixed, axis=1, keepdims=True)
    crossed = jnp.sum(weighted * mixed, axis=1, keepdims=True)
    lane = iota((mixed.shape[0], LANES), 1)
    both = jnp.where(lane == 0, squares, jnp.where(lane == 1, crossed, 0.0))
    stats_ref[...] = both.T[0:8, :]


def product_sums(left, right):
    products = left * right.astype(f32)
    return sum(products[:, at : at + LANES] for at in range(0, left.shape[1], LANES))


def gate_kernel(inner, inner_total, per_piece, pieces, info_ref, *refs):
    grad_refs, refs = refs[:pieces], refs[pieces:]
    (
        stats_ref,
        normed_ref,
        gate_w_ref,
        out_ref,
        gate_ref,
        y_ref,
        chan_ref,
        gate_grad_ref,
        y_grad_ref,
        early_ref,
        gain_grad_ref,
        product_ref,
        gate_acc,
        out_acc,
        grad_ref,
    ) = refs
    block = pl.program_id(0)

    @pl.when(block == 0)
    def _():
        gate_acc[...] = jnp.zeros_like(gate_acc)
        out_acc[...] = jnp.zeros_like(out_acc)
        gain_grad_ref[...] = jnp.zeros_like(gain_grad_ref)

    pick_piece(block, per_piece, info_ref[3], grad_refs, grad_ref)
    stats = stats_ref[...].T
    gate_scale = lax.rsqrt(stats[:, 0:1] / inner_total + epsilon)
    crossed = stats[:, 1:2] / inner_total
    gate = gate_ref[...]
    gate_sig = sigmoid(gate)
    gate_act = gate * gate_sig
    y_val = y_ref[...]
    mixed = y_val * gate_act
    grad = grad_ref[...]
    gain = chan_ref[1:2, :]
    gated_grad = mm(grad, out_ref[...])
    scaled_mixed = mixed * gate_scale
    out_acc[...] += mm(grad, (scaled_mixed * gain).astype(bf16), TN)
    gain_grad_ref[0:1, :] += jnp.sum(gated_grad * scaled_mixed, axis=0, keepdims=True)
    mixed_grad = gate_scale * (gated_grad * gain) - scaled_mixed * (
        gate_scale * gate_scale * crossed
    )
    gate_grad = mixed_grad * y_val * (gate_sig * (1.0 + gate * (1.0 - gate_sig)))
    gate_grad = gate_grad.astype(bf16)
    gate_grad_ref[...] = gate_grad
    y_grad_ref[...] = (mixed_grad * gate_act).astype(bf16)
    gate_acc[...] += mm(normed_ref[...], gate_grad, TN)

    @pl.when(block == pl.num_programs(0) - 1)
    def _():
        early_ref[:, :inner] = gate_acc[...].astype(bf16)
        early_ref[:, inner:] = out_acc[...].astype(bf16)
        product_ref[...] = product_sums(gate_acc[...], gate_w_ref[...])


def backward_kernel(inner, state_count, heads, blocks, info_ref, *refs):
    (
        normed_ref,
        weight_ref,
        gate_w_ref,
        pre_ref,
        halo_ref,
        step_ref,
        conv_ref,
        y_ref,
        y_grad_ref,
        gate_grad_ref,
        cum_ref,
        entering_ref,
        rows_ref,
        chan_ref,
        head_ref,
        expand_ref,
        gather_ref,
    ) = refs[:17]
    refs = refs[17:]
    product_ref, choose_ref, extra_ref, total_ref, late_ref = refs[:5]
    ext_ref, next_ref, pre_grad_ref, state_grad_ref, late_acc, small_ref, heads_ref = refs[5:]
    step = pl.program_id(0)
    block = blocks - 1 - step
    base = block * SPAN
    conv_width = inner + 2 * state_count
    ends = [info_ref[k] for k in range(3)]

    @pl.when(step == 0)
    def _():
        next_ref[...] = jnp.zeros_like(next_ref)
        state_grad_ref[...] = jnp.zeros_like(state_grad_ref)
        late_acc[...] = jnp.zeros_like(late_acc)
        small_ref[...] = jnp.zeros_like(small_ref)
        heads_ref[...] = jnp.zeros_like(heads_ref)

    skip = chan_ref[0:1, :]
    y_val = y_ref[...]
    y_grad_low = y_grad_ref[...]
    y_grad = y_grad_low.astype(f32)

    ext_ref[0:8, :] = halo_ref[...].astype(f32)[8:16, :]
    ext_ref[8 : 8 + SPAN, :] = pre_ref[...].astype(f32)
    position = base + iota((SPAN, LANES), 0)
    start = doc_start(position, ends)
    conv = conv_ref[...]
    conv_sig = sigmoid(conv)
    active = conv * conv_sig
    act_slope = conv_sig * (1.0 + conv * (1.0 - conv_sig))
    x_val = active[:, :inner].astype(bf16).astype(f32)
    in_map = active[:, inner : inner + state_count].astype(bf16)
    out_map = active[:, inner + state_count :].astype(bf16)

    step_pre = step_ref[...] + head_ref[1:2, :]
    step_size = softplus(step_pre)
    rates = head_ref[0:1, :]
    cum = cum_ref[...]
    cum_rows = cum.T
    start_last = scalar_start(base + SPAN - 1, ends)
    keep = (start < base).astype(f32)
    tail = (position >= start_last).astype(f32)
    survives = (start_last < base).astype(f32)
    expand = expand_ref[...]
    step_wide = widen(step_size, expand)
    decay_wide = widen(jnp.exp2(cum), expand)
    into_wide = widen(jnp.exp2(cum[SPAN - 1 :, :] - cum) * tail, expand)
    keep_decay = decay_wide * wide(keep, inner)
    last_decay = decay_wide[SPAN - 1 :, :] * survives

    x_step = x_val * step_wide
    x_step_low = x_step.astype(bf16)
    scaled = (x_step * into_wide).astype(bf16)
    entering = entering_ref[...]
    entering_low = entering.astype(bf16)
    state_grad = state_grad_ref[...]
    state_grad_low = state_grad.astype(bf16)

    outside = mm(out_map, entering_low)
    outside_grad = (y_grad * keep_decay).astype(bf16)
    scaled_grad = mm(in_map, state_grad_low)
    out_map_grad = mm(outside_grad, entering_low, NT)
    in_map_grad = mm(scaled, state_grad_low, NT)
    state_grad_ref[...] = last_decay * state_grad + mm(out_map, outside_grad, TN)

    row_at = iota((SPAN, SPAN), 0)
    col_at = iota((SPAN, SPAN), 1)
    col_start = doc_start(base + col_at, ends)
    visible = (row_at <= col_at) & (base + row_at >= col_start)
    scores = jnp.where(visible, mm(in_map, out_map, NT), 0.0)
    upper_half = iota((SPAN, LANES), 1) >= LANES // 2
    half = SPAN // 2
    top_grad = jnp.zeros((half, SPAN), f32)
    bottom_grad = jnp.zeros((half, half), f32)
    x_step_grads = []
    for pair in range(heads // 2):
        x_pair = x_step_low[:, pair * LANES : (pair + 1) * LANES]
        grad_pair = y_grad_low[:, pair * LANES : (pair + 1) * LANES]
        tops, bottoms = [], []
        for which in range(2):
            head = 2 * pair + which
            column, row = cum[:, head : head + 1], cum_rows[head : head + 1, :]
            chosen = upper_half if which else jnp.logical_not(upper_half)
            grad_head = jnp.where(chosen, grad_pair, jnp.zeros_like(grad_pair))
            near = jnp.exp2(jnp.minimum(row[:, :half] - column[:half], 0.0))
            far = jnp.exp2(row[:, half:] - column[:half])
            decays = jnp.concatenate([near, far], axis=1)
            top_grad = top_grad + mm(x_pair[:half], grad_head, NT) * decays
            tops.append(mm((scores[:half] * decays).astype(bf16), grad_head))
            decays = jnp.exp2(jnp.minimum(row[:, half:] - column[half:], 0.0))
            bottom_grad = bottom_grad + mm(x_pair[half:], grad_head[half:], NT) * decays
            tail_mix = (scores[half:, half:] * decays).astype(bf16)
            bottoms.append(mm(tail_mix, grad_head[half:]))
        x_step_grads.append(
            jnp.concatenate([tops[0] + tops[1], bottoms[0] + bottoms[1]], axis=0)
        )
    x_step_grad = jnp.concatenate(x_step_grads, axis=1)
    bottom_grad = jnp.concatenate([jnp.zeros((half, half), f32), bottom_grad], axis=1)
    score_grad = jnp.concatenate([top_grad, bottom_grad], axis=0)
    score_grad = jnp.where(visible, score_grad, 0.0).astype(bf16)
    in_map_grad = in_map_grad + mm(score_grad, out_map)
    out_map_grad = out_map_grad + mm(score_grad, in_map, TN)

    inside = y_val - skip * x_val - keep_decay * outside
    into_terms = scaled.astype(f32) * scaled_grad
    cum_terms = (
        y_grad * inside
        + outside_grad.astype(f32) * outside
        - x_step_low.astype(f32) * x_step_grad
        - into_terms
    )
    last_terms = jnp.sum(into_terms, axis=0, keepdims=True) + last_decay * jnp.sum(
        state_grad * entering, axis=0, keepdims=True
    )
    last_row = iota((SPAN, inner), 0) == SPAN - 1
    cum_terms = cum_terms + jnp.where(last_row, last_terms, 0.0)
    x_step_grad = x_step_grad + into_wide * scaled_grad
    gather = gather_ref[...]
    cum_grad = mm_right_exact(cum_terms, gather)
    step_grad = mm_right_exact(x_val * x_step_grad, gather)
    upper = (row_at <= col_at).astype(f32).astype(bf16)
    log_grad = mm_left_exact(upper, cum_grad)
    step_grad = (step_grad + log_grad * rates) * sigmoid(step_pre)
    pre_grad_ref[:, conv_width:] = step_grad.astype(bf16)
    x_grad = skip * y_grad + step_wide * x_step_grad

    heads_ref[0:1, :] += jnp.sum(y_grad * x_val, axis=0, keepdims=True)
    heads_ref[1:2, :LANES] += jnp.sum(step_size * rates * log_grad, axis=0, keepdims=True)
    heads_ref[2:3, :LANES] += jnp.sum(step_grad, axis=0, keepdims=True)

    conv_grad = jnp.concatenate([x_grad, in_map_grad, out_map_grad], axis=1) * act_slope
    next_ref[SPAN : SPAN + 8, :] = next_ref[0:8, :]
    next_ref[0:SPAN, :] = conv_grad
    back = [None] + [(position - k >= start).astype(f32) for k in range(1, CONV)]
    ahead = [None] + [
        (position >= doc_start(position + k, ends)).astype(f32) for k in range(1, CONV)
    ]
    for col in range(0, conv_width, LANES):
        cols = slice(col, col + LANES)
        grad_here = next_ref[0:SPAN, cols]
        total = grad_here * tap_row(rows_ref, 0, cols)
        small_ref[TAPS_AT + CONV - 1 : TAPS_AT + CONV, cols] += jnp.sum(
            grad_here * ext_ref[8 : 8 + SPAN, cols], axis=0, keepdims=True
        )
        for k in range(1, CONV):
            total = total + next_ref[k : k + SPAN, cols] * ahead[k] * (
                tap_row(rows_ref, k, cols)
            )
            small_ref[TAPS_AT + CONV - 1 - k : TAPS_AT + CONV - k, cols] += jnp.sum(
                grad_here * back[k] * ext_ref[8 - k : 8 - k + SPAN, cols], axis=0, keepdims=True
            )
        pre_grad_ref[:, cols] = total.astype(bf16)

    pre_grads = pre_grad_ref[...]
    total = mm(pre_grads, weight_ref[...], NT) + mm(gate_grad_ref[...], gate_w_ref[...], NT)
    total_ref[...] = total.astype(bf16)
    late_acc[...] += mm(normed_ref[...], pre_grads, TN)

    @pl.when(step == pl.num_programs(0) - 1)
    def _():
        late = late_acc[...]
        sums = product_sums(late, weight_ref[...]) + product_ref[...]
        gain = weight_ref[:, conv_width + GAIN_AT : conv_width + GAIN_AT + 1].astype(f32)
        sums = jnp.sum(sums, axis=1, keepdims=True) / gain
        chosen = small_ref[...].astype(bf16)
        filler = jnp.zeros((LANES - chosen.shape[0], chosen.shape[1]), bf16)
        misc = mm(choose_ref[...], jnp.concatenate([chosen, filler], axis=0), NT)
        misc = misc + jnp.where(iota(misc.shape, 1) == GAIN_AT, sums, 0.0)
        totals = heads_ref[...]
        skips = mm_right_exact(totals, gather_ref[...])
        per_head = [totals[1:2, :LANES], totals[2:3, :LANES], skips[0:1, :]]
        for at_head, value in enumerate(per_head):
            value = jnp.broadcast_to(value, (8, LANES))
            misc = misc + pltpu.roll(value, HEAD_AT + at_head * heads, 1)[0:1, :]
        late_ref[:, :conv_width] = late[:, :conv_width].astype(bf16)
        late_ref[:, conv_width:] = (late[:, conv_width:] + misc + extra_ref[...]).astype(bf16)


def weights_kernel(early_count, inner, *refs):
    early_refs, late_refs = refs[:early_count], refs[early_count:-3]
    zx_ref, out_ref, rest_ref = refs[-3:]
    early = tree_sum([ref[...].astype(f32) for ref in early_refs])
    late = tree_sum([ref[...].astype(f32) for ref in late_refs])
    zx_ref[0] = early[:, :inner]
    zx_ref[1] = late[:, :inner]
    out_ref[...] = early[:, inner:]
    rest_ref[...] = late[:, inner:]


def hidden_kernel(
    gain_at, hidden_ref, grad_ref, own_ref, near_ref, far_ref, rest_ref, rows_ref, out_ref
):
    gain = rows_ref[GAIN_AT : GAIN_AT + 1, gain_at:]
    half = far_ref.shape[0]
    for at, part_ref in ((0, far_ref), (half, rest_ref)):
        rows = slice(at, at + half)
        total = own_ref[rows, :].astype(f32) + near_ref[rows, :].astype(f32)
        scaled = (total + part_ref[...].astype(f32)) * gain
        residual = hidden_ref[rows, :].astype(f32)
        row_scale = lax.rsqrt(jnp.mean(residual * residual, axis=1, keepdims=True) + epsilon)
        crossed = jnp.mean(scaled * residual, axis=1, keepdims=True)
        result = row_scale * scaled - residual * (row_scale * row_scale * row_scale * crossed)
        out_ref[rows, :] = (result + grad_ref[rows, :].astype(f32)).astype(bf16)


def swap(values, axis, bits):
    size = lax.axis_size(axis)
    return lax.ppermute(values, axis, [(i, i ^ bits) for i in range(size)])


def bits_of(size):
    return [1 << k for k in range(size.bit_length() - 1)]


def after(values, *others):
    return lax.optimization_barrier((values,) + others)[0]


def sum_over(values, axis):
    size = lax.axis_size(axis)
    if size > 8:
        for bit in bits_of(size):
            values = values + swap(values, axis, bit)
        return values
    return tree_sum([values] + [swap(values, axis, k) for k in range(1, size)])


def tree_sum(pieces):
    while len(pieces) > 1:
        pieces = [pieces[k] + pieces[k + 1] for k in range(0, len(pieces), 2)]
    return pieces[0]


def gather_far(values, axis):
    pieces = {0: values}
    bits = bits_of(lax.axis_size(axis))
    for bit in reversed(bits[1:]):
        pieces.update({k | bit: swap(piece, axis, bit) for k, piece in list(pieces.items())})
    pieces[1] = swap(values, axis, 1)
    return pieces


def gather_near(pieces, axis, *others):
    pieces = dict(pieces)
    for k in list(pieces):
        if k > 1:
            pieces[k | 1] = swap(after(pieces[k], *others) if others else pieces[k], axis, 1)
    return [pieces[k] for k in range(len(pieces))]


def gather_direct(values, axis, others):
    size = lax.axis_size(axis)
    near = swap(values, axis, 1)
    far = [swap(values, axis, k) for k in range(size - 2, 2, -2)]
    close = swap(values, axis, 2)
    last = swap(close, axis, 1)
    far, last = lax.optimization_barrier((jnp.stack(far), last, *others))[:2]
    return values, near, far, swap(far, axis, 1), close, last


def assemble(own, near, far, beside, close, last, axis):
    size = lax.axis_size(axis)
    place = lax.axis_index(axis)
    result = jnp.zeros((size,) + own.shape, own.dtype)
    pieces = {0: own, 1: near, 2: close, 3: last}
    for at, k in enumerate(range(size - 2, 2, -2)):
        pieces.update({k: far[at], k + 1: beside[at]})
    for k in range(size):
        result = lax.dynamic_update_slice(
            result, pieces[k][None], (place ^ k,) + (0,) * own.ndim
        )
    return result.reshape((-1,) + own.shape[1:])


def gather_pairs(values, other, axis):
    size = lax.axis_size(axis)
    place = lax.axis_index(axis)
    first = place % 2 == 0
    pair = jnp.stack([jnp.where(first, values, other), jnp.where(first, other, values)])
    result = jnp.zeros((size // 2,) + pair.shape, values.dtype)
    for k in range(0, size, 2):
        piece = swap(pair, axis, k) if k else pair
        result = lax.dynamic_update_slice(
            result, piece[None], ((place ^ k) // 2,) + (0,) * pair.ndim
        )
    return result.reshape((-1,) + values.shape[1:])


def block_of(values, place, share):
    return lax.dynamic_slice_in_dim(values, place * share, share, 0)


def fold_pairs(values, axis, steps):
    size = lax.axis_size(axis)
    place = lax.axis_index(axis)
    share = values.shape[0] // size
    theirs = jnp.stack([block_of(values, place ^ k ^ 1, share) for k in steps])
    return swap(theirs, axis, 1)


def fold_sums(values, theirs, axis, steps):
    place = lax.axis_index(axis)
    share = values.shape[0] // lax.axis_size(axis)
    sums = [
        block_of(values, place ^ k, share).astype(f32) + theirs[at].astype(f32)
        for at, k in enumerate(steps)
    ]
    return [both.astype(bf16) if k else both for k, both in zip(steps, sums)]


def send_sums(folded, axis, steps):
    return [
        swap(both, axis, k) if k else both for k, both in zip(steps, folded)
    ]


def per_device(
    hidden_rows,
    out_grad,
    doc_lengths,
    zx_weight,
    step_weight,
    bc_weight,
    conv_inner,
    conv_shared,
    out_weight,
    decay_log,
    step_bias,
    skip_gain,
    norm_gain,
    gate_gain,
):
    piece_len, _, width = hidden_rows.shape
    tensor = lax.axis_size("tensor")
    data = lax.axis_size("dp")
    full_len = piece_len * tensor
    blocks = full_len // SPAN
    per_piece = piece_len // SPAN
    share = zx_weight.shape[1]
    inner = zx_weight.shape[2]
    heads = step_weight.shape[1]
    head_dim = inner // heads
    state_count = bc_weight.shape[1] // 2
    conv_width = inner + 2 * state_count
    span = conv_width + LANES
    inner_total = float(inner * tensor)
    mine = lax.axis_index("tensor")
    place = lax.axis_index("dp")

    hidden = hidden_rows[:, 0, :]
    hidden_all = gather_far(hidden, "tensor")
    hidden_far = hidden_all[tensor // 2]
    hidden_all = gather_near(hidden_all, "tensor")

    inner_share = conv_inner.size // CONV
    shared_share = conv_shared.size // CONV
    taps = jnp.concatenate([conv_inner.reshape(-1, CONV), conv_shared.reshape(-1, CONV)])
    taps = jnp.pad(taps, ((0, share - inner_share - shared_share), (0, 0)))
    misc = jnp.concatenate(
        [
            jnp.pad(step_weight, ((0, 0), (0, TAPS_AT - heads))),
            taps,
            norm_gain[:, None],
            jnp.zeros((share, LANES - GAIN_AT - 1), bf16),
        ],
        axis=1,
    )
    channel = np.arange(inner)
    per_dev = head_dim // data
    sources = [
        (channel % head_dim) // per_dev * share
        + channel // head_dim * per_dev
        + channel % per_dev,
        np.arange(2 * state_count) // shared_share * share
        + inner_share
        + np.arange(2 * state_count) % shared_share,
        np.arange(width),
    ]
    sources = jnp.asarray(np.concatenate(sources), jnp.int32)
    choose = (jnp.arange(width, dtype=jnp.int32)[:, None] == sources[None, :]).astype(bf16)
    chan = jnp.pad(jnp.stack([jnp.repeat(skip_gain, head_dim), gate_gain]), ((0, 6), (0, 0)))
    head_rows = jnp.pad(
        jnp.stack([-jnp.exp(decay_log), step_bias]), ((0, 6), (0, LANES - heads))
    )
    channel_head = jnp.arange(inner)[None, :] // head_dim
    expand = (jnp.arange(LANES)[:, None] % (LANES // 2) == channel_head).astype(bf16)
    gather = (jnp.arange(LANES)[:, None] == channel_head).astype(bf16).T
    lengths = doc_lengths[0].astype(jnp.int32)
    info = jnp.stack(
        [lengths[0], lengths[0] + lengths[1], lengths[0] + lengths[1] + lengths[2], mine, place]
    ).astype(jnp.int32)

    late_shard = jnp.concatenate([zx_weight[0], out_weight.T], axis=1)
    late_other = swap(late_shard, "dp", 1)
    shard = jnp.concatenate([zx_weight[1], bc_weight, misc], axis=1)
    weight_parts = gather_direct(
        shard, "dp", (hidden_far, late_other, choose, chan, head_rows, expand, info)
    )
    in_kernel = share % 16 == 0
    if not in_kernel:
        weight_parts = (assemble(*weight_parts, "dp"),)
    weights_late = gather_pairs(late_shard, late_other, "dp")
    grad_all = gather_far(after(out_grad, hidden_far)[:, 0, :], "tensor")

    def limits(mebi):
        return pltpu.CompilerParams(
            dimension_semantics=("arbitrary",), vmem_limit_bytes=mebi * 1024 * 1024
        )

    shaped = jax.ShapeDtypeStruct

    def fixed(shape, at=0):
        return pl.BlockSpec(shape, lambda i, info: (0,) * (len(shape) - 1) + (at,))

    def rows(cols, at=0, order=lambda i: i):
        return pl.BlockSpec((SPAN, cols), lambda i, info: (order(i), at))

    def piece_specs(order=lambda i: i):
        return [
            pl.BlockSpec(
                (SPAN, width),
                lambda i, info, k=k: (
                    jnp.clip(order(i) - (info[3] ^ k) * per_piece, 0, per_piece - 1),
                    0,
                ),
            )
            for k in range(tensor)
        ]

    def call(
        kernel, name, micros, steps, in_specs, out_specs, out_shape, scratch, args, aliases={}
    ):
        return pl.pallas_call(
            kernel,
            grid_spec=pltpu.PrefetchScalarGridSpec(
                num_scalar_prefetch=1,
                grid=(steps,),
                in_specs=in_specs,
                out_specs=out_specs,
                scratch_shapes=scratch,
            ),
            out_shape=out_shape,
            compiler_params=limits(56 if name == "backward" else 36),
            input_output_aliases=aliases,
            cost_estimate=pl.CostEstimate(
                flops=int(micros * 1.0e9), bytes_accessed=int(micros * 3.0e6), transcendentals=0
            ),
            name=name,
        )(info, *args)

    def relative(order):
        return pl.BlockSpec(
            (SPAN, width),
            lambda i, info: (
                ((order(i) // per_piece) ^ info[3]) * per_piece + order(i) % per_piece,
                0,
            ),
        )

    natural = lambda i: i
    state_spec = lambda order: pl.BlockSpec(
        (state_count, inner), lambda i, info: (order(i), 0)
    )
    normed, pre, step_pre, y_val, cum, entering, conv, rows_all, *weights = call(
        functools.partial(
            forward_kernel,
            inner,
            state_count,
            heads,
            per_piece,
            tensor,
            len(weight_parts) if in_kernel else 0,
        ),
        "forward",
        22,
        blocks,
        piece_specs()
        + [fixed(part.shape) for part in weight_parts]
        + [
            fixed(choose.shape),
            fixed(chan.shape),
            fixed(head_rows.shape),
            fixed(expand.shape),
        ],
        [
            rows(width),
            rows(conv_width),
            rows(LANES),
            rows(inner),
            rows(LANES),
            state_spec(natural),
            rows(conv_width),
            fixed((16, conv_width + width)),
        ]
        + [fixed((width, span))] * in_kernel,
        [
            shaped((full_len, width), bf16),
            pltpu.HBM((full_len, conv_width), bf16),
            pltpu.HBM((full_len, LANES), f32),
            shaped((full_len, inner), f32),
            pltpu.HBM((full_len, LANES), f32),
            pltpu.HBM((blocks * state_count, inner), f32),
            pltpu.HBM((full_len, conv_width), f32),
            shaped((16, conv_width + width), f32),
        ]
        + [shaped((width, span), bf16)] * in_kernel,
        [
            pltpu.VMEM((SPAN + 8, conv_width), f32),
            pltpu.VMEM((state_count, inner), f32),
            pltpu.VMEM((SPAN, width), bf16),
        ],
        (*hidden_all, *weight_parts, choose, chan, head_rows, expand),
    )
    (weights,) = weights or weight_parts

    tall = lambda cols: pl.BlockSpec((piece_len, cols), lambda i, info: (i, 0))
    whole_pieces = [fixed((piece_len, width))] * tensor
    grad_all = gather_near(grad_all, "tensor", rows_all)
    gate_spec, out_spec = fixed((width, inner)), fixed((width, inner), 1)
    gate, branch, stats = call(
        functools.partial(branch_kernel, 1, tensor),
        "branch",
        11,
        tensor,
        whole_pieces + [tall(width), tall(inner), gate_spec, out_spec, fixed(chan.shape)],
        [tall(inner), pl.BlockSpec((piece_len, width), lambda i, info: (i ^ info[3], 0)), pl.BlockSpec((8, piece_len), lambda i, info: (0, i))],
        [
            shaped((full_len, inner), f32),
            shaped((full_len, width), bf16),
            shaped((8, full_len), f32),
        ],
        [pltpu.VMEM((piece_len, width), bf16)],
        (*grad_all, normed, y_val, weights_late, weights_late, chan),
    )

    cut = lambda values, k: values[k * piece_len : (k + 1) * piece_len]
    branch_sum = cut(branch, 2).astype(f32) + swap(cut(branch, 3), "tensor", 1).astype(f32)
    branch_sum = branch_sum.astype(bf16)
    branch_near = swap(cut(branch, 1), "tensor", 1)
    stats = sum_over(stats, "tensor")

    gate_grad, y_grad, early, gain_grad, product = call(
        functools.partial(gate_kernel, inner, inner_total, 1, tensor),
        "gate_back",
        13,
        tensor,
        whole_pieces
        + [
            pl.BlockSpec((8, piece_len), lambda i, info: (0, i)),
            tall(width),
            gate_spec,
            out_spec,
            tall(inner),
            tall(inner),
            fixed(chan.shape),
        ],
        [
            tall(inner),
            tall(inner),
            fixed((width, 2 * inner)),
            fixed((8, inner)),
            fixed((width, LANES)),
        ],
        [
            pltpu.HBM((full_len, inner), bf16),
            pltpu.HBM((full_len, inner), bf16),
            shaped((width, 2 * inner), bf16),
            shaped((8, inner), f32),
            shaped((width, LANES), f32),
        ],
        [
            pltpu.VMEM((width, inner), f32),
            pltpu.VMEM((width, inner), f32),
            pltpu.VMEM((piece_len, width), bf16),
        ],
        (*grad_all, stats, normed, weights_late, weights_late, gate, y_val, chan),
    )
    far_first = list(range(data - 2, -1, -2))
    early_theirs = fold_pairs(early, "dp", far_first)
    gate_grad, branch_sum = lax.optimization_barrier((gate_grad, branch_sum))
    branch_far = swap(branch_sum, "tensor", 2)

    small_width = conv_width + width
    back = lambda i: blocks - 1 - i
    back_rows = lambda cols: rows(cols, 0, back)
    gate_lanes = inner // share
    extra = jnp.tile(gain_grad[0].reshape(gate_lanes, share).T, (data, 1))
    extra = jnp.pad(extra, ((0, 0), (GATE_AT, LANES - GATE_AT - gate_lanes)))
    total, late = call(
        functools.partial(backward_kernel, inner, state_count, heads, blocks),
        "backward",
        36,
        blocks,
        [
            back_rows(width),
            fixed((width, span)),
            gate_spec,
            back_rows(conv_width),
            pl.BlockSpec(
                (16, conv_width),
                lambda i, info: (jnp.maximum(back(i) * (SPAN // 16) - 1, 0), 0),
            ),
            back_rows(LANES),
            back_rows(conv_width),
            back_rows(inner),
            back_rows(inner),
            back_rows(inner),
            back_rows(LANES),
            state_spec(back),
            fixed((16, small_width)),
            fixed(chan.shape),
            fixed(head_rows.shape),
            fixed(expand.shape),
            fixed(gather.shape),
            fixed((width, LANES)),
            fixed((width, conv_width)),
            fixed((width, LANES)),
        ],
        [relative(back), fixed((width, span))],
        [shaped((full_len, width), bf16), shaped((width, span), bf16)],
        [
            pltpu.VMEM((SPAN + 8, conv_width), f32),
            pltpu.VMEM((SPAN + 8, conv_width), f32),
            pltpu.VMEM((SPAN, span), bf16),
            pltpu.VMEM((state_count, inner), f32),
            pltpu.VMEM((width, span), f32),
            pltpu.VMEM((16, conv_width), f32),
            pltpu.VMEM((8, inner), f32),
        ],
        (
            normed,
            weights,
            weights_late,
            pre,
            pre,
            step_pre,
            conv,
            y_val,
            y_grad,
            gate_grad,
            cum,
            entering,
            rows_all,
            chan,
            head_rows,
            expand,
            gather,
            product,
            choose,
            extra,
        ),
    )

    total, late, branch_near, branch_far, early_theirs = lax.optimization_barrier(
        (total, late, branch_near, branch_far, early_theirs)
    )
    early_pieces = send_sums(
        fold_sums(early, early_theirs, "dp", far_first), "dp", far_first
    )
    total_sum = cut(total, 2).astype(f32) + swap(cut(total, 3), "tensor", 1).astype(f32)
    total_sum = total_sum.astype(bf16)
    groups = far_first[: len(far_first) // 2], far_first[len(far_first) // 2 :]
    theirs = [fold_pairs(late, "dp", steps) for steps in groups]
    total_far = swap(total_sum[: piece_len // 2], "tensor", 2)
    total_rest = swap(total_sum[piece_len // 2 :], "tensor", 2)
    theirs[0], total = lax.optimization_barrier((theirs[0], after(total, total_sum)))
    folded = fold_sums(late, theirs[0], "dp", groups[0])
    theirs[1] = after(theirs[1], total_far, *folded)
    folded += fold_sums(late, theirs[1], "dp", groups[1])
    branch_far, _ = lax.optimization_barrier((branch_far, folded[0]))
    late_pieces = send_sums(folded, "dp", far_first)
    total_own, total_near = cut(total, 0), swap(cut(total, 1), "tensor", 1)

    def whole(kernel, name, out_shape, args):
        return pl.pallas_call(
            kernel, out_shape=out_shape, compiler_params=plain, name=name
        )(*args)

    plain = pltpu.CompilerParams(vmem_limit_bytes=24 * 1024 * 1024)
    zx_part, out_part, rest_part = whole(
        functools.partial(weights_kernel, len(early_pieces), inner),
        "weight_sums",
        [
            shaped((2, share, inner), f32),
            shaped((share, inner), f32),
            shaped((share, span - inner), f32),
        ],
        (*early_pieces, *late_pieces),
    )
    rest_part, total_rest = lax.optimization_barrier((rest_part, total_rest))
    misc_part = rest_part[:, 2 * state_count :]
    shared = [rest_part] + [swap(rest_part, "tensor", k) for k in range(1, tensor)]
    hidden_grad = whole(
        functools.partial(hidden_kernel, conv_width),
        "hidden_back",
        shaped((piece_len, width), bf16),
        (hidden, grad_all[0], total_own, total_near, total_far, total_rest, rows_all),
    )
    hidden_grad, *shared = lax.optimization_barrier((hidden_grad, *shared))
    shared_part = tree_sum(shared)
    bc_part, misc_shared = shared_part[:, : 2 * state_count], shared_part[:, 2 * state_count :]

    residual = hidden.astype(f32)
    gate_scale = lax.rsqrt(
        lax.dynamic_slice_in_dim(stats[0], mine * piece_len, piece_len) / inner_total + epsilon
    )
    branch_local = (
        cut(branch, 0).astype(f32) + branch_near.astype(f32) + branch_far.astype(f32)
    )
    block_out = (residual + branch_local * gate_scale[:, None]).astype(bf16)
    taps_at = slice(TAPS_AT, TAPS_AT + CONV)
    head_values = misc_part[0, HEAD_AT : HEAD_AT + 3 * heads]
    return (
        block_out[:, None, :],
        hidden_grad[:, None, :],
        zx_part,
        misc_part[:, :heads],
        bc_part,
        misc_part[:inner_share, taps_at].reshape(conv_inner.shape),
        misc_shared[inner_share : inner_share + shared_share, taps_at].reshape(-1),
        out_part.T,
        head_values[:heads],
        head_values[heads : 2 * heads],
        head_values[2 * heads :],
        misc_shared[:, GAIN_AT],
        misc_part[:, GATE_AT : GATE_AT + gate_lanes].T.reshape(-1),
    )


def solution(mesh):
    in_specs = (
        P("tensor", "dp", None),
        P("tensor", "dp", None),
        P("dp", None),
        P(None, "dp", "tensor"),
        P("dp", "tensor"),
        P("dp", None),
        P("tensor", "dp"),
        P("dp"),
        P("tensor", "dp"),
        P("tensor"),
        P("tensor"),
        P("tensor"),
        P("dp"),
        P("tensor"),
    )
    out_specs = (
        P("tensor", "dp", None),
        P("tensor", "dp", None),
        P(None, "dp", "tensor"),
        P("dp", "tensor"),
        P("dp", None),
        P("tensor", "dp"),
        P("dp"),
        P("tensor", "dp"),
        P("tensor"),
        P("tensor"),
        P("tensor"),
        P("dp"),
        P("tensor"),
    )
    return jax.shard_map(
        per_device, mesh=mesh, in_specs=in_specs, out_specs=out_specs, check_vma=False
    )
```

```python
import functools

import jax
import jax.numpy as jnp
import numpy as np
from jax import lax
from jax.experimental import pallas as pl
from jax.experimental.pallas import tpu as pltpu
from jax.sharding import PartitionSpec as P

CONV = 4
SPAN = 256
LANES = 128
TAPS_AT = 8
GAIN_AT = 12
GATE_AT = 16
HEAD_AT = 64
LOG2E = 1.4426950408889634
epsilon = 1e-05
bf16 = jnp.bfloat16
f32 = jnp.float32
NN = (((1,), (0,)), ((), ()))
NT = (((1,), (1,)), ((), ()))
TN = (((0,), (0,)), ((), ()))


def mm(left, right, dims=NN):
    return lax.dot_general(left, right, dims, preferred_element_type=f32)


def split(values, parts):
    pieces = []
    for _ in range(parts):
        piece = values.astype(bf16)
        pieces.append(piece)
        values = values - piece.astype(f32)
    return pieces


def mm_left_exact(left, right):
    both = mm(left, jnp.concatenate(split(right, 2), axis=1))
    return both[:, : right.shape[1]] + both[:, right.shape[1] :]


def mm_right_exact(left, right):
    return sum(mm(piece, right) for piece in split(left, 2))


def widen(values, expand):
    half = LANES // 2
    first = jnp.where(iota(values.shape, 1) < half, values, 0.0)
    high = first.astype(bf16).astype(f32)
    packed = (high + pltpu.roll(first - high, half, 1)).astype(bf16)
    return mm(packed, expand)


def sigmoid(values):
    return 1.0 / (1.0 + jnp.exp(-values))


def softplus(values):
    return jnp.maximum(values, 0.0) + jnp.log1p(jnp.exp(-jnp.abs(values)))


def doc_start(position, ends):
    start = jnp.zeros_like(position)
    for end in ends:
        start = jnp.where(position >= end, end, start)
    return start


def scalar_start(position, ends):
    start = jnp.int32(0)
    for end in ends:
        start = jnp.where(position >= end, end, start)
    return start


def iota(shape, dim):
    return lax.broadcasted_iota(jnp.int32, shape, dim)


def tap_row(rows_ref, back, cols):
    at = TAPS_AT + CONV - 1 - back
    return rows_ref[at : at + 1, cols]


def conv_block(ext_ref, rows_ref, position, start, width):
    masks = [None] + [(position - k >= start).astype(f32) for k in range(1, CONV)]
    groups = []
    for at in range(0, width, LANES):
        cols = slice(at, at + LANES)
        total = ext_ref[8 : 8 + SPAN, cols] * tap_row(rows_ref, 0, cols)
        for k in range(1, CONV):
            total = total + ext_ref[8 - k : 8 - k + SPAN, cols] * masks[k] * (
                tap_row(rows_ref, k, cols)
            )
        groups.append(total)
    return jnp.concatenate(groups, axis=1)


def wide(mask, width):
    return jnp.concatenate([mask] * (width // LANES), axis=1)


def pick_piece(block, per_piece, mine, refs, chosen_ref):
    relative = (block // per_piece) ^ mine
    for k, ref in enumerate(refs):

        @pl.when(relative == k)
        def _(ref=ref):
            chosen_ref[...] = ref[...]


def place_rows(ref, slot, values):
    rows = values.shape[0]
    ref[pl.ds(pl.multiple_of(slot * rows, 16), rows), :] = values


def forward_kernel(
    inner,
    state_count,
    heads,
    per_piece,
    pieces,
    parts,
    info_ref,
    *refs,
):
    hidden_refs, refs = refs[:pieces], refs[pieces:]
    part_refs, refs = refs[:parts], refs[parts:]
    if parts:
        refs, weight_ref, scratch = refs[:-4], refs[-4], refs[-3:]
        refs = refs + scratch
    else:
        weight_ref, refs = refs[0], refs[1:]
    (
        choose_ref,
        chan_ref,
        head_ref,
        expand_ref,
        normed_ref,
        pre_ref,
        step_ref,
        y_ref,
        cum_ref,
        entering_ref,
        conv_ref,
        rows_ref,
        ext_ref,
        state_ref,
        hidden_ref,
    ) = refs
    block = pl.program_id(0)
    conv_width = inner + 2 * state_count
    ends = [info_ref[k] for k in range(3)]
    base = block * SPAN

    @pl.when(block == 0)
    def _():
        ext_ref[...] = jnp.zeros_like(ext_ref)
        state_ref[...] = jnp.zeros_like(state_ref)
        if parts:
            put = lambda k, value: place_rows(weight_ref, info_ref[4] ^ k, value)
            own_ref, near_ref, far_ref, beside_ref, close_ref, last_ref = part_refs
            put(2, close_ref[...])
            put(3, last_ref[...])
            put(0, own_ref[...])
            put(1, near_ref[...])
            for at in range(far_ref.shape[0]):
                k = 2 * (far_ref.shape[0] - at) + 2
                put(k, far_ref[at])
                put(k + 1, beside_ref[at])
        rows_ref[...] = mm(weight_ref[:, conv_width:], choose_ref[...], TN)[0:16, :]

    pick_piece(block, per_piece, info_ref[3], hidden_refs, hidden_ref)
    residual = hidden_ref[...].astype(f32)
    row_scale = lax.rsqrt(jnp.mean(residual * residual, axis=1, keepdims=True) + epsilon)
    normed = (residual * row_scale * rows_ref[GAIN_AT : GAIN_AT + 1, conv_width:]).astype(bf16)
    normed_ref[...] = normed
    pre = mm(normed, weight_ref[...])
    pre_ref[...] = pre[:, :conv_width].astype(bf16)
    step_ref[...] = pre[:, conv_width:]

    ext_ref[0:8, :] = ext_ref[SPAN : SPAN + 8, :]
    ext_ref[8 : 8 + SPAN, :] = pre[:, :conv_width]
    position = base + iota((SPAN, LANES), 0)
    start = doc_start(position, ends)
    conv = conv_block(ext_ref, rows_ref, position, start, conv_width)
    conv_ref[...] = conv
    active = conv * sigmoid(conv)
    x_val = active[:, :inner].astype(bf16).astype(f32)
    in_map = active[:, inner : inner + state_count].astype(bf16)
    out_map = active[:, inner + state_count :].astype(bf16)

    step_size = softplus(pre[:, conv_width:] + head_ref[1:2, :])
    log_decay = step_size * head_ref[0:1, :]
    row_at = iota((SPAN, SPAN), 0)
    col_at = iota((SPAN, SPAN), 1)
    lower = (col_at <= row_at).astype(f32).astype(bf16)
    cum = mm_left_exact(lower, log_decay * LOG2E)
    cum_ref[...] = cum
    cum_rows = cum.T

    start_last = scalar_start(base + SPAN - 1, ends)
    keep = (start < base).astype(f32)
    tail = (position >= start_last).astype(f32)
    survives = (start_last < base).astype(f32)
    expand = expand_ref[...]
    step_wide = widen(step_size, expand)
    decay_wide = widen(jnp.exp2(cum), expand)
    into_wide = widen(jnp.exp2(cum[SPAN - 1 :, :] - cum) * tail, expand)

    x_step = x_val * step_wide
    x_step_low = x_step.astype(bf16)
    state = state_ref[...]
    entering_ref[...] = state
    outside = mm(out_map, state.astype(bf16)) * (decay_wide * wide(keep, inner))
    visible = (col_at <= row_at) & (base + col_at >= wide(start, SPAN))
    scores = jnp.where(visible, mm(out_map, in_map, NT), 0.0)
    upper_half = iota((SPAN, LANES), 1) >= LANES // 2
    half = SPAN // 2
    inside = []
    for pair in range(heads // 2):
        x_pair = x_step_low[:, pair * LANES : (pair + 1) * LANES]
        tops, bottoms = [], []
        for which in range(2):
            head = 2 * pair + which
            column, row = cum[:, head : head + 1], cum_rows[head : head + 1, :]
            chosen = upper_half if which else jnp.logical_not(upper_half)
            x_head = jnp.where(chosen, x_pair, jnp.zeros_like(x_pair))
            decays = jnp.exp2(jnp.minimum(column[:half] - row[:, :half], 0.0))
            mixing = (scores[:half, :half] * decays).astype(bf16)
            tops.append(mm(mixing, x_head[:half]))
            far = jnp.exp2(column[half:] - row[:, :half])
            near = jnp.exp2(jnp.minimum(column[half:] - row[:, half:], 0.0))
            mixing = (scores[half:] * jnp.concatenate([far, near], axis=1)).astype(bf16)
            bottoms.append(mm(mixing, x_head))
        inside.append(jnp.concatenate([tops[0] + tops[1], bottoms[0] + bottoms[1]], axis=0))
    y_val = jnp.concatenate(inside, axis=1) + outside + chan_ref[0:1, :] * x_val
    y_ref[...] = y_val

    scaled = (x_step * into_wide).astype(bf16)
    state_ref[...] = (decay_wide[SPAN - 1 :, :] * survives) * state + mm(in_map, scaled, TN)


def branch_kernel(per_piece, pieces, info_ref, *refs):
    grad_refs, refs = refs[:pieces], refs[pieces:]
    normed_ref, y_ref, gate_w_ref, out_ref, chan_ref = refs[:5]
    gate_ref, branch_ref, stats_ref, grad_ref = refs[5:]
    block = pl.program_id(0)
    pick_piece(block, per_piece, info_ref[3], grad_refs, grad_ref)
    gate = mm(normed_ref[...], gate_w_ref[...])
    gate_ref[...] = gate
    mixed = y_ref[...] * (gate * sigmoid(gate))
    out_w = out_ref[...]
    gain = chan_ref[1:2, :]
    branch_ref[...] = mm((mixed * gain).astype(bf16), out_w, NT).astype(bf16)
    weighted = mm(grad_ref[...], out_w) * gain
    squares = jnp.sum(mixed * mixed, axis=1, keepdims=True)
    crossed = jnp.sum(weighted * mixed, axis=1, keepdims=True)
    lane = iota((mixed.shape[0], LANES), 1)
    both = jnp.where(lane == 0, squares, jnp.where(lane == 1, crossed, 0.0))
    stats_ref[...] = both.T[0:8, :]


def product_sums(left, right):
    products = left * right.astype(f32)
    return sum(products[:, at : at + LANES] for at in range(0, left.shape[1], LANES))


def gate_kernel(inner, inner_total, per_piece, pieces, info_ref, *refs):
    grad_refs, refs = refs[:pieces], refs[pieces:]
    (
        stats_ref,
        normed_ref,
        gate_w_ref,
        out_ref,
        gate_ref,
        y_ref,
        chan_ref,
        gate_grad_ref,
        y_grad_ref,
        early_ref,
        gain_grad_ref,
        product_ref,
        gate_acc,
        out_acc,
        grad_ref,
    ) = refs
    block = pl.program_id(0)

    @pl.when(block == 0)
    def _():
        gate_acc[...] = jnp.zeros_like(gate_acc)
        out_acc[...] = jnp.zeros_like(out_acc)
        gain_grad_ref[...] = jnp.zeros_like(gain_grad_ref)

    pick_piece(block, per_piece, info_ref[3], grad_refs, grad_ref)
    stats = stats_ref[...].T
    gate_scale = lax.rsqrt(stats[:, 0:1] / inner_total + epsilon)
    crossed = stats[:, 1:2] / inner_total
    gate = gate_ref[...]
    gate_sig = sigmoid(gate)
    gate_act = gate * gate_sig
    y_val = y_ref[...]
    mixed = y_val * gate_act
    grad = grad_ref[...]
    gain = chan_ref[1:2, :]
    gated_grad = mm(grad, out_ref[...])
    scaled_mixed = mixed * gate_scale
    out_acc[...] += mm(grad, (scaled_mixed * gain).astype(bf16), TN)
    gain_grad_ref[0:1, :] += jnp.sum(gated_grad * scaled_mixed, axis=0, keepdims=True)
    mixed_grad = gate_scale * (gated_grad * gain) - scaled_mixed * (
        gate_scale * gate_scale * crossed
    )
    gate_grad = mixed_grad * y_val * (gate_sig * (1.0 + gate * (1.0 - gate_sig)))
    gate_grad = gate_grad.astype(bf16)
    gate_grad_ref[...] = gate_grad
    y_grad_ref[...] = (mixed_grad * gate_act).astype(bf16)
    gate_acc[...] += mm(normed_ref[...], gate_grad, TN)

    @pl.when(block == pl.num_programs(0) - 1)
    def _():
        early_ref[:, :inner] = gate_acc[...].astype(bf16)
        early_ref[:, inner:] = out_acc[...].astype(bf16)
        product_ref[...] = product_sums(gate_acc[...], gate_w_ref[...])


def backward_kernel(inner, state_count, heads, blocks, info_ref, *refs):
    (
        normed_ref,
        weight_ref,
        gate_w_ref,
        pre_ref,
        halo_ref,
        step_ref,
        conv_ref,
        y_ref,
        y_grad_ref,
        gate_grad_ref,
        cum_ref,
        entering_ref,
        rows_ref,
        chan_ref,
        head_ref,
        expand_ref,
        gather_ref,
    ) = refs[:17]
    refs = refs[17:]
    product_ref, choose_ref, extra_ref, total_ref, late_ref = refs[:5]
    ext_ref, next_ref, pre_grad_ref, state_grad_ref, late_acc, small_ref, heads_ref = refs[5:]
    step = pl.program_id(0)
    block = blocks - 1 - step
    base = block * SPAN
    conv_width = inner + 2 * state_count
    ends = [info_ref[k] for k in range(3)]

    @pl.when(step == 0)
    def _():
        next_ref[...] = jnp.zeros_like(next_ref)
        state_grad_ref[...] = jnp.zeros_like(state_grad_ref)
        late_acc[...] = jnp.zeros_like(late_acc)
        small_ref[...] = jnp.zeros_like(small_ref)
        heads_ref[...] = jnp.zeros_like(heads_ref)

    skip = chan_ref[0:1, :]
    y_val = y_ref[...]
    y_grad_low = y_grad_ref[...]
    y_grad = y_grad_low.astype(f32)

    ext_ref[0:8, :] = halo_ref[...].astype(f32)[8:16, :]
    ext_ref[8 : 8 + SPAN, :] = pre_ref[...].astype(f32)
    position = base + iota((SPAN, LANES), 0)
    start = doc_start(position, ends)
    conv = conv_ref[...]
    conv_sig = sigmoid(conv)
    active = conv * conv_sig
    act_slope = conv_sig * (1.0 + conv * (1.0 - conv_sig))
    x_val = active[:, :inner].astype(bf16).astype(f32)
    in_map = active[:, inner : inner + state_count].astype(bf16)
    out_map = active[:, inner + state_count :].astype(bf16)

    step_pre = step_ref[...] + head_ref[1:2, :]
    step_size = softplus(step_pre)
    rates = head_ref[0:1, :]
    cum = cum_ref[...]
    cum_rows = cum.T
    start_last = scalar_start(base + SPAN - 1, ends)
    keep = (start < base).astype(f32)
    tail = (position >= start_last).astype(f32)
    survives = (start_last < base).astype(f32)
    expand = expand_ref[...]
    step_wide = widen(step_size, expand)
    decay_wide = widen(jnp.exp2(cum), expand)
    into_wide = widen(jnp.exp2(cum[SPAN - 1 :, :] - cum) * tail, expand)
    keep_decay = decay_wide * wide(keep, inner)
    last_decay = decay_wide[SPAN - 1 :, :] * survives

    x_step = x_val * step_wide
    x_step_low = x_step.astype(bf16)
    scaled = (x_step * into_wide).astype(bf16)
    entering = entering_ref[...]
    entering_low = entering.astype(bf16)
    state_grad = state_grad_ref[...]
    state_grad_low = state_grad.astype(bf16)

    outside = mm(out_map, entering_low)
    outside_grad = (y_grad * keep_decay).astype(bf16)
    scaled_grad = mm(in_map, state_grad_low)
    out_map_grad = mm(outside_grad, entering_low, NT)
    in_map_grad = mm(scaled, state_grad_low, NT)
    state_grad_ref[...] = last_decay * state_grad + mm(out_map, outside_grad, TN)

    row_at = iota((SPAN, SPAN), 0)
    col_at = iota((SPAN, SPAN), 1)
    col_start = doc_start(base + col_at, ends)
    visible = (row_at <= col_at) & (base + row_at >= col_start)
    scores = jnp.where(visible, mm(in_map, out_map, NT), 0.0)
    upper_half = iota((SPAN, LANES), 1) >= LANES // 2
    half = SPAN // 2
    top_grad = jnp.zeros((half, SPAN), f32)
    bottom_grad = jnp.zeros((half, half), f32)
    x_step_grads = []
    for pair in range(heads // 2):
        x_pair = x_step_low[:, pair * LANES : (pair + 1) * LANES]
        grad_pair = y_grad_low[:, pair * LANES : (pair + 1) * LANES]
        tops, bottoms = [], []
        for which in range(2):
            head = 2 * pair + which
            column, row = cum[:, head : head + 1], cum_rows[head : head + 1, :]
            chosen = upper_half if which else jnp.logical_not(upper_half)
            grad_head = jnp.where(chosen, grad_pair, jnp.zeros_like(grad_pair))
            near = jnp.exp2(jnp.minimum(row[:, :half] - column[:half], 0.0))
            far = jnp.exp2(row[:, half:] - column[:half])
            decays = jnp.concatenate([near, far], axis=1)
            top_grad = top_grad + mm(x_pair[:half], grad_head, NT) * decays
            tops.append(mm((scores[:half] * decays).astype(bf16), grad_head))
            decays = jnp.exp2(jnp.minimum(row[:, half:] - column[half:], 0.0))
            bottom_grad = bottom_grad + mm(x_pair[half:], grad_head[half:], NT) * decays
            tail_mix = (scores[half:, half:] * decays).astype(bf16)
            bottoms.append(mm(tail_mix, grad_head[half:]))
        x_step_grads.append(
            jnp.concatenate([tops[0] + tops[1], bottoms[0] + bottoms[1]], axis=0)
        )
    x_step_grad = jnp.concatenate(x_step_grads, axis=1)
    bottom_grad = jnp.concatenate([jnp.zeros((half, half), f32), bottom_grad], axis=1)
    score_grad = jnp.concatenate([top_grad, bottom_grad], axis=0)
    score_grad = jnp.where(visible, score_grad, 0.0).astype(bf16)
    in_map_grad = in_map_grad + mm(score_grad, out_map)
    out_map_grad = out_map_grad + mm(score_grad, in_map, TN)

    inside = y_val - skip * x_val - keep_decay * outside
    into_terms = scaled.astype(f32) * scaled_grad
    cum_terms = (
        y_grad * inside
        + outside_grad.astype(f32) * outside
        - x_step_low.astype(f32) * x_step_grad
        - into_terms
    )
    last_terms = jnp.sum(into_terms, axis=0, keepdims=True) + last_decay * jnp.sum(
        state_grad * entering, axis=0, keepdims=True
    )
    last_row = iota((SPAN, inner), 0) == SPAN - 1
    cum_terms = cum_terms + jnp.where(last_row, last_terms, 0.0)
    x_step_grad = x_step_grad + into_wide * scaled_grad
    gather = gather_ref[...]
    cum_grad = mm_right_exact(cum_terms, gather)
    step_grad = mm_right_exact(x_val * x_step_grad, gather)
    upper = (row_at <= col_at).astype(f32).astype(bf16)
    log_grad = mm_left_exact(upper, cum_grad)
    step_grad = (step_grad + log_grad * rates) * sigmoid(step_pre)
    pre_grad_ref[:, conv_width:] = step_grad.astype(bf16)
    x_grad = skip * y_grad + step_wide * x_step_grad

    heads_ref[0:1, :] += jnp.sum(y_grad * x_val, axis=0, keepdims=True)
    heads_ref[1:2, :LANES] += jnp.sum(step_size * rates * log_grad, axis=0, keepdims=True)
    heads_ref[2:3, :LANES] += jnp.sum(step_grad, axis=0, keepdims=True)

    conv_grad = jnp.concatenate([x_grad, in_map_grad, out_map_grad], axis=1) * act_slope
    next_ref[SPAN : SPAN + 8, :] = next_ref[0:8, :]
    next_ref[0:SPAN, :] = conv_grad
    back = [None] + [(position - k >= start).astype(f32) for k in range(1, CONV)]
    ahead = [None] + [
        (position >= doc_start(position + k, ends)).astype(f32) for k in range(1, CONV)
    ]
    for col in range(0, conv_width, LANES):
        cols = slice(col, col + LANES)
        grad_here = next_ref[0:SPAN, cols]
        total = grad_here * tap_row(rows_ref, 0, cols)
        small_ref[TAPS_AT + CONV - 1 : TAPS_AT + CONV, cols] += jnp.sum(
            grad_here * ext_ref[8 : 8 + SPAN, cols], axis=0, keepdims=True
        )
        for k in range(1, CONV):
            total = total + next_ref[k : k + SPAN, cols] * ahead[k] * (
                tap_row(rows_ref, k, cols)
            )
            small_ref[TAPS_AT + CONV - 1 - k : TAPS_AT + CONV - k, cols] += jnp.sum(
                grad_here * back[k] * ext_ref[8 - k : 8 - k + SPAN, cols], axis=0, keepdims=True
            )
        pre_grad_ref[:, cols] = total.astype(bf16)

    pre_grads = pre_grad_ref[...]
    total = mm(pre_grads, weight_ref[...], NT) + mm(gate_grad_ref[...], gate_w_ref[...], NT)
    total_ref[...] = total.astype(bf16)
    late_acc[...] += mm(normed_ref[...], pre_grads, TN)

    @pl.when(step == pl.num_programs(0) - 1)
    def _():
        late = late_acc[...]
        sums = product_sums(late, weight_ref[...]) + product_ref[...]
        gain = weight_ref[:, conv_width + GAIN_AT : conv_width + GAIN_AT + 1].astype(f32)
        sums = jnp.sum(sums, axis=1, keepdims=True) / gain
        chosen = small_ref[...].astype(bf16)
        filler = jnp.zeros((LANES - chosen.shape[0], chosen.shape[1]), bf16)
        misc = mm(choose_ref[...], jnp.concatenate([chosen, filler], axis=0), NT)
        misc = misc + jnp.where(iota(misc.shape, 1) == GAIN_AT, sums, 0.0)
        totals = heads_ref[...]
        skips = mm_right_exact(totals, gather_ref[...])
        per_head = [totals[1:2, :LANES], totals[2:3, :LANES], skips[0:1, :]]
        for at_head, value in enumerate(per_head):
            value = jnp.broadcast_to(value, (8, LANES))
            misc = misc + pltpu.roll(value, HEAD_AT + at_head * heads, 1)[0:1, :]
        late_ref[:, :conv_width] = late[:, :conv_width].astype(bf16)
        late_ref[:, conv_width:] = (late[:, conv_width:] + misc + extra_ref[...]).astype(bf16)


def weights_kernel(early_count, inner, *refs):
    early_refs, late_refs = refs[:early_count], refs[early_count:-3]
    zx_ref, out_ref, rest_ref = refs[-3:]
    early = tree_sum([ref[...].astype(f32) for ref in early_refs])
    late = tree_sum([ref[...].astype(f32) for ref in late_refs])
    zx_ref[0] = early[:, :inner]
    zx_ref[1] = late[:, :inner]
    out_ref[...] = early[:, inner:]
    rest_ref[...] = late[:, inner:]


def hidden_kernel(
    gain_at, hidden_ref, grad_ref, own_ref, near_ref, far_ref, rest_ref, rows_ref, out_ref
):
    gain = rows_ref[GAIN_AT : GAIN_AT + 1, gain_at:]
    half = far_ref.shape[0]
    for at, part_ref in ((0, far_ref), (half, rest_ref)):
        rows = slice(at, at + half)
        total = own_ref[rows, :].astype(f32) + near_ref[rows, :].astype(f32)
        scaled = (total + part_ref[...].astype(f32)) * gain
        residual = hidden_ref[rows, :].astype(f32)
        row_scale = lax.rsqrt(jnp.mean(residual * residual, axis=1, keepdims=True) + epsilon)
        crossed = jnp.mean(scaled * residual, axis=1, keepdims=True)
        result = row_scale * scaled - residual * (row_scale * row_scale * row_scale * crossed)
        out_ref[rows, :] = (result + grad_ref[rows, :].astype(f32)).astype(bf16)


def swap(values, axis, bits):
    size = lax.axis_size(axis)
    return lax.ppermute(values, axis, [(i, i ^ bits) for i in range(size)])


def bits_of(size):
    return [1 << k for k in range(size.bit_length() - 1)]


def after(values, *others):
    return lax.optimization_barrier((values,) + others)[0]


def sum_over(values, axis):
    size = lax.axis_size(axis)
    if size > 8:
        for bit in bits_of(size):
            values = values + swap(values, axis, bit)
        return values
    return tree_sum([values] + [swap(values, axis, k) for k in range(1, size)])


def tree_sum(pieces):
    while len(pieces) > 1:
        pieces = [pieces[k] + pieces[k + 1] for k in range(0, len(pieces), 2)]
    return pieces[0]


def gather_far(values, axis):
    pieces = {0: values}
    bits = bits_of(lax.axis_size(axis))
    for bit in reversed(bits[1:]):
        pieces.update({k | bit: swap(piece, axis, bit) for k, piece in list(pieces.items())})
    pieces[1] = swap(values, axis, 1)
    return pieces


def gather_near(pieces, axis, *others):
    pieces = dict(pieces)
    for k in list(pieces):
        if k > 1:
            pieces[k | 1] = swap(after(pieces[k], *others) if others else pieces[k], axis, 1)
    return [pieces[k] for k in range(len(pieces))]


def gather_direct(values, axis, others):
    size = lax.axis_size(axis)
    near = swap(values, axis, 1)
    far = [swap(values, axis, k) for k in range(size - 2, 2, -2)]
    close = swap(values, axis, 2)
    last = swap(close, axis, 1)
    far, last = lax.optimization_barrier((jnp.stack(far), last, *others))[:2]
    return values, near, far, swap(far, axis, 1), close, last


def assemble(own, near, far, beside, close, last, axis):
    size = lax.axis_size(axis)
    place = lax.axis_index(axis)
    result = jnp.zeros((size,) + own.shape, own.dtype)
    pieces = {0: own, 1: near, 2: close, 3: last}
    for at, k in enumerate(range(size - 2, 2, -2)):
        pieces.update({k: far[at], k + 1: beside[at]})
    for k in range(size):
        result = lax.dynamic_update_slice(
            result, pieces[k][None], (place ^ k,) + (0,) * own.ndim
        )
    return result.reshape((-1,) + own.shape[1:])


def gather_pairs(values, other, axis):
    size = lax.axis_size(axis)
    place = lax.axis_index(axis)
    first = place % 2 == 0
    pair = jnp.stack([jnp.where(first, values, other), jnp.where(first, other, values)])
    result = jnp.zeros((size // 2,) + pair.shape, values.dtype)
    for k in range(0, size, 2):
        piece = swap(pair, axis, k) if k else pair
        result = lax.dynamic_update_slice(
            result, piece[None], ((place ^ k) // 2,) + (0,) * pair.ndim
        )
    return result.reshape((-1,) + values.shape[1:])


def block_of(values, place, share):
    return lax.dynamic_slice_in_dim(values, place * share, share, 0)


def fold_pairs(values, axis, steps):
    size = lax.axis_size(axis)
    place = lax.axis_index(axis)
    share = values.shape[0] // size
    theirs = jnp.stack([block_of(values, place ^ k ^ 1, share) for k in steps])
    return swap(theirs, axis, 1)


def fold_sums(values, theirs, axis, steps):
    place = lax.axis_index(axis)
    share = values.shape[0] // lax.axis_size(axis)
    sums = [
        block_of(values, place ^ k, share).astype(f32) + theirs[at].astype(f32)
        for at, k in enumerate(steps)
    ]
    return [both.astype(bf16) if k else both for k, both in zip(steps, sums)]


def send_sums(folded, axis, steps):
    return [
        swap(both, axis, k) if k else both for k, both in zip(steps, folded)
    ]


def per_device(
    hidden_rows,
    out_grad,
    doc_lengths,
    zx_weight,
    step_weight,
    bc_weight,
    conv_inner,
    conv_shared,
    out_weight,
    decay_log,
    step_bias,
    skip_gain,
    norm_gain,
    gate_gain,
):
    piece_len, _, width = hidden_rows.shape
    tensor = lax.axis_size("tensor")
    data = lax.axis_size("dp")
    full_len = piece_len * tensor
    blocks = full_len // SPAN
    per_piece = piece_len // SPAN
    share = zx_weight.shape[1]
    inner = zx_weight.shape[2]
    heads = step_weight.shape[1]
    head_dim = inner // heads
    state_count = bc_weight.shape[1] // 2
    conv_width = inner + 2 * state_count
    span = conv_width + LANES
    inner_total = float(inner * tensor)
    mine = lax.axis_index("tensor")
    place = lax.axis_index("dp")

    hidden = hidden_rows[:, 0, :]
    hidden_all = gather_far(hidden, "tensor")
    hidden_far = hidden_all[tensor // 2]
    hidden_all = gather_near(hidden_all, "tensor")

    inner_share = conv_inner.size // CONV
    shared_share = conv_shared.size // CONV
    taps = jnp.concatenate([conv_inner.reshape(-1, CONV), conv_shared.reshape(-1, CONV)])
    taps = jnp.pad(taps, ((0, share - inner_share - shared_share), (0, 0)))
    misc = jnp.concatenate(
        [
            jnp.pad(step_weight, ((0, 0), (0, TAPS_AT - heads))),
            taps,
            norm_gain[:, None],
            jnp.zeros((share, LANES - GAIN_AT - 1), bf16),
        ],
        axis=1,
    )
    channel = np.arange(inner)
    per_dev = head_dim // data
    sources = [
        (channel % head_dim) // per_dev * share
        + channel // head_dim * per_dev
        + channel % per_dev,
        np.arange(2 * state_count) // shared_share * share
        + inner_share
        + np.arange(2 * state_count) % shared_share,
        np.arange(width),
    ]
    sources = jnp.asarray(np.concatenate(sources), jnp.int32)
    choose = (jnp.arange(width, dtype=jnp.int32)[:, None] == sources[None, :]).astype(bf16)
    chan = jnp.pad(jnp.stack([jnp.repeat(skip_gain, head_dim), gate_gain]), ((0, 6), (0, 0)))
    head_rows = jnp.pad(
        jnp.stack([-jnp.exp(decay_log), step_bias]), ((0, 6), (0, LANES - heads))
    )
    channel_head = jnp.arange(inner)[None, :] // head_dim
    expand = (jnp.arange(LANES)[:, None] % (LANES // 2) == channel_head).astype(bf16)
    gather = (jnp.arange(LANES)[:, None] == channel_head).astype(bf16).T
    lengths = doc_lengths[0].astype(jnp.int32)
    info = jnp.stack(
        [lengths[0], lengths[0] + lengths[1], lengths[0] + lengths[1] + lengths[2], mine, place]
    ).astype(jnp.int32)

    late_shard = jnp.concatenate([zx_weight[0], out_weight.T], axis=1)
    late_other = swap(late_shard, "dp", 1)
    shard = jnp.concatenate([zx_weight[1], bc_weight, misc], axis=1)
    weight_parts = gather_direct(
        shard, "dp", (hidden_far, late_other, choose, chan, head_rows, expand, info)
    )
    in_kernel = share % 16 == 0
    if not in_kernel:
        weight_parts = (assemble(*weight_parts, "dp"),)
    weights_late = gather_pairs(late_shard, late_other, "dp")
    grad_all = gather_far(after(out_grad, hidden_far)[:, 0, :], "tensor")

    def limits(mebi):
        return pltpu.CompilerParams(
            dimension_semantics=("arbitrary",), vmem_limit_bytes=mebi * 1024 * 1024
        )

    shaped = jax.ShapeDtypeStruct

    def fixed(shape, at=0):
        return pl.BlockSpec(shape, lambda i, info: (0,) * (len(shape) - 1) + (at,))

    def rows(cols, at=0, order=lambda i: i):
        return pl.BlockSpec((SPAN, cols), lambda i, info: (order(i), at))

    def piece_specs(order=lambda i: i):
        return [
            pl.BlockSpec(
                (SPAN, width),
                lambda i, info, k=k: (
                    jnp.clip(order(i) - (info[3] ^ k) * per_piece, 0, per_piece - 1),
                    0,
                ),
            )
            for k in range(tensor)
        ]

    def call(
        kernel, name, micros, steps, in_specs, out_specs, out_shape, scratch, args, aliases={}
    ):
        return pl.pallas_call(
            kernel,
            grid_spec=pltpu.PrefetchScalarGridSpec(
                num_scalar_prefetch=1,
                grid=(steps,),
                in_specs=in_specs,
                out_specs=out_specs,
                scratch_shapes=scratch,
            ),
            out_shape=out_shape,
            compiler_params=limits({"backward": 44, "forward": 32}.get(name, 28)),
            input_output_aliases=aliases,
            cost_estimate=pl.CostEstimate(
                flops=int(micros * 1.0e9), bytes_accessed=int(micros * 3.0e6), transcendentals=0
            ),
            name=name,
        )(info, *args)

    def relative(order):
        return pl.BlockSpec(
            (SPAN, width),
            lambda i, info: (
                ((order(i) // per_piece) ^ info[3]) * per_piece + order(i) % per_piece,
                0,
            ),
        )

    natural = lambda i: i
    state_spec = lambda order: pl.BlockSpec(
        (state_count, inner), lambda i, info: (order(i), 0)
    )
    normed, pre, step_pre, y_val, cum, entering, conv, rows_all, *weights = call(
        functools.partial(
            forward_kernel,
            inner,
            state_count,
            heads,
            per_piece,
            tensor,
            len(weight_parts) if in_kernel else 0,
        ),
        "forward",
        22,
        blocks,
        piece_specs()
        + [fixed(part.shape) for part in weight_parts]
        + [
            fixed(choose.shape),
            fixed(chan.shape),
            fixed(head_rows.shape),
            fixed(expand.shape),
        ],
        [
            rows(width),
            rows(conv_width),
            rows(LANES),
            rows(inner),
            rows(LANES),
            state_spec(natural),
            rows(conv_width),
            fixed((16, conv_width + width)),
        ]
        + [fixed((width, span))] * in_kernel,
        [
            shaped((full_len, width), bf16),
            pltpu.HBM((full_len, conv_width), bf16),
            pltpu.HBM((full_len, LANES), f32),
            shaped((full_len, inner), f32),
            pltpu.HBM((full_len, LANES), f32),
            pltpu.HBM((blocks * state_count, inner), f32),
            pltpu.HBM((full_len, conv_width), f32),
            shaped((16, conv_width + width), f32),
        ]
        + [shaped((width, span), bf16)] * in_kernel,
        [
            pltpu.VMEM((SPAN + 8, conv_width), f32),
            pltpu.VMEM((state_count, inner), f32),
            pltpu.VMEM((SPAN, width), bf16),
        ],
        (*hidden_all, *weight_parts, choose, chan, head_rows, expand),
    )
    (weights,) = weights or weight_parts

    tall = lambda cols: pl.BlockSpec((piece_len, cols), lambda i, info: (i, 0))
    whole_pieces = [fixed((piece_len, width))] * tensor
    grad_all = gather_near(grad_all, "tensor", rows_all)
    gate_spec, out_spec = fixed((width, inner)), fixed((width, inner), 1)
    gate, branch, stats = call(
        functools.partial(branch_kernel, 1, tensor),
        "branch",
        11,
        tensor,
        whole_pieces + [tall(width), tall(inner), gate_spec, out_spec, fixed(chan.shape)],
        [tall(inner), pl.BlockSpec((piece_len, width), lambda i, info: (i ^ info[3], 0)), pl.BlockSpec((8, piece_len), lambda i, info: (0, i))],
        [
            shaped((full_len, inner), f32),
            shaped((full_len, width), bf16),
            shaped((8, full_len), f32),
        ],
        [pltpu.VMEM((piece_len, width), bf16)],
        (*grad_all, normed, y_val, weights_late, weights_late, chan),
    )

    cut = lambda values, k: values[k * piece_len : (k + 1) * piece_len]
    branch_sum = cut(branch, 2).astype(f32) + swap(cut(branch, 3), "tensor", 1).astype(f32)
    branch_sum = branch_sum.astype(bf16)
    branch_near = swap(cut(branch, 1), "tensor", 1)
    stats = sum_over(stats, "tensor")

    gate_grad, y_grad, early, gain_grad, product = call(
        functools.partial(gate_kernel, inner, inner_total, 1, tensor),
        "gate_back",
        13,
        tensor,
        whole_pieces
        + [
            pl.BlockSpec((8, piece_len), lambda i, info: (0, i)),
            tall(width),
            gate_spec,
            out_spec,
            tall(inner),
            tall(inner),
            fixed(chan.shape),
        ],
        [
            tall(inner),
            tall(inner),
            fixed((width, 2 * inner)),
            fixed((8, inner)),
            fixed((width, LANES)),
        ],
        [
            pltpu.HBM((full_len, inner), bf16),
            pltpu.HBM((full_len, inner), bf16),
            shaped((width, 2 * inner), bf16),
            shaped((8, inner), f32),
            shaped((width, LANES), f32),
        ],
        [
            pltpu.VMEM((width, inner), f32),
            pltpu.VMEM((width, inner), f32),
            pltpu.VMEM((piece_len, width), bf16),
        ],
        (*grad_all, stats, normed, weights_late, weights_late, gate, y_val, chan),
    )
    far_first = list(range(data - 2, -1, -2))
    early_theirs = fold_pairs(early, "dp", far_first)
    gate_grad, branch_sum = lax.optimization_barrier((gate_grad, branch_sum))
    branch_far = swap(branch_sum, "tensor", 2)

    small_width = conv_width + width
    back = lambda i: blocks - 1 - i
    back_rows = lambda cols: rows(cols, 0, back)
    gate_lanes = inner // share
    extra = jnp.tile(gain_grad[0].reshape(gate_lanes, share).T, (data, 1))
    extra = jnp.pad(extra, ((0, 0), (GATE_AT, LANES - GATE_AT - gate_lanes)))
    total, late = call(
        functools.partial(backward_kernel, inner, state_count, heads, blocks),
        "backward",
        36,
        blocks,
        [
            back_rows(width),
            fixed((width, span)),
            gate_spec,
            back_rows(conv_width),
            pl.BlockSpec(
                (16, conv_width),
                lambda i, info: (jnp.maximum(back(i) * (SPAN // 16) - 1, 0), 0),
            ),
            back_rows(LANES),
            back_rows(conv_width),
            back_rows(inner),
            back_rows(inner),
            back_rows(inner),
            back_rows(LANES),
            state_spec(back),
            fixed((16, small_width)),
            fixed(chan.shape),
            fixed(head_rows.shape),
            fixed(expand.shape),
            fixed(gather.shape),
            fixed((width, LANES)),
            fixed((width, conv_width)),
            fixed((width, LANES)),
        ],
        [relative(back), fixed((width, span))],
        [shaped((full_len, width), bf16), shaped((width, span), bf16)],
        [
            pltpu.VMEM((SPAN + 8, conv_width), f32),
            pltpu.VMEM((SPAN + 8, conv_width), f32),
            pltpu.VMEM((SPAN, span), bf16),
            pltpu.VMEM((state_count, inner), f32),
            pltpu.VMEM((width, span), f32),
            pltpu.VMEM((16, conv_width), f32),
            pltpu.VMEM((8, inner), f32),
        ],
        (
            normed,
            weights,
            weights_late,
            pre,
            pre,
            step_pre,
            conv,
            y_val,
            y_grad,
            gate_grad,
            cum,
            entering,
            rows_all,
            chan,
            head_rows,
            expand,
            gather,
            product,
            choose,
            extra,
        ),
    )

    total, late, branch_near, branch_far, early_theirs = lax.optimization_barrier(
        (total, late, branch_near, branch_far, early_theirs)
    )
    early_pieces = send_sums(
        fold_sums(early, early_theirs, "dp", far_first), "dp", far_first
    )
    total_sum = cut(total, 2).astype(f32) + swap(cut(total, 3), "tensor", 1).astype(f32)
    total_sum = total_sum.astype(bf16)
    groups = far_first[: len(far_first) // 2], far_first[len(far_first) // 2 :]
    theirs = [fold_pairs(late, "dp", steps) for steps in groups]
    total_far = swap(total_sum[: piece_len // 2], "tensor", 2)
    total_rest = swap(total_sum[piece_len // 2 :], "tensor", 2)
    theirs[0], total = lax.optimization_barrier((theirs[0], after(total, total_sum)))
    folded = fold_sums(late, theirs[0], "dp", groups[0])
    theirs[1] = after(theirs[1], total_far, *folded)
    folded += fold_sums(late, theirs[1], "dp", groups[1])
    branch_far, _ = lax.optimization_barrier((branch_far, folded[0]))
    late_pieces = send_sums(folded, "dp", far_first)
    total_own, total_near = cut(total, 0), swap(cut(total, 1), "tensor", 1)

    def whole(kernel, name, out_shape, args):
        return pl.pallas_call(
            kernel, out_shape=out_shape, compiler_params=plain, name=name
        )(*args)

    plain = pltpu.CompilerParams(vmem_limit_bytes=24 * 1024 * 1024)
    zx_part, out_part, rest_part = whole(
        functools.partial(weights_kernel, len(early_pieces), inner),
        "weight_sums",
        [
            shaped((2, share, inner), f32),
            shaped((share, inner), f32),
            shaped((share, span - inner), f32),
        ],
        (*early_pieces, *late_pieces),
    )
    rest_part, total_rest = lax.optimization_barrier((rest_part, total_rest))
    misc_part = rest_part[:, 2 * state_count :]
    shared = [rest_part] + [swap(rest_part, "tensor", k) for k in range(1, tensor)]
    hidden_grad = whole(
        functools.partial(hidden_kernel, conv_width),
        "hidden_back",
        shaped((piece_len, width), bf16),
        (hidden, grad_all[0], total_own, total_near, total_far, total_rest, rows_all),
    )
    hidden_grad, *shared = lax.optimization_barrier((hidden_grad, *shared))
    shared_part = tree_sum(shared)
    bc_part, misc_shared = shared_part[:, : 2 * state_count], shared_part[:, 2 * state_count :]

    residual = hidden.astype(f32)
    gate_scale = lax.rsqrt(
        lax.dynamic_slice_in_dim(stats[0], mine * piece_len, piece_len) / inner_total + epsilon
    )
    branch_local = (
        cut(branch, 0).astype(f32) + branch_near.astype(f32) + branch_far.astype(f32)
    )
    block_out = (residual + branch_local * gate_scale[:, None]).astype(bf16)
    taps_at = slice(TAPS_AT, TAPS_AT + CONV)
    head_values = misc_part[0, HEAD_AT : HEAD_AT + 3 * heads]
    return (
        block_out[:, None, :],
        hidden_grad[:, None, :],
        zx_part,
        misc_part[:, :heads],
        bc_part,
        misc_part[:inner_share, taps_at].reshape(conv_inner.shape),
        misc_shared[inner_share : inner_share + shared_share, taps_at].reshape(-1),
        out_part.T,
        head_values[:heads],
        head_values[heads : 2 * heads],
        head_values[2 * heads :],
        misc_shared[:, GAIN_AT],
        misc_part[:, GATE_AT : GATE_AT + gate_lanes].T.reshape(-1),
    )


def solution(mesh):
    in_specs = (
        P("tensor", "dp", None),
        P("tensor", "dp", None),
        P("dp", None),
        P(None, "dp", "tensor"),
        P("dp", "tensor"),
        P("dp", None),
        P("tensor", "dp"),
        P("dp"),
        P("tensor", "dp"),
        P("tensor"),
        P("tensor"),
        P("tensor"),
        P("dp"),
        P("tensor"),
    )
    out_specs = (
        P("tensor", "dp", None),
        P("tensor", "dp", None),
        P(None, "dp", "tensor"),
        P("dp", "tensor"),
        P("dp", None),
        P("tensor", "dp"),
        P("dp"),
        P("tensor", "dp"),
        P("tensor"),
        P("tensor"),
        P("tensor"),
        P("dp"),
        P("tensor"),
    )
    return jax.shard_map(
        per_device, mesh=mesh, in_specs=in_specs, out_specs=out_specs, check_vma=False
    )
```
